32 devices in a mesh: kt: 8 (over y, x, core), en: 4 (over z).
Axes of the slice: x: 2, y: 2, z: 4, core: 2. Of those that a mesh axis runs over, the one named last changes fastest.
Arguments:
- counts: int32 [8], P('kt'), may hold values from 1 to 4, 16 in all
- contact_slabs: int32 [2], replicated, may hold values from 0 to 15
- onsite: float32 [16, 384], P('en'), may hold values from -0.5 to 0.5
- hopping: float32 [16, 384], P('en'), may hold values from 0.1 to 0.5
- potential_in: float32 [16, 384], P('en'), may hold values from -2 to 2
- couple_base: bfloat16 [16, 384, 384], P('en'), may hold values from -0.25 to 0.25
- couple_wave: bfloat16 [16, 384, 384], P('en'), may hold values from -0.25 to 0.25
- doping: float32 [16, 384], P('en'), may hold values from 0 to 2
- poisson_inverse: float32 [384, 384], replicated, may hold values from -0.3125 to 0.3125
Outputs:
- electron_populace: float32 [16, 384], P('en')
- potential_out: float32 [16, 384], P('en')
The draws below stay inside these ranges and needn't reach their ends.
Inputs may be any that keep to these rules, and one draw needn't show every extreme that they name: counts sum to 16 and the largest is 4.
All inputs are finite; a program needn't handle non-finite values. No bound on the sum of `counts` on one device may be relied on, other than what follows from the above.
Results may differ from the reference program's by a relative error of at most 0.00045.
Values may be sent and summed in bfloat16 or wider, within the bound.
No kernel may reach another device: no remote copies, remote signals or barrier semaphores. Data moves between devices by JAX's collectives and lax.ppermute only.
A program may use at most 64 MiB of HBM per device.

```python
import math
import jax
import jax.numpy as jnp
import numpy as np
from jax import lax

ORB = 384
EMAX = 4
SLABS = 16
CROSS_IMPULSES = 8
LIVE = 16


def steps_of(stream_key, extent, cuts, smallest, high):
    def one(dim, parts):
        steps = jax.random.uniform(jax.random.fold_in(jax.random.fold_in(stream_key, 6), dim), (parts,), jnp.float32, smallest / len(cuts), high / len(cuts))
        return jnp.repeat(jnp.exp(steps), extent[dim] // parts).reshape((-1,) + (1,) * (len(extent) - dim - 1))

    loudness = one(*cuts[0])
    for cut in cuts[1:]:
        loudness = loudness * one(*cut)
    return loudness


def split_up(count, total, reach, skew):
    weights = [(1 << 20) // math.isqrt(rank ** skew) + 1 for rank in range(2, count + 1)]
    rest, holding = total - reach - (count - 1), [1] * (count - 1)
    while rest > 0:
        free = [i for i in range(count - 1) if holding[i] < reach]
        pool, remaining = sum([weights[i] for i in free]), rest
        for i in free:
            addition = min(reach - holding[i], max(1, remaining * weights[i] // pool), rest)
            holding[i] = holding[i] + addition
            rest = rest - addition
    return np.array([reach] + holding)


def uneven_parts(rng, number_of, total, limit, lean):
    if number_of == 2:
        one = jax.random.randint(rng, (), max(1, total - limit), min(limit, total - 1) + 1)
        return jnp.stack([one, total - one])
    sizes = jnp.asarray(split_up(number_of, total, limit, lean), jnp.int32)
    couples = (number_of - 1) // 2
    source_of, taker = sizes[1:1 + 2 * couples:2], sizes[2:2 + 2 * couples:2]
    room = jnp.minimum(source_of - 1, limit - taker)
    moved = jax.random.randint(jax.random.fold_in(rng, 1), (couples,), 0, 1 << 20) % (room + 1)
    sizes = sizes.at[1:1 + 2 * couples:2].set(source_of - moved).at[2:2 + 2 * couples:2].set(taker + moved)
    return sizes[jax.random.permutation(jax.random.fold_in(rng, 2), number_of)]


def centred(rng, shape, width, limit, split=(), kind=jnp.bfloat16):
    level = steps_of(rng, shape, split, -0.22, 0.18) if split else 1.0
    entries = jax.random.normal(rng, shape, jnp.float32) * width * level
    return jnp.minimum(jnp.maximum(entries, -limit), limit).astype(kind)


def setup_inputs(seed: int = 0) -> dict:
    arg_keys = jax.random.split(jax.random.key(seed), 10)
    return {
        "counts": uneven_parts(arg_keys[0], CROSS_IMPULSES, 2 * CROSS_IMPULSES, EMAX, 2).astype(jnp.int32),
        "contact_slabs": jax.random.randint(arg_keys[1], (2,), 0, SLABS).astype(jnp.int32),
        "onsite": jnp.clip(jax.random.uniform(arg_keys[2], (SLABS, ORB), jnp.float32, -0.5, 0.5) * steps_of(arg_keys[2], (SLABS, ORB), ((0, 4),), -0.4, 0.0), -0.5, 0.5),
        "hopping": jnp.clip(0.1 + 0.4 * jax.random.uniform(arg_keys[3], (SLABS, ORB), jnp.float32) ** steps_of(arg_keys[3], (SLABS, ORB), ((0, 4),), -0.2, 0.2), 0.1, 0.5),
        "potential_in": centred(arg_keys[4], (SLABS, ORB), 0.3, 2.0, ((0, 4),), jnp.float32),
        "couple_base": centred(arg_keys[5], (SLABS, ORB, ORB), (5 * ORB // 3) ** -0.5, 0.25, ((0, 4),)),
        "couple_wave": centred(arg_keys[6], (SLABS, ORB, ORB), (5 * ORB // 3) ** -0.5, 0.25, ((0, 4),)),
        "doping": jnp.clip(2.0 * jax.random.uniform(arg_keys[7], (SLABS, ORB), jnp.float32) ** steps_of(arg_keys[7], (SLABS, ORB), ((0, 4),), -0.2, 0.2), 0.0, 2.0),
        "poisson_inverse": centred(arg_keys[8], (ORB, ORB), ORB ** -0.5, 0.3125, (), jnp.float32),
    }


bottom_sample_mark = -1.0
sample_gap = 0.25
electrode_filling = -0.5
boltzmann_spread = 0.1
broadening = 1.0
contact_width = 0.5


def item_tables(counts, first_index, number):
    include_endpoint = jnp.cumsum(counts).astype(jnp.int32)
    exclusive = include_endpoint - counts
    item_index = first_index + jnp.arange(number, dtype=jnp.int32)
    transverse_impulse = jnp.sum((include_endpoint[None, :] <= item_index[:, None]).astype(jnp.int32), axis=1)
    selector = (jnp.arange(counts.shape[0], dtype=jnp.int32)[None, :] == transverse_impulse[:, None]).astype(jnp.int32)
    eigen_height = item_index - jnp.sum(selector * exclusive[None, :], axis=1)
    return transverse_impulse, eigen_height


def entry_amounts(transverse_impulse, eigen_height, impulse_count):
    wave_vector_number = jnp.pi * (transverse_impulse.astype(jnp.float32) + 0.5) / impulse_count
    angular_projection = jnp.cos(wave_vector_number)
    occupancy_mark = bottom_sample_mark + sample_gap * eigen_height.astype(jnp.float32)
    summation_multiplier = sample_gap / (1.0 + jnp.exp((occupancy_mark - electrode_filling) / boltzmann_spread)) / jnp.pi
    return angular_projection, occupancy_mark, summation_multiplier


def slab_step(carried, couple_base, couple_wave, angular_projection, diag_real, diag_imag):
    coupled = (couple_base.astype(jnp.float32) + angular_projection * couple_wave.astype(jnp.float32)).astype(jnp.bfloat16)
    left_part = jnp.einsum("rm,pmn->prn", coupled.astype(jnp.float32), carried.astype(jnp.float32)).astype(jnp.bfloat16)
    self_energy = jnp.einsum("prn,cn->prc", left_part.astype(jnp.float32), coupled.astype(jnp.float32))
    magnitude = diag_real * diag_real + diag_imag * diag_imag
    inv_real = diag_real / magnitude
    inv_imag = -diag_imag / magnitude
    half_real = inv_real[:, None] * self_energy[0] - inv_imag[:, None] * self_energy[1]
    half_imag = inv_real[:, None] * self_energy[1] + inv_imag[:, None] * self_energy[0]
    identity = jnp.eye(diag_real.shape[0], dtype=jnp.float32)
    green_real = half_real * inv_real[None, :] - half_imag * inv_imag[None, :] + identity * inv_real[None, :]
    green_imag = half_real * inv_imag[None, :] + half_imag * inv_real[None, :] + identity * inv_imag[None, :]
    return jnp.stack([green_real, green_imag]).astype(jnp.bfloat16), -jnp.diagonal(green_imag)


def reference(counts, contact_slabs, onsite, hopping, potential_in, couple_base, couple_wave, doping, poisson_inverse):
    transverse_impulse, eigen_height = item_tables(counts, 0, LIVE)
    angular_projection, occupancy_mark, summation_multiplier = entry_amounts(transverse_impulse, eigen_height, CROSS_IMPULSES)
    slab_ids = jnp.arange(SLABS, dtype=jnp.int32)
    contact_flag = jnp.any(slab_ids[:, None] == contact_slabs[None, :], axis=1).astype(jnp.float32)
    diag_imag = broadening + contact_width * contact_flag
    real_base = -onsite - potential_in

    def each_entry_share(values):
        item_cos, item_energy, item_weight = values
        carried = jnp.zeros((2, ORB, ORB), jnp.bfloat16)
        slab_rows = []
        for slab_index in range(SLABS):
            diag_real = item_energy + real_base[slab_index] - item_cos * hopping[slab_index]
            imag_row = jnp.full((ORB,), 1.0, jnp.float32) * diag_imag[slab_index]
            carried, diag_part = slab_step(carried, couple_base[slab_index], couple_wave[slab_index], item_cos, diag_real, imag_row)
            slab_rows.append(item_weight * diag_part)
        return jnp.stack(slab_rows)

    electron_populace = jnp.sum(lax.map(each_entry_share, (angular_projection, occupancy_mark, summation_multiplier)), axis=0)
    potential_out = jnp.dot(electron_populace - doping, poisson_inverse.T, precision=lax.Precision.HIGHEST)
    return electron_populace, potential_out
```

```python
import functools

import jax
import jax.numpy as jnp
import numpy as np
from jax import lax
from jax.experimental import pallas as pl
from jax.experimental.pallas import tpu as pltpu
from jax.sharding import PartitionSpec as P

EMAX = 4
LANE = 128
F32 = jnp.float32
BF16 = jnp.bfloat16

bottom_sample_mark = -1.0
sample_gap = 0.25
electrode_filling = -0.5
boltzmann_spread = 0.1
broadening = 1.0
contact_width = 0.5


def item_constants(impulse_count):
    wave = np.float32(np.pi) * (np.arange(impulse_count, dtype=np.float32) + np.float32(0.5))
    cosine = np.cos(wave / np.float32(impulse_count))
    energy = bottom_sample_mark + sample_gap * np.arange(EMAX)
    weight = sample_gap / (1.0 + np.exp((energy - electrode_filling) / boltzmann_spread)) / np.pi
    return np.concatenate([cosine, weight]).astype(np.float32)


def span(k):
    return slice(k * LANE, (k + 1) * LANE)


def place(parts, half, c):
    if c == parts - 1:
        return parts - 1 + half
    return c if half == 0 else parts + 1 + c


def blocks_on_or_below(parts):
    return [(r, c) for r in range(parts) for c in range(r + 1)]


def packed_rows(orbitals):
    parts = orbitals // LANE
    return parts * parts * LANE + 16


def pairs_below(parts):
    return [(r, c) for r in range(parts) for c in range(r)]


def pair_slot(parts, r, c, half):
    return 2 * pairs_below(parts).index((r, c)) + half


def middle_slot(parts, r):
    return parts * (parts - 1) + r


def tile_indices():
    rows = lax.broadcasted_iota(jnp.int32, (LANE, LANE), 0)
    cols = lax.broadcasted_iota(jnp.int32, (LANE, LANE), 1)
    return rows, cols


def unpack_blocks(packed, g, parts):
    rows, cols = tile_indices()
    for r, c in pairs_below(parts):
        for half in range(2):
            block = packed[span(pair_slot(parts, r, c, half)), :]
            g[span(r), span(place(parts, half, c))] = block
            g[span(c), span(place(parts, half, r))] = block.T
    at = parts * parts * LANE
    for r in range(parts):
        block = packed[span(middle_slot(parts, r)), :]
        turned = block.T
        middle = packed[at : at + 16, :][r : r + 1, :]
        g[span(r), span(place(parts, 0, r))] = jnp.where(rows <= cols, block, turned)
        g[span(r), span(place(parts, 1, r))] = jnp.where(
            rows > cols, block, jnp.where(rows == cols, middle, turned)
        )


def extra_item(counts, mine):
    def one(k, state):
        momentum, before = state
        extra = counts[k] - 1
        take = jnp.logical_and(momentum == k, before + extra <= mine)
        return (jnp.where(take, k + 1, momentum), jnp.where(take, before + extra, before))

    momentum, before = lax.fori_loop(0, counts.shape[0], one, (jnp.int32(0), jnp.int32(0)))
    momentum = jnp.minimum(momentum, counts.shape[0] - 1)
    return momentum, jnp.clip(1 + mine - before, 0, EMAX - 1)


def entry_amounts(constants, impulse_count, momentum, level):
    energy = bottom_sample_mark + sample_gap * level.astype(F32)
    return constants[momentum], energy, constants[impulse_count + level]


def inverse_diagonal(position, cosine, energy, contact, onsite, hopping, potential):
    slabs, orbitals = onsite.shape
    diag_real = energy + (-onsite[...] - potential[...]) - cosine * hopping[...]
    slab_in = lax.broadcasted_iota(jnp.int32, (slabs, orbitals), 0) + position * slabs
    at_contact = jnp.logical_or(slab_in == contact[0], slab_in == contact[1])
    diag_imag = broadening + contact_width * at_contact.astype(F32)
    magnitude = diag_real * diag_real + diag_imag * diag_imag
    inv_real = diag_real / magnitude
    inv_imag = -diag_imag / magnitude
    return inv_real, inv_imag


def scale_rows(parts):
    return 2 * len(blocks_on_or_below(parts)) * LANE


def form_scales(slabs_wanted, inv_real, inv_imag, scales, parts):
    slabs = inv_real.shape[0]
    down = jnp.concatenate([inv_real, inv_imag], axis=0).T
    for s in slabs_wanted:
        for k, (r, c) in enumerate(blocks_on_or_below(parts)):
            real_col = down[span(r), s : s + 1]
            imag_col = down[span(r), slabs + s : slabs + s + 1]
            rr = inv_real[s : s + 1, span(c)]
            ri = inv_imag[s : s + 1, span(c)]
            scales[s, span(2 * k), :] = real_col * rr - imag_col * ri
            scales[s, span(2 * k + 1), :] = real_col * ri + imag_col * rr


def store_left(left, piece, half, c, parts):
    last = (parts - 1) * LANE
    left[half * last : (half + 1) * last, span(c)] = piece[:last]
    bottom = 2 * last + half * LANE
    left[bottom : bottom + LANE, span(c)] = piece[last:]


def times_carried(coupled, g, left, parts):
    last = (parts - 1) * LANE
    for begin, width in ((last, 2 * LANE), (0, last), (last + 2 * LANE, last)):
        product = jnp.dot(
            coupled, g[:, begin : begin + width], preferred_element_type=F32
        ).astype(BF16)
        for k in range(width // LANE):
            column = begin // LANE + k
            half, c = (
                (0, column)
                if column < parts
                else (1, parts - 1 if column == parts else column - parts - 1)
            )
            store_left(left, product[:, span(k)], half, c, parts)


def finish_slab(s, times_turned, left, g, packed, inv_real, inv_imag, scales, weight, density, parts):
    last = (parts - 1) * LANE
    rows, cols = tile_indices()
    diagonal = rows == cols
    numbers = {block: k for k, block in enumerate(blocks_on_or_below(parts))}
    middles = {}

    def finish(r, c, sr, si):
        k = numbers[r, c]
        scale_real = scales[s, span(2 * k), :]
        scale_imag = scales[s, span(2 * k + 1), :]
        green_real = scale_real * sr - scale_imag * si
        green_imag = scale_real * si + scale_imag * sr
        if r == c:
            green_real = green_real + jnp.where(diagonal, inv_real[s : s + 1, span(c)], 0.0)
            green_imag = green_imag + jnp.where(diagonal, inv_imag[s : s + 1, span(c)], 0.0)
            middles[r] = jnp.sum(jnp.where(diagonal, green_imag, 0.0), axis=0, keepdims=True)
            density[s : s + 1, span(r)] += -weight * middles[r]
        if packed is not None:
            if r == c:
                packed[span(middle_slot(parts, r)), :] = jnp.where(
                    rows <= cols, green_real, green_imag
                ).astype(BF16)
            else:
                packed[span(pair_slot(parts, r, c, 0)), :] = green_real.astype(BF16)
                packed[span(pair_slot(parts, r, c, 1)), :] = green_imag.astype(BF16)
            return
        if g is None:
            return
        for half, green in ((0, green_real), (1, green_imag)):
            rounded = green.astype(BF16)
            g[span(r), span(place(parts, half, c))] = rounded
            if r != c:
                g[span(c), span(place(parts, half, r))] = rounded.T

    far = times_turned(left[2 * last :, :], last + LANE)
    near = times_turned(left[: 2 * last, :], last)
    for c in range(parts):
        finish(parts - 1, c, far[:LANE, span(c)], far[LANE:, span(c)])
    for r in range(parts - 1):
        for c in range(r + 1):
            finish(r, c, near[span(r), span(c)], near[last:, :][span(r), span(c)])
    if packed is not None:
        rest = jnp.zeros((16 - parts, LANE), F32)
        at = parts * parts * LANE
        packed[at : at + 16, :] = jnp.concatenate(
            [middles[r] for r in range(parts)] + [rest], axis=0
        ).astype(BF16)


def coupling_of(base, wave, cosine):
    return (base.astype(F32) + cosine * wave.astype(F32)).astype(BF16)


def first_segment(coupled_of, inv_real, inv_imag, scales, weight, g, left, sent, density):
    slabs, orbitals = inv_real.shape
    parts = orbitals // LANE
    density[0:1, :] = -weight * inv_imag[0:1, :]
    for s in range(1, slabs):
        coupled = coupled_of(s)
        if s == 1:
            wide = coupled.astype(F32)
            for half, inv in ((0, inv_real), (1, inv_imag)):
                piece = (wide * inv[0:1, :].astype(BF16).astype(F32)).astype(BF16)
                for c in range(parts):
                    store_left(left, piece[:, span(c)], half, c, parts)
        else:
            times_carried(coupled, g, left, parts)

        def times_turned(rows, upto):
            return lax.dot_general(
                rows, coupled[:upto], (((1,), (1,)), ((), ())), preferred_element_type=F32
            )

        finish_slab(
            s, times_turned, left, g, sent if s == slabs - 1 else None,
            inv_real, inv_imag, scales, weight, density, parts,
        )


def own_kernel(
    impulse_count,
    constants_hbm, contact_hbm, onsite_hbm, hopping_hbm, potential_hbm, base_hbm, wave_hbm,
    sent, density,
    constants, contact, tables, base, wave, scales, g, left, small_sem, table_sem, couple_sem,
):
    slabs, orbitals = onsite_hbm.shape
    parts = orbitals // LANE
    position = lax.axis_index("en")
    density[...] = jnp.zeros_like(density)

    @pl.when(position == 0)
    def _():
        small_copies = [
            pltpu.make_async_copy(source, target, small_sem.at[k])
            for k, (source, target) in enumerate(
                ((constants_hbm, constants), (contact_hbm, contact))
            )
        ] + [
            pltpu.make_async_copy(source, tables.at[k], table_sem.at[k])
            for k, source in enumerate((onsite_hbm, hopping_hbm, potential_hbm))
        ]
        couple_copies = {
            s: (
                pltpu.make_async_copy(base_hbm.at[s], base.at[s], couple_sem.at[0, s]),
                pltpu.make_async_copy(wave_hbm.at[s], wave.at[s], couple_sem.at[1, s]),
            )
            for s in range(1, slabs)
        }
        for copy in small_copies:
            copy.start()
        for s in range(1, slabs):
            for copy in couple_copies[s]:
                copy.start()
        for copy in small_copies:
            copy.wait()
        cosine, energy, weight = entry_amounts(
            constants, impulse_count, lax.axis_index("kt"), jnp.int32(0)
        )
        inv_real, inv_imag = inverse_diagonal(
            position, cosine, energy, contact, tables.at[0], tables.at[1], tables.at[2]
        )
        form_scales(range(1, slabs), inv_real, inv_imag, scales, parts)

        def coupled_of(s):
            for copy in couple_copies[s]:
                copy.wait()
            return coupling_of(base[s], wave[s], cosine)

        first_segment(coupled_of, inv_real, inv_imag, scales, weight, g, left, sent, density)


def extra_kernel(
    impulse_count,
    constants, contact, counts, onsite, hopping, potential, base, wave, so_far,
    sent, density,
    couple_own, turned_own, scales_own, entry_own,
    couple_extra, turned_extra, scales_extra, entry_extra,
    scales, g, left,
):
    slabs, orbitals = onsite.shape
    parts = orbitals // LANE
    position = lax.axis_index("en")
    mine = lax.axis_index("kt")
    density[...] = so_far[...]
    momentum, level = extra_item(counts, mine)
    cosine, energy, weight = entry_amounts(constants, impulse_count, momentum, level)
    inv_real, inv_imag = inverse_diagonal(
        position, cosine, energy, contact, onsite, hopping, potential
    )

    @pl.when(position == 0)
    def _():
        form_scales(range(1, slabs), inv_real, inv_imag, scales, parts)
        first = jnp.zeros_like(density)
        kept = density[...]
        density[...] = first

        def coupled_of(s):
            return coupling_of(base[s], wave[s], cosine)

        first_segment(coupled_of, inv_real, inv_imag, scales, weight, g, left, sent, density)
        density[...] += kept

    def prepare(cosine, weight, inv_real, inv_imag, couple, turned, scales_out, entry):
        form_scales(range(slabs), inv_real, inv_imag, scales_out, parts)
        entry[:slabs, :] = inv_real
        entry[slabs : 2 * slabs, :] = inv_imag
        entry[2 * slabs :, :] = jnp.full((slabs, orbitals), weight, F32)
        for s in range(slabs):
            coupled = coupling_of(base[s], wave[s], cosine)
            couple[s] = coupled
            for r in range(parts):
                for c in range(parts):
                    turned[s, span(c), span(r)] = coupled[span(r), span(c)].T

    @pl.when(position > 0)
    def _():
        own_cosine, own_energy, own_weight = entry_amounts(
            constants, impulse_count, mine, jnp.int32(0)
        )
        own_real, own_imag = inverse_diagonal(
            position, own_cosine, own_energy, contact, onsite, hopping, potential
        )
        prepare(
            own_cosine, own_weight, own_real, own_imag,
            couple_own, turned_own, scales_own, entry_own,
        )
        prepare(
            cosine, weight, inv_real, inv_imag,
            couple_extra, turned_extra, scales_extra, entry_extra,
        )


def stage_kernel(stage, last_stage, couple, turned, scales, entry, arrived, so_far, *refs):
    if last_stage:
        density, g, left = refs
        sent = None
    else:
        sent, density, g, left = refs
    slabs, orbitals = so_far.shape
    parts = orbitals // LANE
    density[...] = so_far[...]

    @pl.when(lax.axis_index("en") == stage)
    def _():
        inv_real = entry[:slabs, :]
        inv_imag = entry[slabs : 2 * slabs, :]
        weight = entry[2 * slabs : 2 * slabs + 1, :LANE]
        unpack_blocks(arrived, g, parts)
        for s in range(slabs):
            times_carried(couple[s], g, left, parts)

            def times_turned(rows, upto):
                return jnp.dot(rows, turned[s, :, :upto], preferred_element_type=F32)

            final = s == slabs - 1
            finish_slab(
                s, times_turned, left, None if final else g, sent if final else None,
                inv_real, inv_imag, scales, weight, density, parts,
            )


def vmem_call(kernel, outs, operands, in_specs, scratch, name, flops, **more):
    vmem = pl.BlockSpec(memory_space=pltpu.VMEM)
    return pl.pallas_call(
        kernel,
        out_shape=tuple(outs),
        in_specs=in_specs,
        out_specs=(vmem,) * len(outs),
        scratch_shapes=scratch,
        compiler_params=pltpu.CompilerParams(vmem_limit_bytes=24 * 2**20),
        cost_estimate=pl.CostEstimate(flops=flops, bytes_accessed=2**21, transcendentals=0),
        name=name,
        **more,
    )(*operands)


def last_kernel(gathered, doping, inverse, summed, potential):
    total = jnp.sum(gathered[...], axis=0)
    summed[...] = total
    potential[...] = lax.dot_general(
        total - doping[...],
        inverse[...],
        (((1,), (1,)), ((), ())),
        preferred_element_type=F32,
        precision=lax.Precision.HIGHEST,
    )


def gather_over(values, axis):
    copies = jnp.broadcast_to(values[None], (lax.axis_size(axis),) + values.shape)
    return lax.all_to_all(copies, axis, 0, 0)


def body(
    counts,
    contact_slabs,
    onsite,
    hopping,
    potential_in,
    couple_base,
    couple_wave,
    doping,
    poisson_inverse,
):
    kt_size = lax.axis_size("kt")
    en_size = lax.axis_size("en")
    slabs, orbitals = onsite.shape
    parts = orbitals // LANE
    position = lax.axis_index("en")
    impulse_count = counts.shape[0] * kt_size
    constants = jnp.asarray(item_constants(impulse_count))
    smem = pl.BlockSpec(memory_space=pltpu.SMEM)
    hbm = pl.BlockSpec(memory_space=pltpu.HBM)
    vmem = pl.BlockSpec(memory_space=pltpu.VMEM)
    flops = 2 * slabs * orbitals**3

    def forward(block, stage):
        return lax.ppermute(block, "en", [(stage, stage + 1)])

    block_shape = jax.ShapeDtypeStruct((packed_rows(orbitals), LANE), BF16)
    density_shape = jax.ShapeDtypeStruct((slabs, orbitals), F32)
    couple_shape = jax.ShapeDtypeStruct((slabs, orbitals, orbitals), BF16)
    scales_shape = jax.ShapeDtypeStruct((slabs, scale_rows(parts), LANE), F32)
    entry_shape = jax.ShapeDtypeStruct((3 * slabs, orbitals), F32)
    scales_scratch = pltpu.VMEM(scales_shape.shape, F32)
    work = [
        pltpu.VMEM((orbitals, 2 * orbitals), BF16),
        pltpu.VMEM((2 * orbitals, orbitals), BF16),
    ]

    half = en_size // 2
    counts_here = lax.cond(
        position >= half,
        lambda c: lax.all_gather(c, "kt", tiled=True),
        lambda c: jnp.zeros((impulse_count,), jnp.int32),
        counts,
    )
    pinned, counts_here = lax.optimization_barrier(
        (
            (constants, contact_slabs, onsite, hopping, potential_in, couple_base, couple_wave),
            counts_here,
        )
    )
    pinned = [pltpu.with_memory_space_constraint(t, pltpu.HBM) for t in pinned]
    block, density = vmem_call(
        functools.partial(own_kernel, impulse_count),
        (block_shape, density_shape),
        pinned,
        [hbm] * len(pinned),
        [
            pltpu.SMEM(constants.shape, F32),
            pltpu.SMEM(contact_slabs.shape, jnp.int32),
            pltpu.VMEM((3, slabs, orbitals), F32),
            pltpu.VMEM((slabs, orbitals, orbitals), BF16),
            pltpu.VMEM((slabs, orbitals, orbitals), BF16),
            scales_scratch,
        ]
        + work
        + [
            pltpu.SemaphoreType.DMA((2,)),
            pltpu.SemaphoreType.DMA((3,)),
            pltpu.SemaphoreType.DMA((2, slabs)),
        ],
        "first_own",
        3 * flops,
    )
    arrived_own = forward(block, 0)
    counts_all = counts_here + lax.ppermute(
        counts_here, "en", [(p + half, p) for p in range(half)]
    )
    held, density, *made = vmem_call(
        functools.partial(extra_kernel, impulse_count),
        (block_shape, density_shape) + (couple_shape, couple_shape, scales_shape, entry_shape) * 2,
        (
            constants, contact_slabs, counts_all,
            onsite, hopping, potential_in, couple_base, couple_wave, density,
        ),
        [smem] * 3 + [vmem] * 6,
        [scales_scratch] + work,
        "first_extra",
        3 * flops,
        input_output_aliases={8: 1},
    )
    made_own, made_extra = made[:4], made[4:]

    def run_stage(stage, made, arrived, density, name):
        last_stage = stage == en_size - 1
        results = vmem_call(
            functools.partial(stage_kernel, stage, last_stage),
            (density_shape,) if last_stage else (block_shape, density_shape),
            (*made, arrived, density),
            [vmem] * 6,
            work,
            f"stage_{stage}_{name}",
            4 * flops,
            input_output_aliases={5: 0 if last_stage else 1},
        )
        return (None, *results) if last_stage else results

    for stage in range(1, en_size):
        arrived_own, held = lax.optimization_barrier((arrived_own, held))
        arrived_extra = forward(held, stage - 1)
        block, density = run_stage(stage, made_own, arrived_own, density, "own")
        if stage < en_size - 1:
            arrived_own = forward(block, stage)
        held, density = run_stage(stage, made_extra, arrived_extra, density, "extra")
    return pl.pallas_call(
        last_kernel,
        out_shape=(density_shape, density_shape),
        in_specs=[vmem] * 3,
        out_specs=(vmem, vmem),
        name="last",
    )(gather_over(density, "kt"), doping, poisson_inverse)


def solution(mesh):
    return jax.shard_map(
        body,
        mesh=mesh,
        in_specs=(
            P("kt"),
            P(),
            P("en", None),
            P("en", None),
            P("en", None),
            P("en", None, None),
            P("en", None, None),
            P("en", None),
            P(),
        ),
        out_specs=(P("en", None), P("en", None)),
        check_vma=False,
    )
```

```python
import functools

import jax
import jax.numpy as jnp
import numpy as np
from jax import lax
from jax.experimental import pallas as pl
from jax.experimental.pallas import tpu as pltpu
from jax.sharding import PartitionSpec as P

EMAX = 4
LANE = 128
F32 = jnp.float32
BF16 = jnp.bfloat16

bottom_sample_mark = -1.0
sample_gap = 0.25
electrode_filling = -0.5
boltzmann_spread = 0.1
broadening = 1.0
contact_width = 0.5


def item_constants(impulse_count):
    wave = np.float32(np.pi) * (np.arange(impulse_count, dtype=np.float32) + np.float32(0.5))
    cosine = np.cos(wave / np.float32(impulse_count))
    energy = bottom_sample_mark + sample_gap * np.arange(EMAX)
    weight = sample_gap / (1.0 + np.exp((energy - electrode_filling) / boltzmann_spread)) / np.pi
    return np.concatenate([cosine, weight]).astype(np.float32)


def span(k):
    return slice(k * LANE, (k + 1) * LANE)


def place(parts, half, c):
    if c == parts - 1:
        return parts - 1 + half
    return c if half == 0 else parts + 1 + c


def blocks_on_or_below(parts):
    return [(r, c) for r in range(parts) for c in range(r + 1)]


def packed_rows(orbitals):
    parts = orbitals // LANE
    return parts * parts * LANE + 16


def pairs_below(parts):
    return [(r, c) for r in range(parts) for c in range(r)]


def pair_slot(parts, r, c, half):
    return 2 * pairs_below(parts).index((r, c)) + half


def middle_slot(parts, r):
    return parts * (parts - 1) + r


def tile_indices():
    rows = lax.broadcasted_iota(jnp.int32, (LANE, LANE), 0)
    cols = lax.broadcasted_iota(jnp.int32, (LANE, LANE), 1)
    return rows, cols


def unpack_blocks(packed, g, parts):
    rows, cols = tile_indices()
    for r, c in pairs_below(parts):
        for half in range(2):
            block = packed[span(pair_slot(parts, r, c, half)), :]
            g[span(r), span(place(parts, half, c))] = block
            g[span(c), span(place(parts, half, r))] = block.T
    at = parts * parts * LANE
    for r in range(parts):
        block = packed[span(middle_slot(parts, r)), :]
        turned = block.T
        middle = packed[at : at + 16, :][r : r + 1, :]
        g[span(r), span(place(parts, 0, r))] = jnp.where(rows <= cols, block, turned)
        g[span(r), span(place(parts, 1, r))] = jnp.where(
            rows > cols, block, jnp.where(rows == cols, middle, turned)
        )


def extra_item(counts, mine):
    def one(k, state):
        momentum, before = state
        extra = counts[0, k] - 1
        take = jnp.logical_and(momentum == k, before + extra <= mine)
        return (jnp.where(take, k + 1, momentum), jnp.where(take, before + extra, before))

    momentum, before = lax.fori_loop(0, counts.shape[1], one, (jnp.int32(0), jnp.int32(0)))
    momentum = jnp.minimum(momentum, counts.shape[1] - 1)
    return momentum, jnp.clip(1 + mine - before, 0, EMAX - 1)


def entry_amounts(constants, impulse_count, momentum, level):
    energy = bottom_sample_mark + sample_gap * level.astype(F32)
    return constants[momentum], energy, constants[impulse_count + level]


def inverse_diagonal(position, cosine, energy, contact, onsite, hopping, potential):
    slabs, orbitals = onsite.shape
    diag_real = energy + (-onsite[...] - potential[...]) - cosine * hopping[...]
    slab_in = lax.broadcasted_iota(jnp.int32, (slabs, orbitals), 0) + position * slabs
    at_contact = jnp.logical_or(slab_in == contact[0], slab_in == contact[1])
    diag_imag = broadening + contact_width * at_contact.astype(F32)
    magnitude = diag_real * diag_real + diag_imag * diag_imag
    inv_real = diag_real / magnitude
    inv_imag = -diag_imag / magnitude
    return inv_real, inv_imag


def scale_rows(parts):
    return 2 * len(blocks_on_or_below(parts)) * LANE


def form_scales(slabs_wanted, inv_real, inv_imag, scales, parts):
    slabs = inv_real.shape[0]
    down = jnp.concatenate([inv_real, inv_imag], axis=0).T
    for s in slabs_wanted:
        for k, (r, c) in enumerate(blocks_on_or_below(parts)):
            real_col = down[span(r), s : s + 1]
            imag_col = down[span(r), slabs + s : slabs + s + 1]
            rr = inv_real[s : s + 1, span(c)]
            ri = inv_imag[s : s + 1, span(c)]
            scales[s, span(2 * k), :] = real_col * rr - imag_col * ri
            scales[s, span(2 * k + 1), :] = real_col * ri + imag_col * rr


def store_left(left, piece, half, c, parts):
    last = (parts - 1) * LANE
    left[half * last : (half + 1) * last, span(c)] = piece[:last]
    bottom = 2 * last + half * LANE
    left[bottom : bottom + LANE, span(c)] = piece[last:]


def times_carried(coupled, g, left, parts):
    product = jnp.dot(coupled, g[...], preferred_element_type=F32).astype(BF16)
    for column in range(2 * parts):
        half, c = (
            (0, column)
            if column < parts
            else (1, parts - 1 if column == parts else column - parts - 1)
        )
        store_left(left, product[:, span(column)], half, c, parts)


def finish_slab(s, times_turned, left, g, packed, inv_real, inv_imag, scales, weight, density, parts):
    last = (parts - 1) * LANE
    rows, cols = tile_indices()
    diagonal = rows == cols
    numbers = {block: k for k, block in enumerate(blocks_on_or_below(parts))}
    middles = {}

    def finish(r, c, sr, si):
        k = numbers[r, c]
        scale_real = scales[s, span(2 * k), :]
        scale_imag = scales[s, span(2 * k + 1), :]
        green_real = scale_real * sr - scale_imag * si
        green_imag = scale_real * si + scale_imag * sr
        if r == c:
            green_real = green_real + jnp.where(diagonal, inv_real[s : s + 1, span(c)], 0.0)
            green_imag = green_imag + jnp.where(diagonal, inv_imag[s : s + 1, span(c)], 0.0)
            middles[r] = jnp.sum(jnp.where(diagonal, green_imag, 0.0), axis=0, keepdims=True)
            density[s : s + 1, span(r)] += -weight * middles[r]
        if packed is not None:
            if r == c:
                packed[span(middle_slot(parts, r)), :] = jnp.where(
                    rows <= cols, green_real, green_imag
                ).astype(BF16)
            else:
                packed[span(pair_slot(parts, r, c, 0)), :] = green_real.astype(BF16)
                packed[span(pair_slot(parts, r, c, 1)), :] = green_imag.astype(BF16)
            return
        if g is None:
            return
        for half, green in ((0, green_real), (1, green_imag)):
            rounded = green.astype(BF16)
            g[span(r), span(place(parts, half, c))] = rounded
            if r != c:
                g[span(c), span(place(parts, half, r))] = rounded.T

    turned = times_turned(left[...])
    far = turned[2 * last :, :]
    near = turned[: 2 * last, :]
    for c in range(parts):
        finish(parts - 1, c, far[:LANE, span(c)], far[LANE:, span(c)])
    for r in range(parts - 1):
        for c in range(r + 1):
            finish(r, c, near[span(r), span(c)], near[last:, :][span(r), span(c)])
    if packed is not None:
        rest = jnp.zeros((16 - parts, LANE), F32)
        at = parts * parts * LANE
        packed[at : at + 16, :] = jnp.concatenate(
            [middles[r] for r in range(parts)] + [rest], axis=0
        ).astype(BF16)


def coupling_of(base, wave, cosine):
    return (base.astype(F32) + cosine * wave.astype(F32)).astype(BF16)


def first_segment(coupled_of, inv_real, inv_imag, scales, weight, g, left, sent, density):
    slabs, orbitals = inv_real.shape
    parts = orbitals // LANE
    density[0:1, :] += -weight * inv_imag[0:1, :]
    for s in range(1, slabs):
        coupled = coupled_of(s)
        if s == 1:
            wide = coupled.astype(F32)
            for half, inv in ((0, inv_real), (1, inv_imag)):
                piece = (wide * inv[0:1, :].astype(BF16).astype(F32)).astype(BF16)
                for c in range(parts):
                    store_left(left, piece[:, span(c)], half, c, parts)
        else:
            times_carried(coupled, g, left, parts)

        def times_turned(rows):
            return lax.dot_general(
                rows, coupled, (((1,), (1,)), ((), ())), preferred_element_type=F32
            )

        finish_slab(
            s, times_turned, left, g, sent if s == slabs - 1 else None,
            inv_real, inv_imag, scales, weight, density, parts,
        )


def own_kernel(
    impulse_count,
    counts, constants_hbm, contact_hbm, onsite_hbm, hopping_hbm, potential_hbm, base_hbm, wave_hbm,
    sent, density, spread,
    constants, contact, tables, base, wave, scales, g, left, small_sem, table_sem, couple_sem,
):
    slabs, orbitals = onsite_hbm.shape
    parts = orbitals // LANE
    position = lax.axis_index("en")
    density[...] = jnp.zeros_like(density)
    lanes = lax.broadcasted_iota(jnp.int32, spread.shape, 1)
    spread[...] = jnp.where(lanes == lax.axis_index("kt"), counts[0], 0)

    @pl.when(position == 0)
    def _():
        small_copies = [
            pltpu.make_async_copy(source, target, small_sem.at[k])
            for k, (source, target) in enumerate(
                ((constants_hbm, constants), (contact_hbm, contact))
            )
        ] + [
            pltpu.make_async_copy(source, tables.at[k], table_sem.at[k])
            for k, source in enumerate((onsite_hbm, hopping_hbm, potential_hbm))
        ]
        couple_copies = {
            s: (
                pltpu.make_async_copy(base_hbm.at[s], base.at[s], couple_sem.at[0, s]),
                pltpu.make_async_copy(wave_hbm.at[s], wave.at[s], couple_sem.at[1, s]),
            )
            for s in range(1, slabs)
        }
        for copy in small_copies:
            copy.start()
        for s in range(1, slabs):
            for copy in couple_copies[s]:
                copy.start()
        for copy in small_copies:
            copy.wait()
        cosine, energy, weight = entry_amounts(
            constants, impulse_count, lax.axis_index("kt"), jnp.int32(0)
        )
        inv_real, inv_imag = inverse_diagonal(
            position, cosine, energy, contact, tables.at[0], tables.at[1], tables.at[2]
        )
        form_scales(range(1, slabs), inv_real, inv_imag, scales, parts)

        def coupled_of(s):
            for copy in couple_copies[s]:
                copy.wait()
            return coupling_of(base[s], wave[s], cosine)

        first_segment(coupled_of, inv_real, inv_imag, scales, weight, g, left, sent, density)


def prepare(cosine, weight, inv_real, inv_imag, base, wave, couple, turned, scales, entry):
    slabs, orbitals = inv_real.shape
    parts = orbitals // LANE
    form_scales(range(slabs), inv_real, inv_imag, scales, parts)
    entry[:slabs, :] = inv_real
    entry[slabs : 2 * slabs, :] = inv_imag
    entry[2 * slabs :, :] = jnp.full((slabs, orbitals), weight, F32)
    for s in range(slabs):
        coupled = coupling_of(base[s], wave[s], cosine)
        couple[s] = coupled
        for r in range(parts):
            for c in range(parts):
                turned[s, span(c), span(r)] = coupled[span(r), span(c)].T


def prepare_kernel(
    impulse_count,
    constants, contact, onsite, hopping, potential, base, wave,
    couple, turned, scales, entry,
):
    position = lax.axis_index("en")

    @pl.when(position > 0)
    def _():
        cosine, energy, weight = entry_amounts(
            constants, impulse_count, lax.axis_index("kt"), jnp.int32(0)
        )
        inv_real, inv_imag = inverse_diagonal(
            position, cosine, energy, contact, onsite, hopping, potential
        )
        prepare(cosine, weight, inv_real, inv_imag, base, wave, couple, turned, scales, entry)


def extra_kernel(
    impulse_count,
    constants, contact, counts, onsite, hopping, potential, base, wave, so_far,
    sent, density, couple, turned, scales, entry,
    g, left,
):
    slabs, orbitals = onsite.shape
    parts = orbitals // LANE
    position = lax.axis_index("en")
    density[...] = so_far[...]
    momentum, level = extra_item(counts, lax.axis_index("kt"))
    cosine, energy, weight = entry_amounts(constants, impulse_count, momentum, level)
    inv_real, inv_imag = inverse_diagonal(
        position, cosine, energy, contact, onsite, hopping, potential
    )

    @pl.when(position == 0)
    def _():
        form_scales(range(1, slabs), inv_real, inv_imag, scales, parts)

        def coupled_of(s):
            return coupling_of(base[s], wave[s], cosine)

        first_segment(coupled_of, inv_real, inv_imag, scales, weight, g, left, sent, density)

    @pl.when(position > 0)
    def _():
        prepare(cosine, weight, inv_real, inv_imag, base, wave, couple, turned, scales, entry)


def stage_kernel(stage, last_stage, couple, turned, scales, entry, arrived, so_far, *refs):
    if last_stage:
        density, g, left = refs
        sent = None
    else:
        sent, density, g, left = refs
    slabs, orbitals = so_far.shape
    parts = orbitals // LANE
    density[...] = so_far[...]

    @pl.when(lax.axis_index("en") == stage)
    def _():
        inv_real = entry[:slabs, :]
        inv_imag = entry[slabs : 2 * slabs, :]
        weight = entry[2 * slabs : 2 * slabs + 1, :LANE]
        unpack_blocks(arrived, g, parts)
        for s in range(slabs):
            times_carried(couple[s], g, left, parts)

            def times_turned(rows):
                return jnp.dot(rows, turned[s], preferred_element_type=F32)

            final = s == slabs - 1
            finish_slab(
                s, times_turned, left, None if final else g, sent if final else None,
                inv_real, inv_imag, scales, weight, density, parts,
            )


def vmem_call(kernel, outs, operands, in_specs, scratch, name, flops, **more):
    vmem = pl.BlockSpec(memory_space=pltpu.VMEM)
    return pl.pallas_call(
        kernel,
        out_shape=tuple(outs),
        in_specs=in_specs,
        out_specs=(vmem,) * len(outs),
        scratch_shapes=scratch,
        compiler_params=pltpu.CompilerParams(vmem_limit_bytes=24 * 2**20),
        cost_estimate=pl.CostEstimate(flops=flops, bytes_accessed=2**21, transcendentals=0),
        name=name,
        **more,
    )(*operands)


def last_kernel(gathered, doping, inverse, summed, potential):
    total = jnp.sum(gathered[...], axis=0)
    summed[...] = total
    potential[...] = lax.dot_general(
        total - doping[...],
        inverse[...],
        (((1,), (1,)), ((), ())),
        preferred_element_type=F32,
        precision=lax.Precision.HIGHEST,
    )


def gather_over(values, axis):
    copies = jnp.broadcast_to(values[None], (lax.axis_size(axis),) + values.shape)
    return lax.all_to_all(copies, axis, 0, 0)


def body(
    counts,
    contact_slabs,
    onsite,
    hopping,
    potential_in,
    couple_base,
    couple_wave,
    doping,
    poisson_inverse,
):
    kt_size = lax.axis_size("kt")
    en_size = lax.axis_size("en")
    slabs, orbitals = onsite.shape
    parts = orbitals // LANE
    impulse_count = counts.shape[0] * kt_size
    constants = jnp.asarray(item_constants(impulse_count))
    smem = pl.BlockSpec(memory_space=pltpu.SMEM)
    hbm = pl.BlockSpec(memory_space=pltpu.HBM)
    vmem = pl.BlockSpec(memory_space=pltpu.VMEM)
    flops = 2 * slabs * orbitals**3

    def forward(block, stage):
        return lax.ppermute(block, "en", [(stage, stage + 1)])

    block_shape = jax.ShapeDtypeStruct((packed_rows(orbitals), LANE), BF16)
    density_shape = jax.ShapeDtypeStruct((slabs, orbitals), F32)
    couple_shape = jax.ShapeDtypeStruct((slabs, orbitals, orbitals), BF16)
    scales_shape = jax.ShapeDtypeStruct((slabs, scale_rows(parts), LANE), F32)
    entry_shape = jax.ShapeDtypeStruct((3 * slabs, orbitals), F32)
    scales_scratch = pltpu.VMEM(scales_shape.shape, F32)
    work = [
        pltpu.VMEM((orbitals, 2 * orbitals), BF16),
        pltpu.VMEM((2 * orbitals, orbitals), BF16),
    ]

    given = (constants, contact_slabs, onsite, hopping, potential_in, couple_base, couple_wave)
    pinned = [pltpu.with_memory_space_constraint(t, pltpu.HBM) for t in given]
    made_shapes = (couple_shape, couple_shape, scales_shape, entry_shape)
    block, density, spread = vmem_call(
        functools.partial(own_kernel, impulse_count),
        (block_shape, density_shape, jax.ShapeDtypeStruct((1, impulse_count), jnp.int32)),
        [counts] + pinned,
        [smem] + [hbm] * len(pinned),
        [
            pltpu.SMEM(constants.shape, F32),
            pltpu.SMEM(contact_slabs.shape, jnp.int32),
            pltpu.VMEM((3, slabs, orbitals), F32),
            pltpu.VMEM((slabs, orbitals, orbitals), BF16),
            pltpu.VMEM((slabs, orbitals, orbitals), BF16),
            scales_scratch,
        ]
        + work
        + [
            pltpu.SemaphoreType.DMA((2,)),
            pltpu.SemaphoreType.DMA((3,)),
            pltpu.SemaphoreType.DMA((2, slabs)),
        ],
        "first_own",
        3 * flops,
    )
    arrived_own = forward(block, 0)
    made_own = vmem_call(
        functools.partial(prepare_kernel, impulse_count),
        made_shapes,
        given,
        [smem] * 2 + [vmem] * 5,
        [],
        "prepare_own",
        flops,
    )
    spread, *made_own = lax.optimization_barrier((spread, *made_own))
    counts_all = lax.psum(spread, "kt")
    held, density, *made_extra = vmem_call(
        functools.partial(extra_kernel, impulse_count),
        (block_shape, density_shape) + made_shapes,
        given[:2] + (counts_all,) + given[2:] + (density,),
        [smem] * 3 + [vmem] * 6,
        work,
        "first_extra",
        3 * flops,
        input_output_aliases={8: 1},
    )

    def run_stage(stage, made, arrived, density, name):
        last_stage = stage == en_size - 1
        results = vmem_call(
            functools.partial(stage_kernel, stage, last_stage),
            (density_shape,) if last_stage else (block_shape, density_shape),
            (*made, arrived, density),
            [vmem] * 6,
            work,
            f"stage_{stage}_{name}",
            4 * flops,
            input_output_aliases={5: 0 if last_stage else 1},
        )
        return (None, *results) if last_stage else results

    for stage in range(1, en_size):
        arrived_own, held = lax.optimization_barrier((arrived_own, held))
        arrived_extra = forward(held, stage - 1)
        block, density = run_stage(stage, made_own, arrived_own, density, "own")
        if stage < en_size - 1:
            arrived_own = forward(block, stage)
        held, density = run_stage(stage, made_extra, arrived_extra, density, "extra")
    return pl.pallas_call(
        last_kernel,
        out_shape=(density_shape, density_shape),
        in_specs=[vmem] * 3,
        out_specs=(vmem, vmem),
        name="last",
    )(gather_over(density, "kt"), doping, poisson_inverse)


def solution(mesh):
    return jax.shard_map(
        body,
        mesh=mesh,
        in_specs=(
            P("kt"),
            P(),
            P("en", None),
            P("en", None),
            P("en", None),
            P("en", None, None),
            P("en", None, None),
            P("en", None),
            P(),
        ),
        out_specs=(P("en", None), P("en", None)),
        check_vma=False,
    )
```

```python
import functools

import jax
import jax.numpy as jnp
import numpy as np
from jax import lax
from jax.experimental import pallas as pl
from jax.experimental.pallas import tpu as pltpu
from jax.sharding import PartitionSpec as P

EMAX = 4
LANE = 128
F32 = jnp.float32
BF16 = jnp.bfloat16

bottom_sample_mark = -1.0
sample_gap = 0.25
electrode_filling = -0.5
boltzmann_spread = 0.1
broadening = 1.0
contact_width = 0.5


def item_constants(impulse_count):
    wave = np.float32(np.pi) * (np.arange(impulse_count, dtype=np.float32) + np.float32(0.5))
    cosine = np.cos(wave / np.float32(impulse_count))
    energy = bottom_sample_mark + sample_gap * np.arange(EMAX)
    weight = sample_gap / (1.0 + np.exp((energy - electrode_filling) / boltzmann_spread)) / np.pi
    return np.concatenate([cosine, weight]).astype(np.float32)


def span(k):
    return slice(k * LANE, (k + 1) * LANE)


def place(parts, half, c):
    if c == parts - 1:
        return parts - 1 + half
    return c if half == 0 else parts + 1 + c


def blocks_on_or_below(parts):
    return [(r, c) for r in range(parts) for c in range(r + 1)]


def packed_rows(orbitals):
    parts = orbitals // LANE
    return parts * parts * LANE + 16


def pairs_below(parts):
    return [(r, c) for r in range(parts) for c in range(r)]


def pair_slot(parts, r, c, half):
    return 2 * pairs_below(parts).index((r, c)) + half


def middle_slot(parts, r):
    return parts * (parts - 1) + r


def tile_indices():
    rows = lax.broadcasted_iota(jnp.int32, (LANE, LANE), 0)
    cols = lax.broadcasted_iota(jnp.int32, (LANE, LANE), 1)
    return rows, cols


def unpack_blocks(packed, put, parts):
    rows, cols = tile_indices()
    for r, c in pairs_below(parts):
        for half in range(2):
            block = packed[span(pair_slot(parts, r, c, half)), :]
            put(half, r, c, block)
            put(half, c, r, block.T)
    at = parts * parts * LANE
    for r in range(parts):
        block = packed[span(middle_slot(parts, r)), :]
        turned = block.T
        middle = packed[at : at + 16, :][r : r + 1, :]
        put(0, r, r, jnp.where(rows <= cols, block, turned))
        put(1, r, r, jnp.where(rows > cols, block, jnp.where(rows == cols, middle, turned)))


def pack_block(packed, r, c, green_real, green_imag, parts):
    rows, cols = tile_indices()
    if r == c:
        packed[span(middle_slot(parts, r)), :] = jnp.where(
            rows <= cols, green_real, green_imag
        ).astype(BF16)
    else:
        packed[span(pair_slot(parts, r, c, 0)), :] = green_real.astype(BF16)
        packed[span(pair_slot(parts, r, c, 1)), :] = green_imag.astype(BF16)


def pack_middles(packed, middles, parts):
    rest = jnp.zeros((16 - parts, LANE), F32)
    at = parts * parts * LANE
    packed[at : at + 16, :] = jnp.concatenate(middles + [rest], axis=0).astype(BF16)


def diagonal_row(block):
    rows, cols = tile_indices()
    return jnp.sum(jnp.where(rows == cols, block, 0.0), axis=0, keepdims=True)


def takes_first_levels():
    return lax.axis_index("kt") % 2 == 1


def first_level_item(slot):
    return lax.axis_index("kt") - 1 + slot, jnp.int32(0)


def item_of(counts, slot):
    wanted = lax.axis_index("kt") + slot

    def one(k, state):
        momentum, before = state
        extra = counts[k] - 1
        take = jnp.logical_and(momentum == k, before + extra <= wanted)
        return (jnp.where(take, k + 1, momentum), jnp.where(take, before + extra, before))

    momentum, before = lax.fori_loop(0, counts.shape[0], one, (jnp.int32(0), jnp.int32(0)))
    momentum = jnp.minimum(momentum, counts.shape[0] - 1)
    level = jnp.clip(1 + wanted - before, 0, EMAX - 1)
    own_momentum, own_level = first_level_item(slot)
    own = takes_first_levels()
    return jnp.where(own, own_momentum, momentum), jnp.where(own, own_level, level)


def entry_amounts(constants, impulse_count, momentum, level):
    energy = bottom_sample_mark + sample_gap * level.astype(F32)
    return constants[momentum], energy, constants[impulse_count + level]


def inverse_diagonal(position, cosine, energy, contact, onsite, hopping, potential):
    slabs, orbitals = onsite.shape
    diag_real = energy + (-onsite[...] - potential[...]) - cosine * hopping[...]
    slab_in = lax.broadcasted_iota(jnp.int32, (slabs, orbitals), 0) + position * slabs
    at_contact = jnp.logical_or(slab_in == contact[0], slab_in == contact[1])
    diag_imag = broadening + contact_width * at_contact.astype(F32)
    magnitude = diag_real * diag_real + diag_imag * diag_imag
    inv_real = diag_real / magnitude
    inv_imag = -diag_imag / magnitude
    return inv_real, inv_imag


def scale_rows(parts):
    return 2 * len(blocks_on_or_below(parts)) * LANE


def form_scales(slabs_wanted, inv_real, inv_imag, scales, parts):
    slabs = inv_real.shape[0]
    down = jnp.concatenate([inv_real, inv_imag], axis=0).T
    for s in slabs_wanted:
        for k, (r, c) in enumerate(blocks_on_or_below(parts)):
            real_col = down[span(r), s : s + 1]
            imag_col = down[span(r), slabs + s : slabs + s + 1]
            rr = inv_real[s : s + 1, span(c)]
            ri = inv_imag[s : s + 1, span(c)]
            scales[s, span(2 * k), :] = real_col * rr - imag_col * ri
            scales[s, span(2 * k + 1), :] = real_col * ri + imag_col * rr


def store_left(left, piece, half, c, parts):
    last = (parts - 1) * LANE
    left[half * last : (half + 1) * last, span(c)] = piece[:last]
    bottom = 2 * last + half * LANE
    left[bottom : bottom + LANE, span(c)] = piece[last:]


def times_carried(coupled, g, left, parts):
    product = jnp.dot(coupled, g[...], preferred_element_type=F32).astype(BF16)
    for column in range(2 * parts):
        half, c = (
            (0, column)
            if column < parts
            else (1, parts - 1 if column == parts else column - parts - 1)
        )
        store_left(left, product[:, span(column)], half, c, parts)


def finish_slab(
    s, times_turned, left, g, packed, real_row, imag_row, scales, note, parts, local=None
):
    last = (parts - 1) * LANE
    rows, cols = tile_indices()
    diagonal = rows == cols
    numbers = {block: k for k, block in enumerate(blocks_on_or_below(parts))}
    middles = {}

    def finish(r, c, sr, si):
        k = numbers[r, c]
        scale_real = scales[s, span(2 * k), :]
        scale_imag = scales[s, span(2 * k + 1), :]
        green_real = scale_real * sr - scale_imag * si
        green_imag = scale_real * si + scale_imag * sr
        if r == c:
            green_real = green_real + jnp.where(diagonal, real_row[:, span(c)], 0.0)
            green_imag = green_imag + jnp.where(diagonal, imag_row[:, span(c)], 0.0)
            if note is not None:
                middles[r] = diagonal_row(green_imag)
                note(r, middles[r])
        if packed is not None:
            pack_block(packed, r, c, green_real, green_imag, parts)
        if local is not None:
            local[span(2 * k), :] = green_real
            local[span(2 * k + 1), :] = green_imag
        if g is None:
            return
        for half, green in ((0, green_real), (1, green_imag)):
            rounded = green.astype(BF16)
            g[span(r), span(place(parts, half, c))] = rounded
            if r != c:
                g[span(c), span(place(parts, half, r))] = rounded.T

    turned = times_turned(left[...])
    far = turned[2 * last :, :]
    near = turned[: 2 * last, :]
    for c in range(parts):
        finish(parts - 1, c, far[:LANE, span(c)], far[LANE:, span(c)])
    for r in range(parts - 1):
        for c in range(r + 1):
            finish(r, c, near[span(r), span(c)], near[last:, :][span(r), span(c)])
    if packed is not None:
        pack_middles(packed, [middles[r] for r in range(parts)], parts)


def coupling_of(base, wave, cosine):
    return (base.astype(F32) + cosine * wave.astype(F32)).astype(BF16)


def first_segment(
    coupled_of, inv_real, inv_imag, scales, weight, g, left, sent, density, local=None
):
    slabs, orbitals = inv_real.shape
    parts = orbitals // LANE
    if density is not None:
        density[0:1, :] += -weight * inv_imag[0:1, :]
    for s in range(1, slabs):
        coupled = coupled_of(s)
        if s == 1:
            wide = coupled.astype(F32)
            for half, inv in ((0, inv_real), (1, inv_imag)):
                piece = (wide * inv[0:1, :].astype(BF16).astype(F32)).astype(BF16)
                for c in range(parts):
                    store_left(left, piece[:, span(c)], half, c, parts)
        else:
            times_carried(coupled, g, left, parts)

        def times_turned(rows):
            return lax.dot_general(
                rows, coupled, (((1,), (1,)), ((), ())), preferred_element_type=F32
            )

        def note(r, middle):
            density[s : s + 1, span(r)] += -weight * middle

        final = s == slabs - 1
        finish_slab(
            s, times_turned, left, None if final else g, sent if final else None,
            inv_real[s : s + 1, :], inv_imag[s : s + 1, :], scales, None if density is None else note, parts,
            local if final else None,
        )


def copies_of_constants(constants_hbm, contact_hbm, constants, contact, sem):
    return [
        pltpu.make_async_copy(constants_hbm, constants, sem.at[0]),
        pltpu.make_async_copy(contact_hbm, contact, sem.at[1]),
    ]


def copies_of_couplings(base_hbm, wave_hbm, base, wave, sem, slabs_wanted):
    return {
        s: (
            pltpu.make_async_copy(base_hbm.at[s], base.at[s], sem.at[0, s]),
            pltpu.make_async_copy(wave_hbm.at[s], wave.at[s], sem.at[1, s]),
        )
        for s in slabs_wanted
    }


def lead_kernel(
    impulse_count,
    constants_hbm, contact_hbm, onsite_hbm, hopping_hbm, potential_hbm, base_hbm, wave_hbm,
    sent, density, base, wave,
    constants, contact, tables, scales, g, left, small_sem, table_sem, couple_sem,
):
    slabs, orbitals = onsite_hbm.shape
    parts = orbitals // LANE
    position = lax.axis_index("en")
    density[...] = jnp.zeros_like(density)

    @pl.when(position == 0)
    def _():
        small_copies = copies_of_constants(
            constants_hbm, contact_hbm, constants, contact, small_sem
        ) + [
            pltpu.make_async_copy(source, tables.at[k], table_sem.at[k])
            for k, source in enumerate((onsite_hbm, hopping_hbm, potential_hbm))
        ]
        couple_copies = copies_of_couplings(
            base_hbm, wave_hbm, base, wave, couple_sem, range(1, slabs)
        )
        for copy in small_copies:
            copy.start()
        for s in couple_copies:
            for copy in couple_copies[s]:
                copy.start()
        for copy in small_copies:
            copy.wait()

        @pl.when(takes_first_levels())
        def _():
            momentum, level = first_level_item(0)
            cosine, energy, weight = entry_amounts(
                constants, impulse_count, momentum, level
            )
            inv_real, inv_imag = inverse_diagonal(
                position, cosine, energy, contact, tables.at[0], tables.at[1], tables.at[2]
            )
            form_scales(range(1, slabs), inv_real, inv_imag, scales, parts)

            def coupled_of(s):
                for copy in couple_copies[s]:
                    copy.wait()
                return coupling_of(base[s], wave[s], cosine)

            first_segment(
                coupled_of, inv_real, inv_imag, scales, weight, g, left, sent, density
            )

        @pl.when(jnp.logical_not(takes_first_levels()))
        def _():
            for s in couple_copies:
                for copy in couple_copies[s]:
                    copy.wait()


    @pl.when(position > 0)
    def _():
        couple_copies = copies_of_couplings(
            base_hbm, wave_hbm, base, wave, couple_sem, range(slabs)
        )
        for s in couple_copies:
            for copy in couple_copies[s]:
                copy.start()
        for s in couple_copies:
            for copy in couple_copies[s]:
                copy.wait()


def begin_kernel(
    impulse_count, slot,
    constants, contact, counts, onsite, hopping, potential, base, wave, so_far, held,
    density, sent,
    scales, g, left,
):
    del held
    slabs, orbitals = onsite.shape
    parts = orbitals // LANE
    position = lax.axis_index("en")
    density[...] = so_far[...]
    active = position == 0
    if slot == 0:
        active = jnp.logical_and(active, jnp.logical_not(takes_first_levels()))

    @pl.when(active)
    def _():
        momentum, level = item_of(counts, slot)
        cosine, energy, weight = entry_amounts(constants, impulse_count, momentum, level)
        inv_real, inv_imag = inverse_diagonal(
            position, cosine, energy, contact, onsite, hopping, potential
        )
        form_scales(range(1, slabs), inv_real, inv_imag, scales, parts)

        def coupled_of(s):
            return coupling_of(base[s], wave[s], cosine)

        first_segment(coupled_of, inv_real, inv_imag, scales, weight, g, left, sent, density)


def prepare(cosine, weight, inv_real, inv_imag, base, wave, couple, turned, scales, entry):
    slabs, orbitals = inv_real.shape
    parts = orbitals // LANE
    form_scales(range(slabs), inv_real, inv_imag, scales, parts)
    for s in range(slabs):
        entry[s] = jnp.broadcast_to(inv_real[s : s + 1, :], entry.shape[1:])
        entry[slabs + s] = jnp.broadcast_to(inv_imag[s : s + 1, :], entry.shape[1:])
    entry[2 * slabs] = jnp.full(entry.shape[1:], weight, F32)

    def one(s, carry):
        coupled = coupling_of(base[s], wave[s], cosine)
        couple[s] = coupled
        for r in range(parts):
            for c in range(parts):
                turned[s, span(c), span(r)] = coupled[span(r), span(c)].T
        return carry

    lax.fori_loop(0, slabs, one, 0)


def prepare_kernel(
    impulse_count,
    constants, contact, counts, onsite, hopping, potential, base, wave,
    couple_0, turned_0, scales_0, entry_0,
    couple_1, turned_1, scales_1, entry_1,
):
    position = lax.axis_index("en")

    @pl.when(position > 0)
    def _():
        for slot, made in (
            (0, (couple_0, turned_0, scales_0, entry_0)),
            (1, (couple_1, turned_1, scales_1, entry_1)),
        ):
            momentum, level = item_of(counts, slot)
            cosine, energy, weight = entry_amounts(constants, impulse_count, momentum, level)
            inv_real, inv_imag = inverse_diagonal(
                position, cosine, energy, contact, onsite, hopping, potential
            )
            prepare(cosine, weight, inv_real, inv_imag, base, wave, *made)


def stage_kernel(stage, last_stage, couple, turned, scales, entry, arrived, so_far, *refs):
    if last_stage:
        density, g, left, noted = refs
        sent = None
    else:
        sent, density, g, left, noted = refs
    slabs, orbitals = so_far.shape
    parts = orbitals // LANE
    density[...] = so_far[...]

    @pl.when(lax.axis_index("en") == stage)
    def _():
        def put(half, r, c, block):
            column = place(parts, half, c)
            g[span(r), span(column)] = block

        unpack_blocks(arrived, put, parts)
        def slab(s, final):
            times_carried(couple[s], g, left, parts)

            def times_turned(rows):
                return jnp.dot(rows, turned[s], preferred_element_type=F32)

            def note(r, middle):
                noted[s, 0:1, span(r)] = middle

            finish_slab(
                s, times_turned, left, None if final else g, sent if final else None,
                entry[s, 0:1, :], entry[slabs + s, 0:1, :], scales, note, parts,
            )

        def inner(s, carry):
            slab(s, False)
            return carry

        lax.fori_loop(0, slabs - 1, inner, 0)
        slab(slabs - 1, True)
        for s in range(slabs):
            density[s : s + 1, :] += -entry[2 * slabs, 0:1, :] * noted[s, 0:1, :]


def operator_kernel(stage, couple, turned, scales, entry, local, carrier, cross, g, left):
    slabs, orbitals, _ = couple.shape
    parts = orbitals // LANE

    @pl.when(lax.axis_index("en") == stage)
    def _():
        inv_real = jnp.concatenate([entry[s, 0:1, :] for s in range(slabs)], axis=0)
        inv_imag = jnp.concatenate([entry[slabs + s, 0:1, :] for s in range(slabs)], axis=0)
        first_segment(
            lambda s: couple[s], inv_real, inv_imag, scales, None, g, left, None, None, local
        )
        down = jnp.concatenate([inv_real, inv_imag], axis=0).T
        for s in range(slabs):
            real_col = down[:, s : s + 1]
            imag_col = down[:, slabs + s : slabs + s + 1]
            if s == 0:
                wide = couple[0].astype(F32)
                real, imag = real_col * wide, imag_col * wide
            else:
                product = jnp.dot(couple[s], carrier[...], preferred_element_type=F32)
                from_real, from_imag = product[:, :orbitals], product[:, orbitals:]
                real = real_col * from_real - imag_col * from_imag
                imag = real_col * from_imag + imag_col * from_real
            carrier[:, :orbitals] = real.astype(BF16)
            carrier[:, orbitals:] = imag.astype(BF16)
        for r in range(parts):
            for c in range(parts):
                real = carrier[span(r), span(c)].T
                imag = carrier[span(r), span(parts + c)].T
                cross[span(c), span(r)] = real
                cross[span(parts + c), span(parts + r)] = real
                cross[span(c), span(parts + r)] = imag
                cross[span(parts + c), span(r)] = -imag


def pass_kernel(stage, local, carrier, cross, arrived, sent, wide, half_way):
    orbitals = carrier.shape[0]
    parts = orbitals // LANE

    @pl.when(lax.axis_index("en") == stage)
    def _():
        def put(half, r, c, block):
            if half == 0:
                wide[span(r), span(c)] = block
                wide[span(parts + r), span(parts + c)] = block
            else:
                wide[span(r), span(parts + c)] = block
                wide[span(parts + r), span(c)] = -block

        unpack_blocks(arrived, put, parts)
        half_way[...] = jnp.dot(carrier[...], wide[...], preferred_element_type=F32).astype(BF16)
        out = jnp.dot(half_way[...], cross[...], preferred_element_type=F32)
        middles = []
        for k, (r, c) in enumerate(blocks_on_or_below(parts)):
            green_real = local[span(2 * k), :] + out[span(r), span(c)]
            green_imag = local[span(2 * k + 1), :] + out[span(r), span(parts + c)]
            pack_block(sent, r, c, green_real, green_imag, parts)
            if r == c:
                middles.append(diagonal_row(green_imag))
        pack_middles(sent, middles, parts)


def vmem_call(kernel, outs, operands, in_specs, scratch, name, flops, **more):
    vmem = pl.BlockSpec(memory_space=pltpu.VMEM)
    return pl.pallas_call(
        kernel,
        out_shape=tuple(outs),
        in_specs=in_specs,
        out_specs=(vmem,) * len(outs),
        scratch_shapes=scratch,
        compiler_params=pltpu.CompilerParams(vmem_limit_bytes=16 * 2**20),
        cost_estimate=pl.CostEstimate(flops=flops, bytes_accessed=2**21, transcendentals=0),
        name=name,
        **more,
    )(*operands)


def split_kernel(inverse, high, middle, low):
    for r in range(inverse.shape[0] // LANE):
        for c in range(inverse.shape[1] // LANE):
            block = inverse[span(r), span(c)].T
            for part in (high, middle, low):
                rounded = block.astype(BF16)
                part[span(c), span(r)] = rounded
                block = block - rounded.astype(F32)


def last_kernel(gathered, doping, high, middle, low, summed, potential):
    total = jnp.sum(gathered[...], axis=0)
    summed[...] = total
    rest = total - doping[...]
    pieces = []
    for _ in range(3):
        pieces.append(rest.astype(BF16).astype(F32))
        rest = rest - pieces[-1]
    rows = total.shape[0]
    answer = jnp.zeros_like(total)
    for count, part in ((1, low), (2, middle), (3, high)):
        padded = -(-3 * rows // 16) * 16 - count * rows
        stacked = jnp.concatenate(
            pieces[:count] + [jnp.zeros((padded, total.shape[1]), F32)], axis=0
        ).astype(BF16)
        product = jnp.dot(stacked, part[...], preferred_element_type=F32)
        for k in reversed(range(count)):
            answer = answer + product[k * rows : (k + 1) * rows]
    potential[...] = answer


def gather_over(values, axis):
    copies = jnp.broadcast_to(values[None], (lax.axis_size(axis),) + values.shape)
    return lax.all_to_all(copies, axis, 0, 0)


def body(
    counts,
    contact_slabs,
    onsite,
    hopping,
    potential_in,
    couple_base,
    couple_wave,
    doping,
    poisson_inverse,
):
    kt_size = lax.axis_size("kt")
    en_size = lax.axis_size("en")
    slabs, orbitals = onsite.shape
    parts = orbitals // LANE
    impulse_count = counts.shape[0] * kt_size
    constants = jnp.asarray(item_constants(impulse_count))
    smem = pl.BlockSpec(memory_space=pltpu.SMEM)
    hbm = pl.BlockSpec(memory_space=pltpu.HBM)
    vmem = pl.BlockSpec(memory_space=pltpu.VMEM)
    flops = 2 * slabs * orbitals**3

    def forward(block, stage):
        return lax.ppermute(block, "en", [(stage, stage + 1)])

    block_shape = jax.ShapeDtypeStruct((packed_rows(orbitals), LANE), BF16)
    density_shape = jax.ShapeDtypeStruct((slabs, orbitals), F32)
    couple_shape = jax.ShapeDtypeStruct((slabs, orbitals, orbitals), BF16)
    scales_shape = jax.ShapeDtypeStruct((slabs, scale_rows(parts), LANE), F32)
    entry_shape = jax.ShapeDtypeStruct((2 * slabs + 1, 8, orbitals), F32)
    scales_scratch = pltpu.VMEM(scales_shape.shape, F32)
    work = [
        pltpu.VMEM((orbitals, 2 * orbitals), BF16),
        pltpu.VMEM((2 * orbitals, orbitals), BF16),
    ]

    counts_all = lax.all_to_all(jnp.tile(counts, kt_size), "kt", 0, 0, tiled=True)
    given = (constants, contact_slabs, onsite, hopping, potential_in, couple_base, couple_wave)
    pinned = [pltpu.with_memory_space_constraint(t, pltpu.HBM) for t in given]
    block, density, *loaded = vmem_call(
        functools.partial(lead_kernel, impulse_count),
        (block_shape, density_shape, couple_shape, couple_shape),
        pinned,
        [hbm] * len(pinned),
        [
            pltpu.SMEM(constants.shape, F32),
            pltpu.SMEM(contact_slabs.shape, jnp.int32),
            pltpu.VMEM((3, slabs, orbitals), F32),
            scales_scratch,
        ]
        + work
        + [
            pltpu.SemaphoreType.DMA((2,)),
            pltpu.SemaphoreType.DMA((3,)),
            pltpu.SemaphoreType.DMA((2, slabs)),
        ],
        "lead",
        3 * flops,
    )
    block, counts_all = lax.optimization_barrier((block, counts_all))
    small = (constants, contact_slabs, counts_all, onsite, hopping, potential_in)

    def begin(slot, density, held):
        return vmem_call(
            functools.partial(begin_kernel, impulse_count, slot),
            (density_shape, block_shape),
            (*small, *loaded, density, held),
            [smem] * 3 + [vmem] * 7,
            [scales_scratch] + work,
            f"begin_{slot}",
            3 * flops,
            input_output_aliases={8: 0, 9: 1},
        )

    density, block = begin(0, density, block)
    arrived = [forward(block, 0)]
    density, block = begin(1, density, jnp.zeros(block_shape.shape, BF16))
    arrived.append(forward(block, 0))
    made = vmem_call(
        functools.partial(prepare_kernel, impulse_count),
        (couple_shape, couple_shape, scales_shape, entry_shape) * 2,
        (*small, *loaded),
        [smem] * 3 + [vmem] * 5,
        [],
        "prepare",
        flops,
    )
    made = (made[:4], made[4:])

    def run_stage(stage, made, arrived, density, name, last_stage):
        results = vmem_call(
            functools.partial(stage_kernel, stage, last_stage),
            (density_shape,) if last_stage else (block_shape, density_shape),
            (*made, arrived, density),
            [vmem] * 6,
            work + [pltpu.VMEM((slabs, 8, orbitals), F32)],
            f"stage_{stage}_{name}",
            4 * flops,
            input_output_aliases={5: 0 if last_stage else 1},
        )
        return (None, *results) if last_stage else results

    def operator_of(stage, slot):
        return vmem_call(
            functools.partial(operator_kernel, stage),
            (
                jax.ShapeDtypeStruct((scale_rows(parts), LANE), F32),
                jax.ShapeDtypeStruct((orbitals, 2 * orbitals), BF16),
                jax.ShapeDtypeStruct((2 * orbitals, 2 * orbitals), BF16),
            ),
            made[slot],
            [vmem] * 4,
            work,
            f"operator_{stage}_{slot}",
            6 * flops,
        )

    def pass_on(stage, slot, operator, block):
        return vmem_call(
            functools.partial(pass_kernel, stage),
            (block_shape,),
            (*operator, block),
            [vmem] * 4,
            [
                pltpu.VMEM((2 * orbitals, 2 * orbitals), BF16),
                pltpu.VMEM((orbitals, 2 * orbitals), BF16),
            ],
            f"pass_{stage}_{slot}",
            2 * flops,
        )[0]

    by_operator = range(2, en_size - 1)
    operators = {
        stage: [operator_of(stage, slot) for slot in range(2)] for stage in by_operator
    }
    waiting = []
    for stage in range(1, en_size):
        for slot in range(2):
            if stage in by_operator:
                waiting.append((stage, slot, arrived[slot]))
                block = pass_on(stage, slot, operators[stage][slot], arrived[slot])
            else:
                block, density = run_stage(
                    stage, made[slot], arrived[slot], density, f"{slot}", stage == en_size - 1
                )
            if stage < en_size - 1:
                arrived[slot] = forward(block, stage)
        if stage == en_size - 2:
            for early, slot, came in waiting:
                _, density = run_stage(early, made[slot], came, density, f"{slot}_density", True)
    part_shape = jax.ShapeDtypeStruct(poisson_inverse.shape, BF16)
    inverse, _ = lax.optimization_barrier((poisson_inverse, made[1][3]))
    split = vmem_call(
        split_kernel, (part_shape,) * 3, (inverse,), [vmem], [], "split_inverse", 2 * flops
    )
    density, *split = lax.optimization_barrier((density, *split))
    return vmem_call(
        last_kernel,
        (density_shape, density_shape),
        (gather_over(density, "kt"), doping, *split),
        [vmem] * 5,
        [],
        "last",
        flops // slabs,
    )


def solution(mesh):
    return jax.shard_map(
        body,
        mesh=mesh,
        in_specs=(
            P("kt"),
            P(),
            P("en", None),
            P("en", None),
            P("en", None),
            P("en", None, None),
            P("en", None, None),
            P("en", None),
            P(),
        ),
        out_specs=(P("en", None), P("en", None)),
        check_vma=False,
    )
```

```python
import functools

import jax
import jax.numpy as jnp
import numpy as np
from jax import lax
from jax.experimental import pallas as pl
from jax.experimental.pallas import tpu as pltpu
from jax.sharding import PartitionSpec as P

EMAX = 4
LANE = 128
F32 = jnp.float32
BF16 = jnp.bfloat16

bottom_sample_mark = -1.0
sample_gap = 0.25
electrode_filling = -0.5
boltzmann_spread = 0.1
broadening = 1.0
contact_width = 0.5


def item_constants(impulse_count):
    wave = np.float32(np.pi) * (np.arange(impulse_count, dtype=np.float32) + np.float32(0.5))
    cosine = np.cos(wave / np.float32(impulse_count))
    energy = bottom_sample_mark + sample_gap * np.arange(EMAX)
    weight = sample_gap / (1.0 + np.exp((energy - electrode_filling) / boltzmann_spread)) / np.pi
    return np.concatenate([cosine, weight]).astype(np.float32)


def span(k):
    return slice(k * LANE, (k + 1) * LANE)


def place(parts, half, c):
    if c == parts - 1:
        return parts - 1 + half
    return c if half == 0 else parts + 1 + c


def blocks_on_or_below(parts):
    return [(r, c) for r in range(parts) for c in range(r + 1)]


def packed_rows(orbitals):
    parts = orbitals // LANE
    return parts * parts * LANE + 16


def pairs_below(parts):
    return [(r, c) for r in range(parts) for c in range(r)]


def pair_slot(parts, r, c, half):
    return 2 * pairs_below(parts).index((r, c)) + half


def middle_slot(parts, r):
    return parts * (parts - 1) + r


def tile_indices():
    rows = lax.broadcasted_iota(jnp.int32, (LANE, LANE), 0)
    cols = lax.broadcasted_iota(jnp.int32, (LANE, LANE), 1)
    return rows, cols


def unpack_blocks(packed, put, parts):
    rows, cols = tile_indices()
    for r, c in pairs_below(parts):
        for half in range(2):
            block = packed[span(pair_slot(parts, r, c, half)), :]
            put(half, r, c, block)
            put(half, c, r, block.T)
    at = parts * parts * LANE
    for r in range(parts):
        block = packed[span(middle_slot(parts, r)), :]
        turned = block.T
        middle = packed[at : at + 16, :][r : r + 1, :]
        put(0, r, r, jnp.where(rows <= cols, block, turned))
        put(1, r, r, jnp.where(rows > cols, block, jnp.where(rows == cols, middle, turned)))


def pack_block(packed, r, c, green_real, green_imag, parts):
    rows, cols = tile_indices()
    if r == c:
        packed[span(middle_slot(parts, r)), :] = jnp.where(
            rows <= cols, green_real, green_imag
        ).astype(BF16)
    else:
        packed[span(pair_slot(parts, r, c, 0)), :] = green_real.astype(BF16)
        packed[span(pair_slot(parts, r, c, 1)), :] = green_imag.astype(BF16)


def pack_middles(packed, middles, parts):
    rest = jnp.zeros((16 - parts, LANE), F32)
    at = parts * parts * LANE
    packed[at : at + 16, :] = jnp.concatenate(middles + [rest], axis=0).astype(BF16)


def diagonal_row(block):
    rows, cols = tile_indices()
    return jnp.sum(jnp.where(rows == cols, block, 0.0), axis=0, keepdims=True)


def takes_first_levels():
    return lax.axis_index("kt") % 2 == 1


def first_level_item(slot):
    return lax.axis_index("kt") - 1 + slot, jnp.int32(0)


def item_of(counts, slot):
    wanted = lax.axis_index("kt") + slot

    def one(k, state):
        momentum, before = state
        extra = counts[k] - 1
        take = jnp.logical_and(momentum == k, before + extra <= wanted)
        return (jnp.where(take, k + 1, momentum), jnp.where(take, before + extra, before))

    momentum, before = lax.fori_loop(0, counts.shape[0], one, (jnp.int32(0), jnp.int32(0)))
    momentum = jnp.minimum(momentum, counts.shape[0] - 1)
    level = jnp.clip(1 + wanted - before, 0, EMAX - 1)
    own_momentum, own_level = first_level_item(slot)
    own = takes_first_levels()
    return jnp.where(own, own_momentum, momentum), jnp.where(own, own_level, level)


def entry_amounts(constants, impulse_count, momentum, level):
    energy = bottom_sample_mark + sample_gap * level.astype(F32)
    return constants[momentum], energy, constants[impulse_count + level]


def inverse_diagonal(position, cosine, energy, contact, onsite, hopping, potential):
    slabs, orbitals = onsite.shape
    diag_real = energy + (-onsite[...] - potential[...]) - cosine * hopping[...]
    slab_in = lax.broadcasted_iota(jnp.int32, (slabs, orbitals), 0) + position * slabs
    at_contact = jnp.logical_or(slab_in == contact[0], slab_in == contact[1])
    diag_imag = broadening + contact_width * at_contact.astype(F32)
    magnitude = diag_real * diag_real + diag_imag * diag_imag
    inv_real = diag_real / magnitude
    inv_imag = -diag_imag / magnitude
    return inv_real, inv_imag


def scale_rows(parts):
    return 2 * len(blocks_on_or_below(parts)) * LANE


def form_scales(slabs_wanted, inv_real, inv_imag, scales, parts):
    slabs = inv_real.shape[0]
    down = jnp.concatenate([inv_real, inv_imag], axis=0).T
    for s in slabs_wanted:
        for k, (r, c) in enumerate(blocks_on_or_below(parts)):
            real_col = down[span(r), s : s + 1]
            imag_col = down[span(r), slabs + s : slabs + s + 1]
            rr = inv_real[s : s + 1, span(c)]
            ri = inv_imag[s : s + 1, span(c)]
            scales[s, span(2 * k), :] = real_col * rr - imag_col * ri
            scales[s, span(2 * k + 1), :] = real_col * ri + imag_col * rr


def store_left(left, piece, half, c, parts):
    last = (parts - 1) * LANE
    left[half * last : (half + 1) * last, span(c)] = piece[:last]
    bottom = 2 * last + half * LANE
    left[bottom : bottom + LANE, span(c)] = piece[last:]


def times_carried(coupled, g, left, parts):
    product = jnp.dot(coupled, g[...], preferred_element_type=F32).astype(BF16)
    for column in range(2 * parts):
        half, c = (
            (0, column)
            if column < parts
            else (1, parts - 1 if column == parts else column - parts - 1)
        )
        store_left(left, product[:, span(column)], half, c, parts)


def finish_slab(
    s, times_turned, left, g, packed, real_row, imag_row, scales, note, parts, local=None
):
    last = (parts - 1) * LANE
    rows, cols = tile_indices()
    diagonal = rows == cols
    numbers = {block: k for k, block in enumerate(blocks_on_or_below(parts))}
    middles = {}

    def finish(r, c, sr, si):
        k = numbers[r, c]
        scale_real = scales[s, span(2 * k), :]
        scale_imag = scales[s, span(2 * k + 1), :]
        green_real = scale_real * sr - scale_imag * si
        green_imag = scale_real * si + scale_imag * sr
        if r == c:
            green_real = green_real + jnp.where(diagonal, real_row[:, span(c)], 0.0)
            green_imag = green_imag + jnp.where(diagonal, imag_row[:, span(c)], 0.0)
            if note is not None:
                middles[r] = diagonal_row(green_imag)
                note(r, middles[r])
        if packed is not None:
            pack_block(packed, r, c, green_real, green_imag, parts)
        if local is not None:
            local[span(2 * k), :] = green_real
            local[span(2 * k + 1), :] = green_imag
        if g is None:
            return
        for half, green in ((0, green_real), (1, green_imag)):
            rounded = green.astype(BF16)
            g[span(r), span(place(parts, half, c))] = rounded
            if r != c:
                g[span(c), span(place(parts, half, r))] = rounded.T

    turned = times_turned(left[...])
    far = turned[2 * last :, :]
    near = turned[: 2 * last, :]
    for c in range(parts):
        finish(parts - 1, c, far[:LANE, span(c)], far[LANE:, span(c)])
    for r in range(parts - 1):
        for c in range(r + 1):
            finish(r, c, near[span(r), span(c)], near[last:, :][span(r), span(c)])
    if packed is not None:
        pack_middles(packed, [middles[r] for r in range(parts)], parts)


def coupling_of(base, wave, cosine):
    return (base.astype(F32) + cosine * wave.astype(F32)).astype(BF16)


def first_segment(
    coupled_of, inv_real, inv_imag, scales, weight, g, left, sent, density, local=None
):
    slabs, orbitals = inv_real.shape
    parts = orbitals // LANE
    if density is not None:
        density[0:1, :] += -weight * inv_imag[0:1, :]
    for s in range(1, slabs):
        coupled = coupled_of(s)
        if s == 1:
            wide = coupled.astype(F32)
            for half, inv in ((0, inv_real), (1, inv_imag)):
                piece = (wide * inv[0:1, :].astype(BF16).astype(F32)).astype(BF16)
                for c in range(parts):
                    store_left(left, piece[:, span(c)], half, c, parts)
        else:
            times_carried(coupled, g, left, parts)

        def times_turned(rows):
            return lax.dot_general(
                rows, coupled, (((1,), (1,)), ((), ())), preferred_element_type=F32
            )

        def note(r, middle):
            density[s : s + 1, span(r)] += -weight * middle

        final = s == slabs - 1
        finish_slab(
            s, times_turned, left, None if final else g, sent if final else None,
            inv_real[s : s + 1, :], inv_imag[s : s + 1, :], scales, None if density is None else note, parts,
            local if final else None,
        )


def copies_of_constants(constants_hbm, contact_hbm, constants, contact, sem):
    return [
        pltpu.make_async_copy(constants_hbm, constants, sem.at[0]),
        pltpu.make_async_copy(contact_hbm, contact, sem.at[1]),
    ]


def copies_of_couplings(base_hbm, wave_hbm, base, wave, sem, slabs_wanted):
    return {
        s: (
            pltpu.make_async_copy(base_hbm.at[s], base.at[s], sem.at[0, s]),
            pltpu.make_async_copy(wave_hbm.at[s], wave.at[s], sem.at[1, s]),
        )
        for s in slabs_wanted
    }


def lead_kernel(
    impulse_count,
    constants_hbm, contact_hbm, onsite_hbm, hopping_hbm, potential_hbm, base_hbm, wave_hbm,
    sent, density, base, wave,
    constants, contact, tables, scales, g, left, small_sem, table_sem, couple_sem,
):
    slabs, orbitals = onsite_hbm.shape
    parts = orbitals // LANE
    position = lax.axis_index("en")
    density[...] = jnp.zeros_like(density)

    @pl.when(position == 0)
    def _():
        small_copies = copies_of_constants(
            constants_hbm, contact_hbm, constants, contact, small_sem
        ) + [
            pltpu.make_async_copy(source, tables.at[k], table_sem.at[k])
            for k, source in enumerate((onsite_hbm, hopping_hbm, potential_hbm))
        ]
        couple_copies = copies_of_couplings(
            base_hbm, wave_hbm, base, wave, couple_sem, range(1, slabs)
        )
        for copy in small_copies:
            copy.start()
        for s in couple_copies:
            for copy in couple_copies[s]:
                copy.start()
        for copy in small_copies:
            copy.wait()

        @pl.when(takes_first_levels())
        def _():
            momentum, level = first_level_item(0)
            cosine, energy, weight = entry_amounts(
                constants, impulse_count, momentum, level
            )
            inv_real, inv_imag = inverse_diagonal(
                position, cosine, energy, contact, tables.at[0], tables.at[1], tables.at[2]
            )
            form_scales(range(1, slabs), inv_real, inv_imag, scales, parts)

            def coupled_of(s):
                for copy in couple_copies[s]:
                    copy.wait()
                return coupling_of(base[s], wave[s], cosine)

            first_segment(
                coupled_of, inv_real, inv_imag, scales, weight, g, left, sent, density
            )

        @pl.when(jnp.logical_not(takes_first_levels()))
        def _():
            for s in couple_copies:
                for copy in couple_copies[s]:
                    copy.wait()


    @pl.when(position > 0)
    def _():
        couple_copies = copies_of_couplings(
            base_hbm, wave_hbm, base, wave, couple_sem, range(slabs)
        )
        for s in couple_copies:
            for copy in couple_copies[s]:
                copy.start()
        for s in couple_copies:
            for copy in couple_copies[s]:
                copy.wait()


def with_scalars(refs, scratch, sem):
    copies = [
        pltpu.make_async_copy(source, target, sem.at[k])
        for k, (source, target) in enumerate(zip(refs, scratch))
    ]
    for copy in copies:
        copy.start()
    for copy in copies:
        copy.wait()


def begin_kernel(
    impulse_count, slot,
    constants_ref, contact_ref, counts_ref,
    onsite, hopping, potential, base, wave, so_far, held,
    density, sent,
    constants, contact, counts, scalar_sem, scales, g, left,
):
    del held
    slabs, orbitals = onsite.shape
    parts = orbitals // LANE
    position = lax.axis_index("en")
    density[...] = so_far[...]
    active = position == 0
    if slot == 0:
        active = jnp.logical_and(active, jnp.logical_not(takes_first_levels()))

    @pl.when(active)
    def _():
        with_scalars(
            (constants_ref, contact_ref, counts_ref), (constants, contact, counts), scalar_sem
        )
        momentum, level = item_of(counts, slot)
        cosine, energy, weight = entry_amounts(constants, impulse_count, momentum, level)
        inv_real, inv_imag = inverse_diagonal(
            position, cosine, energy, contact, onsite, hopping, potential
        )
        form_scales(range(1, slabs), inv_real, inv_imag, scales, parts)

        def coupled_of(s):
            return coupling_of(base[s], wave[s], cosine)

        first_segment(coupled_of, inv_real, inv_imag, scales, weight, g, left, sent, density)


def prepare(cosine, weight, inv_real, inv_imag, base, wave, couple, turned, scales, entry):
    slabs, orbitals = inv_real.shape
    parts = orbitals // LANE
    form_scales(range(slabs), inv_real, inv_imag, scales, parts)
    for s in range(slabs):
        entry[s] = jnp.broadcast_to(inv_real[s : s + 1, :], entry.shape[1:])
        entry[slabs + s] = jnp.broadcast_to(inv_imag[s : s + 1, :], entry.shape[1:])
    entry[2 * slabs] = jnp.full(entry.shape[1:], weight, F32)

    def one(s, carry):
        coupled = coupling_of(base[s], wave[s], cosine)
        couple[s] = coupled
        for r in range(parts):
            for c in range(parts):
                turned[s, span(c), span(r)] = coupled[span(r), span(c)].T
        return carry

    lax.fori_loop(0, slabs, one, 0)


def prepare_kernel(
    impulse_count,
    constants_ref, contact_ref, counts_ref, onsite, hopping, potential, base, wave,
    couple_0, turned_0, scales_0, entry_0,
    couple_1, turned_1, scales_1, entry_1,
    constants, contact, counts, scalar_sem,
):
    position = lax.axis_index("en")

    @pl.when(position > 0)
    def _():
        with_scalars(
            (constants_ref, contact_ref, counts_ref), (constants, contact, counts), scalar_sem
        )
        for slot, made in (
            (0, (couple_0, turned_0, scales_0, entry_0)),
            (1, (couple_1, turned_1, scales_1, entry_1)),
        ):
            momentum, level = item_of(counts, slot)
            cosine, energy, weight = entry_amounts(constants, impulse_count, momentum, level)
            inv_real, inv_imag = inverse_diagonal(
                position, cosine, energy, contact, onsite, hopping, potential
            )
            prepare(cosine, weight, inv_real, inv_imag, base, wave, *made)


def density_kernel(couple, turned, scales, entry, so_far, *refs):
    arrived, (density, g, left, noted) = refs[:-4], refs[-4:]
    slabs, orbitals = so_far.shape
    parts = orbitals // LANE
    position = lax.axis_index("en")
    density[...] = so_far[...]

    def put(half, r, c, block):
        column = place(parts, half, c)
        g[span(r), span(column)] = block

    for stage, block in enumerate(arrived, 1):

        @pl.when(position == stage)
        def _():
            unpack_blocks(block, put, parts)

    @pl.when(position > 0)
    def _():
        def slab(s, final):
            times_carried(couple[s], g, left, parts)

            def times_turned(rows):
                return jnp.dot(rows, turned[s], preferred_element_type=F32)

            def note(r, middle):
                noted[s, 0:1, span(r)] = middle

            finish_slab(
                s, times_turned, left, None if final else g, None,
                entry[s, 0:1, :], entry[slabs + s, 0:1, :], scales, note, parts,
            )

        def inner(s, carry):
            slab(s, False)
            return carry

        lax.fori_loop(0, slabs - 1, inner, 0)
        slab(slabs - 1, True)
        for s in range(slabs):
            density[s : s + 1, :] += -entry[2 * slabs, 0:1, :] * noted[s, 0:1, :]


def operator_kernel(couple, turned, scales, entry, local, carrier, cross, g, left):
    slabs, orbitals, _ = couple.shape
    parts = orbitals // LANE
    position = lax.axis_index("en")

    @pl.when(jnp.logical_and(position > 0, position < lax.axis_size("en") - 1))
    def _():
        inv_real = jnp.concatenate([entry[s, 0:1, :] for s in range(slabs)], axis=0)
        inv_imag = jnp.concatenate([entry[slabs + s, 0:1, :] for s in range(slabs)], axis=0)
        first_segment(
            lambda s: couple[s], inv_real, inv_imag, scales, None, g, left, None, None, local
        )
        down = jnp.concatenate([inv_real, inv_imag], axis=0).T
        for s in range(slabs):
            real_col = down[:, s : s + 1]
            imag_col = down[:, slabs + s : slabs + s + 1]
            if s == 0:
                wide = couple[0].astype(F32)
                real, imag = real_col * wide, imag_col * wide
            else:
                product = jnp.dot(couple[s], carrier[...], preferred_element_type=F32)
                from_real, from_imag = product[:, :orbitals], product[:, orbitals:]
                real = real_col * from_real - imag_col * from_imag
                imag = real_col * from_imag + imag_col * from_real
            carrier[:, :orbitals] = real.astype(BF16)
            carrier[:, orbitals:] = imag.astype(BF16)
        for r in range(parts):
            for c in range(parts):
                real = carrier[span(r), span(c)].T
                imag = carrier[span(r), span(parts + c)].T
                cross[span(c), span(r)] = real
                cross[span(parts + c), span(parts + r)] = real
                cross[span(c), span(parts + r)] = imag
                cross[span(parts + c), span(r)] = -imag


def pass_kernel(stage, local, carrier, cross, arrived, sent, wide, half_way):
    orbitals = carrier.shape[0]
    parts = orbitals // LANE

    @pl.when(lax.axis_index("en") == stage)
    def _():
        def put(half, r, c, block):
            if half == 0:
                wide[span(r), span(c)] = block
                wide[span(parts + r), span(parts + c)] = block
            else:
                wide[span(r), span(parts + c)] = block
                wide[span(parts + r), span(c)] = -block

        unpack_blocks(arrived, put, parts)
        half_way[...] = jnp.dot(carrier[...], wide[...], preferred_element_type=F32).astype(BF16)
        out = jnp.dot(half_way[...], cross[...], preferred_element_type=F32)
        middles = []
        for k, (r, c) in enumerate(blocks_on_or_below(parts)):
            green_real = local[span(2 * k), :] + out[span(r), span(c)]
            green_imag = local[span(2 * k + 1), :] + out[span(r), span(parts + c)]
            pack_block(sent, r, c, green_real, green_imag, parts)
            if r == c:
                middles.append(diagonal_row(green_imag))
        pack_middles(sent, middles, parts)


def vmem_call(kernel, outs, operands, in_specs, scratch, name, flops, **more):
    vmem = pl.BlockSpec(memory_space=pltpu.VMEM)
    return pl.pallas_call(
        kernel,
        out_shape=tuple(outs),
        in_specs=in_specs,
        out_specs=(vmem,) * len(outs),
        scratch_shapes=scratch,
        compiler_params=pltpu.CompilerParams(vmem_limit_bytes=16 * 2**20),
        cost_estimate=pl.CostEstimate(flops=flops, bytes_accessed=2**21, transcendentals=0),
        name=name,
        **more,
    )(*operands)


def split_kernel(inverse, high, middle, low):
    for r in range(inverse.shape[0] // LANE):
        for c in range(inverse.shape[1] // LANE):
            block = inverse[span(r), span(c)].T
            for part in (high, middle, low):
                rounded = block.astype(BF16)
                part[span(c), span(r)] = rounded
                block = block - rounded.astype(F32)


def last_kernel(gathered, doping, high, middle, low, summed, potential):
    total = jnp.sum(gathered[...], axis=0)
    summed[...] = total
    rest = total - doping[...]
    pieces = []
    for _ in range(3):
        pieces.append(rest.astype(BF16).astype(F32))
        rest = rest - pieces[-1]
    rows = total.shape[0]
    answer = jnp.zeros_like(total)
    for count, part in ((1, low), (2, middle), (3, high)):
        padded = -(-3 * rows // 16) * 16 - count * rows
        stacked = jnp.concatenate(
            pieces[:count] + [jnp.zeros((padded, total.shape[1]), F32)], axis=0
        ).astype(BF16)
        product = jnp.dot(stacked, part[...], preferred_element_type=F32)
        for k in reversed(range(count)):
            answer = answer + product[k * rows : (k + 1) * rows]
    potential[...] = answer


def gather_over(values, axis):
    copies = jnp.broadcast_to(values[None], (lax.axis_size(axis),) + values.shape)
    return lax.all_to_all(copies, axis, 0, 0)


def body(
    counts,
    contact_slabs,
    onsite,
    hopping,
    potential_in,
    couple_base,
    couple_wave,
    doping,
    poisson_inverse,
):
    kt_size = lax.axis_size("kt")
    en_size = lax.axis_size("en")
    slabs, orbitals = onsite.shape
    parts = orbitals // LANE
    impulse_count = counts.shape[0] * kt_size
    constants = jnp.asarray(item_constants(impulse_count))
    smem = pl.BlockSpec(memory_space=pltpu.SMEM)
    hbm = pl.BlockSpec(memory_space=pltpu.HBM)
    vmem = pl.BlockSpec(memory_space=pltpu.VMEM)
    flops = 2 * slabs * orbitals**3

    def forward(block, stage):
        return lax.ppermute(block, "en", [(stage, stage + 1)])

    block_shape = jax.ShapeDtypeStruct((packed_rows(orbitals), LANE), BF16)
    density_shape = jax.ShapeDtypeStruct((slabs, orbitals), F32)
    couple_shape = jax.ShapeDtypeStruct((slabs, orbitals, orbitals), BF16)
    scales_shape = jax.ShapeDtypeStruct((slabs, scale_rows(parts), LANE), F32)
    entry_shape = jax.ShapeDtypeStruct((2 * slabs + 1, 8, orbitals), F32)
    scales_scratch = pltpu.VMEM(scales_shape.shape, F32)
    work = [
        pltpu.VMEM((orbitals, 2 * orbitals), BF16),
        pltpu.VMEM((2 * orbitals, orbitals), BF16),
    ]

    counts_all = lax.all_to_all(jnp.tile(counts, kt_size), "kt", 0, 0, tiled=True)
    given = (constants, contact_slabs, onsite, hopping, potential_in, couple_base, couple_wave)
    pinned = [pltpu.with_memory_space_constraint(t, pltpu.HBM) for t in given]
    block, density, *loaded = vmem_call(
        functools.partial(lead_kernel, impulse_count),
        (block_shape, density_shape, couple_shape, couple_shape),
        pinned,
        [hbm] * len(pinned),
        [
            pltpu.SMEM(constants.shape, F32),
            pltpu.SMEM(contact_slabs.shape, jnp.int32),
            pltpu.VMEM((3, slabs, orbitals), F32),
            scales_scratch,
        ]
        + work
        + [
            pltpu.SemaphoreType.DMA((2,)),
            pltpu.SemaphoreType.DMA((3,)),
            pltpu.SemaphoreType.DMA((2, slabs)),
        ],
        "lead",
        3 * flops,
    )
    block, counts_all = lax.optimization_barrier((block, counts_all))
    small = (constants, contact_slabs, counts_all, onsite, hopping, potential_in)

    anywhere = pl.BlockSpec(memory_space=pl.ANY)
    scalar_scratch = [
        pltpu.SMEM(constants.shape, F32),
        pltpu.SMEM(contact_slabs.shape, jnp.int32),
        pltpu.SMEM(counts_all.shape, jnp.int32),
        pltpu.SemaphoreType.DMA((3,)),
    ]

    def begin(slot, density, held):
        return vmem_call(
            functools.partial(begin_kernel, impulse_count, slot),
            (density_shape, block_shape),
            (*small, *loaded, density, held),
            [anywhere] * 3 + [vmem] * 7,
            scalar_scratch + [scales_scratch] + work,
            f"begin_{slot}",
            3 * flops,
            input_output_aliases={8: 0, 9: 1},
        )

    density, block = begin(0, density, block)
    arrived = [forward(block, 0)]
    density, block = begin(1, density, jnp.zeros(block_shape.shape, BF16))
    arrived.append(forward(block, 0))
    small, _ = lax.optimization_barrier((small, block))
    made = vmem_call(
        functools.partial(prepare_kernel, impulse_count),
        (couple_shape, couple_shape, scales_shape, entry_shape) * 2,
        (*small, *loaded),
        [anywhere] * 3 + [vmem] * 5,
        scalar_scratch,
        "prepare",
        flops,
    )
    made = [made[:4], made[4:]]

    def operator_of(slot, made):
        return vmem_call(
            operator_kernel,
            (
                jax.ShapeDtypeStruct((scale_rows(parts), LANE), F32),
                jax.ShapeDtypeStruct((orbitals, 2 * orbitals), BF16),
                jax.ShapeDtypeStruct((2 * orbitals, 2 * orbitals), BF16),
            ),
            made,
            [vmem] * 4,
            work,
            f"operator_{slot}",
            6 * flops,
        )

    def pass_on(stage, slot, operator, block):
        return vmem_call(
            functools.partial(pass_kernel, stage),
            (block_shape,),
            (*operator, block),
            [vmem] * 4,
            [
                pltpu.VMEM((2 * orbitals, 2 * orbitals), BF16),
                pltpu.VMEM((orbitals, 2 * orbitals), BF16),
            ],
            f"pass_{stage}_{slot}",
            2 * flops,
        )[0]

    def densities(slot, density, came):
        return vmem_call(
            density_kernel,
            (density_shape,),
            (*made[slot], density, *came),
            [vmem] * (5 + len(came)),
            work + [pltpu.VMEM((slabs, 8, orbitals), F32)],
            f"density_{slot}",
            4 * flops,
            input_output_aliases={4: 0},
        )[0]

    operators = []
    came = [[arrived[0]], [arrived[1]]]
    for stage in range(1, en_size - 1):
        for slot in range(2):
            if stage == 1:
                if slot == 1:
                    made[1], _ = lax.optimization_barrier((made[1], block))
                operators.append(operator_of(slot, made[slot]))
            block = pass_on(stage, slot, operators[slot], came[slot][-1])
            came[slot].append(forward(block, stage))
    for slot in range(2):
        density = densities(slot, density, came[slot])
    part_shape = jax.ShapeDtypeStruct(poisson_inverse.shape, BF16)
    inverse, _ = lax.optimization_barrier((poisson_inverse, block))
    split = vmem_call(
        split_kernel, (part_shape,) * 3, (inverse,), [vmem], [], "split_inverse", 2 * flops
    )
    density, *split = lax.optimization_barrier((density, *split))
    return vmem_call(
        last_kernel,
        (density_shape, density_shape),
        (gather_over(density, "kt"), doping, *split),
        [vmem] * 5,
        [],
        "last",
        flops // slabs,
    )


def solution(mesh):
    return jax.shard_map(
        body,
        mesh=mesh,
        in_specs=(
            P("kt"),
            P(),
            P("en", None),
            P("en", None),
            P("en", None),
            P("en", None, None),
            P("en", None, None),
            P("en", None),
            P(),
        ),
        out_specs=(P("en", None), P("en", None)),
        check_vma=False,
    )
```

```python
import functools

import jax
import jax.numpy as jnp
import numpy as np
from jax import lax
from jax.experimental import pallas as pl
from jax.experimental.pallas import tpu as pltpu
from jax.sharding import PartitionSpec as P

EMAX = 4
LANE = 128
F32 = jnp.float32
BF16 = jnp.bfloat16

bottom_sample_mark = -1.0
sample_gap = 0.25
electrode_filling = -0.5
boltzmann_spread = 0.1
broadening = 1.0
contact_width = 0.5


def item_constants(impulse_count):
    wave = np.float32(np.pi) * (np.arange(impulse_count, dtype=np.float32) + np.float32(0.5))
    cosine = np.cos(wave / np.float32(impulse_count))
    energy = bottom_sample_mark + sample_gap * np.arange(EMAX)
    weight = sample_gap / (1.0 + np.exp((energy - electrode_filling) / boltzmann_spread)) / np.pi
    return np.concatenate([cosine, weight]).astype(np.float32)


def span(k):
    return slice(k * LANE, (k + 1) * LANE)


def place(parts, half, c):
    if c == parts - 1:
        return parts - 1 + half
    return c if half == 0 else parts + 1 + c


def blocks_on_or_below(parts):
    return [(r, c) for r in range(parts) for c in range(r + 1)]


def packed_rows(orbitals):
    parts = orbitals // LANE
    return parts * parts * LANE + 16


def pairs_below(parts):
    return [(r, c) for r in range(parts) for c in range(r)]


def pair_slot(parts, r, c, half):
    return 2 * pairs_below(parts).index((r, c)) + half


def middle_slot(parts, r):
    return parts * (parts - 1) + r


def tile_indices():
    rows = lax.broadcasted_iota(jnp.int32, (LANE, LANE), 0)
    cols = lax.broadcasted_iota(jnp.int32, (LANE, LANE), 1)
    return rows, cols


def unpack_blocks(packed, put, parts):
    rows, cols = tile_indices()
    for r, c in pairs_below(parts):
        for half in range(2):
            block = packed[span(pair_slot(parts, r, c, half)), :]
            put(half, r, c, block)
            put(half, c, r, block.T)
    at = parts * parts * LANE
    for r in range(parts):
        block = packed[span(middle_slot(parts, r)), :]
        turned = block.T
        middle = packed[at : at + 16, :][r : r + 1, :]
        put(0, r, r, jnp.where(rows <= cols, block, turned))
        put(1, r, r, jnp.where(rows > cols, block, jnp.where(rows == cols, middle, turned)))


def pack_block(packed, r, c, green_real, green_imag, parts):
    rows, cols = tile_indices()
    if r == c:
        packed[span(middle_slot(parts, r)), :] = jnp.where(
            rows <= cols, green_real, green_imag
        ).astype(BF16)
    else:
        packed[span(pair_slot(parts, r, c, 0)), :] = green_real.astype(BF16)
        packed[span(pair_slot(parts, r, c, 1)), :] = green_imag.astype(BF16)


def pack_middles(packed, middles, parts):
    rest = jnp.zeros((16 - parts, LANE), F32)
    at = parts * parts * LANE
    packed[at : at + 16, :] = jnp.concatenate(middles + [rest], axis=0).astype(BF16)


def diagonal_row(block):
    rows, cols = tile_indices()
    return jnp.sum(jnp.where(rows == cols, block, 0.0), axis=0, keepdims=True)


def takes_first_levels():
    return lax.axis_index("kt") % 2 == 1


def first_level_item(slot):
    return lax.axis_index("kt") - 1 + slot, jnp.int32(0)


def item_of(counts, slot):
    wanted = lax.axis_index("kt") + slot

    def one(k, state):
        momentum, before = state
        extra = counts[k] - 1
        take = jnp.logical_and(momentum == k, before + extra <= wanted)
        return (jnp.where(take, k + 1, momentum), jnp.where(take, before + extra, before))

    momentum, before = lax.fori_loop(0, counts.shape[0], one, (jnp.int32(0), jnp.int32(0)))
    momentum = jnp.minimum(momentum, counts.shape[0] - 1)
    level = jnp.clip(1 + wanted - before, 0, EMAX - 1)
    own_momentum, own_level = first_level_item(slot)
    own = takes_first_levels()
    return jnp.where(own, own_momentum, momentum), jnp.where(own, own_level, level)


def entry_amounts(constants, impulse_count, momentum, level):
    energy = bottom_sample_mark + sample_gap * level.astype(F32)
    return constants[momentum], energy, constants[impulse_count + level]


def inverse_diagonal(position, cosine, energy, contact, onsite, hopping, potential):
    slabs, orbitals = onsite.shape
    diag_real = energy + (-onsite[...] - potential[...]) - cosine * hopping[...]
    slab_in = lax.broadcasted_iota(jnp.int32, (slabs, orbitals), 0) + position * slabs
    at_contact = jnp.logical_or(slab_in == contact[0], slab_in == contact[1])
    diag_imag = broadening + contact_width * at_contact.astype(F32)
    magnitude = diag_real * diag_real + diag_imag * diag_imag
    inv_real = diag_real / magnitude
    inv_imag = -diag_imag / magnitude
    return inv_real, inv_imag


def scale_rows(parts):
    return 2 * len(blocks_on_or_below(parts)) * LANE


def form_scales(slabs_wanted, inv_real, inv_imag, scales, parts):
    slabs = inv_real.shape[0]
    down = jnp.concatenate([inv_real, inv_imag], axis=0).T
    for s in slabs_wanted:
        for k, (r, c) in enumerate(blocks_on_or_below(parts)):
            real_col = down[span(r), s : s + 1]
            imag_col = down[span(r), slabs + s : slabs + s + 1]
            rr = inv_real[s : s + 1, span(c)]
            ri = inv_imag[s : s + 1, span(c)]
            scales[s, span(2 * k), :] = real_col * rr - imag_col * ri
            scales[s, span(2 * k + 1), :] = real_col * ri + imag_col * rr


def store_left(left, piece, half, c, parts):
    last = (parts - 1) * LANE
    left[half * last : (half + 1) * last, span(c)] = piece[:last]
    bottom = 2 * last + half * LANE
    left[bottom : bottom + LANE, span(c)] = piece[last:]


def times_carried(coupled, g, left, parts):
    product = jnp.dot(coupled, g[...], preferred_element_type=F32).astype(BF16)
    for column in range(2 * parts):
        half, c = (
            (0, column)
            if column < parts
            else (1, parts - 1 if column == parts else column - parts - 1)
        )
        store_left(left, product[:, span(column)], half, c, parts)


def finish_slab(
    s, times_turned, left, g, packed, real_row, imag_row, scales, note, parts, local=None
):
    last = (parts - 1) * LANE
    rows, cols = tile_indices()
    diagonal = rows == cols
    numbers = {block: k for k, block in enumerate(blocks_on_or_below(parts))}
    middles = {}

    def finish(r, c, sr, si):
        k = numbers[r, c]
        scale_real = scales[s, span(2 * k), :]
        scale_imag = scales[s, span(2 * k + 1), :]
        green_real = scale_real * sr - scale_imag * si
        green_imag = scale_real * si + scale_imag * sr
        if r == c:
            green_real = green_real + jnp.where(diagonal, real_row[:, span(c)], 0.0)
            green_imag = green_imag + jnp.where(diagonal, imag_row[:, span(c)], 0.0)
            if note is not None:
                middles[r] = diagonal_row(green_imag)
                note(r, middles[r])
        if packed is not None:
            pack_block(packed, r, c, green_real, green_imag, parts)
        if local is not None:
            local[span(2 * k), :] = green_real
            local[span(2 * k + 1), :] = green_imag
        if g is None:
            return
        for half, green in ((0, green_real), (1, green_imag)):
            rounded = green.astype(BF16)
            g[span(r), span(place(parts, half, c))] = rounded
            if r != c:
                g[span(c), span(place(parts, half, r))] = rounded.T

    turned = times_turned(left[...])
    far = turned[2 * last :, :]
    near = turned[: 2 * last, :]
    for c in range(parts):
        finish(parts - 1, c, far[:LANE, span(c)], far[LANE:, span(c)])
    for r in range(parts - 1):
        for c in range(r + 1):
            finish(r, c, near[span(r), span(c)], near[last:, :][span(r), span(c)])
    if packed is not None:
        pack_middles(packed, [middles[r] for r in range(parts)], parts)


def coupling_of(base, wave, cosine):
    return (base.astype(F32) + cosine * wave.astype(F32)).astype(BF16)


def first_segment(
    coupled_of, inv_real, inv_imag, scales, weight, g, left, sent, density, local=None
):
    slabs, orbitals = inv_real.shape
    parts = orbitals // LANE
    if density is not None:
        density[0:1, :] += -weight * inv_imag[0:1, :]
    for s in range(1, slabs):
        coupled = coupled_of(s)
        if s == 1:
            wide = coupled.astype(F32)
            for half, inv in ((0, inv_real), (1, inv_imag)):
                piece = (wide * inv[0:1, :].astype(BF16).astype(F32)).astype(BF16)
                for c in range(parts):
                    store_left(left, piece[:, span(c)], half, c, parts)
        else:
            times_carried(coupled, g, left, parts)

        def times_turned(rows):
            return lax.dot_general(
                rows, coupled, (((1,), (1,)), ((), ())), preferred_element_type=F32
            )

        def note(r, middle):
            density[s : s + 1, span(r)] += -weight * middle

        final = s == slabs - 1
        finish_slab(
            s, times_turned, left, None if final else g, sent if final else None,
            inv_real[s : s + 1, :], inv_imag[s : s + 1, :], scales, None if density is None else note, parts,
            local if final else None,
        )


def copies_of_constants(constants_hbm, contact_hbm, constants, contact, sem):
    return [
        pltpu.make_async_copy(constants_hbm, constants, sem.at[0]),
        pltpu.make_async_copy(contact_hbm, contact, sem.at[1]),
    ]


def copies_of_couplings(base_hbm, wave_hbm, base, wave, sem, slabs_wanted):
    return {
        s: (
            pltpu.make_async_copy(base_hbm.at[s], base.at[s], sem.at[0, s]),
            pltpu.make_async_copy(wave_hbm.at[s], wave.at[s], sem.at[1, s]),
        )
        for s in slabs_wanted
    }


def lead_kernel(
    impulse_count,
    constants_hbm, contact_hbm, onsite_hbm, hopping_hbm, potential_hbm, base_hbm, wave_hbm,
    sent, density, base, wave,
    constants, contact, tables, scales, g, left, small_sem, table_sem, couple_sem,
):
    slabs, orbitals = onsite_hbm.shape
    parts = orbitals // LANE
    position = lax.axis_index("en")
    density[...] = jnp.zeros_like(density)

    @pl.when(position == 0)
    def _():
        small_copies = copies_of_constants(
            constants_hbm, contact_hbm, constants, contact, small_sem
        ) + [
            pltpu.make_async_copy(source, tables.at[k], table_sem.at[k])
            for k, source in enumerate((onsite_hbm, hopping_hbm, potential_hbm))
        ]
        couple_copies = copies_of_couplings(
            base_hbm, wave_hbm, base, wave, couple_sem, range(1, slabs)
        )
        for copy in small_copies:
            copy.start()
        for s in couple_copies:
            for copy in couple_copies[s]:
                copy.start()
        for copy in small_copies:
            copy.wait()

        @pl.when(takes_first_levels())
        def _():
            momentum, level = first_level_item(0)
            cosine, energy, weight = entry_amounts(
                constants, impulse_count, momentum, level
            )
            inv_real, inv_imag = inverse_diagonal(
                position, cosine, energy, contact, tables.at[0], tables.at[1], tables.at[2]
            )
            form_scales(range(1, slabs), inv_real, inv_imag, scales, parts)

            def coupled_of(s):
                for copy in couple_copies[s]:
                    copy.wait()
                return coupling_of(base[s], wave[s], cosine)

            first_segment(
                coupled_of, inv_real, inv_imag, scales, weight, g, left, sent, density
            )

        @pl.when(jnp.logical_not(takes_first_levels()))
        def _():
            for s in couple_copies:
                for copy in couple_copies[s]:
                    copy.wait()


    @pl.when(position > 0)
    def _():
        couple_copies = copies_of_couplings(
            base_hbm, wave_hbm, base, wave, couple_sem, range(slabs)
        )
        for s in couple_copies:
            for copy in couple_copies[s]:
                copy.start()
        for s in couple_copies:
            for copy in couple_copies[s]:
                copy.wait()


def with_scalars(refs, scratch, sem):
    copies = [
        pltpu.make_async_copy(source, target, sem.at[k])
        for k, (source, target) in enumerate(zip(refs, scratch))
    ]
    for copy in copies:
        copy.start()
    for copy in copies:
        copy.wait()


def begin_kernel(
    impulse_count, slot,
    constants_ref, contact_ref, counts_ref,
    onsite, hopping, potential, base, wave, so_far, held,
    density, sent,
    constants, contact, counts, scalar_sem, scales, g, left,
):
    del held
    slabs, orbitals = onsite.shape
    parts = orbitals // LANE
    position = lax.axis_index("en")
    density[...] = so_far[...]
    active = position == 0
    if slot == 0:
        active = jnp.logical_and(active, jnp.logical_not(takes_first_levels()))

    @pl.when(active)
    def _():
        with_scalars(
            (constants_ref, contact_ref, counts_ref), (constants, contact, counts), scalar_sem
        )
        momentum, level = item_of(counts, slot)
        cosine, energy, weight = entry_amounts(constants, impulse_count, momentum, level)
        inv_real, inv_imag = inverse_diagonal(
            position, cosine, energy, contact, onsite, hopping, potential
        )
        form_scales(range(1, slabs), inv_real, inv_imag, scales, parts)

        def coupled_of(s):
            return coupling_of(base[s], wave[s], cosine)

        first_segment(coupled_of, inv_real, inv_imag, scales, weight, g, left, sent, density)


def prepare(cosine, weight, inv_real, inv_imag, base, wave, couple, scales, entry):
    slabs, orbitals = inv_real.shape
    parts = orbitals // LANE
    form_scales(range(slabs), inv_real, inv_imag, scales, parts)
    for s in range(slabs):
        entry[s] = jnp.broadcast_to(inv_real[s : s + 1, :], entry.shape[1:])
        entry[slabs + s] = jnp.broadcast_to(inv_imag[s : s + 1, :], entry.shape[1:])
    entry[2 * slabs] = jnp.full(entry.shape[1:], weight, F32)

    def one(s, carry):
        couple[s] = coupling_of(base[s], wave[s], cosine)
        return carry

    lax.fori_loop(0, slabs, one, 0)


def prepare_kernel(
    impulse_count,
    constants_ref, contact_ref, counts_ref, onsite, hopping, potential, base, wave,
    couple_0, scales_0, entry_0,
    couple_1, scales_1, entry_1,
    constants, contact, counts, scalar_sem,
):
    position = lax.axis_index("en")

    @pl.when(position > 0)
    def _():
        with_scalars(
            (constants_ref, contact_ref, counts_ref), (constants, contact, counts), scalar_sem
        )
        for slot, made in (
            (0, (couple_0, scales_0, entry_0)),
            (1, (couple_1, scales_1, entry_1)),
        ):
            momentum, level = item_of(counts, slot)
            cosine, energy, weight = entry_amounts(constants, impulse_count, momentum, level)
            inv_real, inv_imag = inverse_diagonal(
                position, cosine, energy, contact, onsite, hopping, potential
            )
            prepare(cosine, weight, inv_real, inv_imag, base, wave, *made)


def rows_of_entry(entry, slabs):
    inv_real = jnp.concatenate([entry[s, 0:1, :] for s in range(slabs)], axis=0)
    inv_imag = jnp.concatenate([entry[slabs + s, 0:1, :] for s in range(slabs)], axis=0)
    return inv_real, inv_imag, entry[2 * slabs, 0:1, 0:1]


def carrier_kernel(couple, entry, carriers, cross):
    slabs, orbitals, _ = couple.shape
    parts = orbitals // LANE

    @pl.when(lax.axis_index("en") > 0)
    def _():
        inv_real, inv_imag, _ = rows_of_entry(entry, slabs)
        down = jnp.concatenate([inv_real, inv_imag], axis=0).T
        for s in range(slabs):
            here = slice(s * orbitals, (s + 1) * orbitals)
            real_col = down[:, s : s + 1]
            imag_col = down[:, slabs + s : slabs + s + 1]
            if s == 0:
                wide = couple[0].astype(F32)
                real, imag = real_col * wide, imag_col * wide
            else:
                ahead = slice((s - 1) * orbitals, s * orbitals)
                product = jnp.dot(couple[s], carriers[ahead, :], preferred_element_type=F32)
                from_real, from_imag = product[:, :orbitals], product[:, orbitals:]
                real = real_col * from_real - imag_col * from_imag
                imag = real_col * from_imag + imag_col * from_real
            carriers[here, :orbitals] = real.astype(BF16)
            carriers[here, orbitals:] = imag.astype(BF16)
        top = (slabs - 1) * parts
        for r in range(parts):
            for c in range(parts):
                real = carriers[span(top + r), span(c)].T
                imag = carriers[span(top + r), span(parts + c)].T
                cross[span(c), span(r)] = real
                cross[span(parts + c), span(parts + r)] = real
                cross[span(c), span(parts + r)] = imag
                cross[span(parts + c), span(r)] = -imag


def local_kernel(couple, scales, entry, local, densities, g, left):
    slabs = couple.shape[0]

    @pl.when(lax.axis_index("en") > 0)
    def _():
        inv_real, inv_imag, weight = rows_of_entry(entry, slabs)
        densities[...] = jnp.zeros_like(densities)
        first_segment(
            lambda s: couple[s], inv_real, inv_imag, scales, weight, g, left, None, densities, local
        )


def pass_kernel(stage, local, carriers, cross, arrived, sent, wide, half_way):
    orbitals = carriers.shape[1] // 2
    parts = orbitals // LANE

    @pl.when(lax.axis_index("en") == stage)
    def _():
        def put(half, r, c, block):
            if half == 0:
                wide[span(r), span(c)] = block
                wide[span(parts + r), span(parts + c)] = block
            else:
                wide[span(r), span(parts + c)] = block
                wide[span(parts + r), span(c)] = -block

        unpack_blocks(arrived, put, parts)
        half_way[...] = jnp.dot(
            carriers[carriers.shape[0] - orbitals :, :], wide[...], preferred_element_type=F32
        ).astype(BF16)
        out = jnp.dot(half_way[...], cross[...], preferred_element_type=F32)
        middles = []
        for k, (r, c) in enumerate(blocks_on_or_below(parts)):
            green_real = local[span(2 * k), :] + out[span(r), span(c)]
            green_imag = local[span(2 * k + 1), :] + out[span(r), span(parts + c)]
            pack_block(sent, r, c, green_real, green_imag, parts)
            if r == c:
                middles.append(diagonal_row(green_imag))
        pack_middles(sent, middles, parts)


def density_kernel(carriers, entry, local_densities, so_far, *refs):
    arrived, (density, wide, total) = refs[:-3], refs[-3:]
    slabs, orbitals = so_far.shape
    parts = orbitals // LANE
    position = lax.axis_index("en")
    density[...] = so_far[...]

    def put(half, r, c, block):
        if half == 0:
            wide[span(r), span(2 * c)] = block
            wide[span(parts + r), span(2 * c + 1)] = block
        else:
            wide[span(r), span(2 * c + 1)] = block
            wide[span(parts + r), span(2 * c)] = -block

    for stage, block in enumerate(arrived, 1):

        @pl.when(position == stage)
        def _():
            unpack_blocks(block, put, parts)

    @pl.when(position > 0)
    def _():
        for c in range(parts):
            product = jnp.dot(
                carriers[...],
                wide[:, 2 * c * LANE : 2 * (c + 1) * LANE],
                preferred_element_type=F32,
            )
            term = product[:, :LANE] * carriers[:, span(parts + c)].astype(F32) + product[
                :, LANE:
            ] * carriers[:, span(c)].astype(F32)
            if c == 0:
                total[...] = term
            else:
                total[...] += term
        weight = entry[2 * slabs, 0:1, :LANE]
        for s in range(slabs):
            for r in range(parts):
                row = jnp.sum(total[span(s * parts + r), :].T, axis=0, keepdims=True)
                density[s : s + 1, span(r)] += (
                    local_densities[s : s + 1, span(r)] - weight * row
                )


def vmem_call(kernel, outs, operands, in_specs, scratch, name, flops, traffic=2**21, **more):
    vmem = pl.BlockSpec(memory_space=pltpu.VMEM)
    return pl.pallas_call(
        kernel,
        out_shape=tuple(outs),
        in_specs=in_specs,
        out_specs=(vmem,) * len(outs),
        scratch_shapes=scratch,
        compiler_params=pltpu.CompilerParams(vmem_limit_bytes=16 * 2**20),
        cost_estimate=pl.CostEstimate(flops=flops, bytes_accessed=traffic, transcendentals=0),
        name=name,
        **more,
    )(*operands)


def split_kernel(inverse, high, middle, low):
    for r in range(inverse.shape[0] // LANE):
        for c in range(inverse.shape[1] // LANE):
            block = inverse[span(r), span(c)].T
            for part in (high, middle, low):
                rounded = block.astype(BF16)
                part[span(c), span(r)] = rounded
                block = block - rounded.astype(F32)


def last_kernel(gathered, doping, high, middle, low, summed, potential):
    total = jnp.sum(gathered[...], axis=0)
    summed[...] = total
    rest = total - doping[...]
    pieces = []
    for _ in range(3):
        pieces.append(rest.astype(BF16).astype(F32))
        rest = rest - pieces[-1]
    rows = total.shape[0]
    answer = jnp.zeros_like(total)
    for count, part in ((1, low), (2, middle), (3, high)):
        padded = -(-3 * rows // 16) * 16 - count * rows
        stacked = jnp.concatenate(
            pieces[:count] + [jnp.zeros((padded, total.shape[1]), F32)], axis=0
        ).astype(BF16)
        product = jnp.dot(stacked, part[...], preferred_element_type=F32)
        for k in reversed(range(count)):
            answer = answer + product[k * rows : (k + 1) * rows]
    potential[...] = answer


def gather_over(values, axis):
    copies = jnp.broadcast_to(values[None], (lax.axis_size(axis),) + values.shape)
    return lax.all_to_all(copies, axis, 0, 0)


def body(
    counts,
    contact_slabs,
    onsite,
    hopping,
    potential_in,
    couple_base,
    couple_wave,
    doping,
    poisson_inverse,
):
    kt_size = lax.axis_size("kt")
    en_size = lax.axis_size("en")
    slabs, orbitals = onsite.shape
    parts = orbitals // LANE
    impulse_count = counts.shape[0] * kt_size
    constants = jnp.asarray(item_constants(impulse_count))
    smem = pl.BlockSpec(memory_space=pltpu.SMEM)
    hbm = pl.BlockSpec(memory_space=pltpu.HBM)
    vmem = pl.BlockSpec(memory_space=pltpu.VMEM)
    flops = 2 * slabs * orbitals**3

    def forward(block, stage):
        return lax.ppermute(block, "en", [(stage, stage + 1)])

    block_shape = jax.ShapeDtypeStruct((packed_rows(orbitals), LANE), BF16)
    density_shape = jax.ShapeDtypeStruct((slabs, orbitals), F32)
    couple_shape = jax.ShapeDtypeStruct((slabs, orbitals, orbitals), BF16)
    scales_shape = jax.ShapeDtypeStruct((slabs, scale_rows(parts), LANE), F32)
    entry_shape = jax.ShapeDtypeStruct((2 * slabs + 1, 8, orbitals), F32)
    scales_scratch = pltpu.VMEM(scales_shape.shape, F32)
    work = [
        pltpu.VMEM((orbitals, 2 * orbitals), BF16),
        pltpu.VMEM((2 * orbitals, orbitals), BF16),
    ]

    counts_all = lax.all_to_all(jnp.tile(counts, kt_size), "kt", 0, 0, tiled=True)
    given = (constants, contact_slabs, onsite, hopping, potential_in, couple_base, couple_wave)
    pinned = [pltpu.with_memory_space_constraint(t, pltpu.HBM) for t in given]
    block, density, *loaded = vmem_call(
        functools.partial(lead_kernel, impulse_count),
        (block_shape, density_shape, couple_shape, couple_shape),
        pinned,
        [hbm] * len(pinned),
        [
            pltpu.SMEM(constants.shape, F32),
            pltpu.SMEM(contact_slabs.shape, jnp.int32),
            pltpu.VMEM((3, slabs, orbitals), F32),
            scales_scratch,
        ]
        + work
        + [
            pltpu.SemaphoreType.DMA((2,)),
            pltpu.SemaphoreType.DMA((3,)),
            pltpu.SemaphoreType.DMA((2, slabs)),
        ],
        "lead",
        3 * flops,
    )
    block, counts_all = lax.optimization_barrier((block, counts_all))
    small = (constants, contact_slabs, counts_all, onsite, hopping, potential_in)

    anywhere = pl.BlockSpec(memory_space=pl.ANY)
    scalar_scratch = [
        pltpu.SMEM(constants.shape, F32),
        pltpu.SMEM(contact_slabs.shape, jnp.int32),
        pltpu.SMEM(counts_all.shape, jnp.int32),
        pltpu.SemaphoreType.DMA((3,)),
    ]

    def begin(slot, density, held):
        return vmem_call(
            functools.partial(begin_kernel, impulse_count, slot),
            (density_shape, block_shape),
            (*small, *loaded, density, held),
            [anywhere] * 3 + [vmem] * 7,
            scalar_scratch + [scales_scratch] + work,
            f"begin_{slot}",
            3 * flops,
            input_output_aliases={8: 0, 9: 1},
        )

    density, block = begin(0, density, block)
    arrived = [forward(block, 0)]
    density, block = begin(1, density, jnp.zeros(block_shape.shape, BF16))
    arrived.append(forward(block, 0))
    small, _ = lax.optimization_barrier((small, block))
    made = vmem_call(
        functools.partial(prepare_kernel, impulse_count),
        (couple_shape, scales_shape, entry_shape) * 2,
        (*small, *loaded),
        [anywhere] * 3 + [vmem] * 5,
        scalar_scratch,
        "prepare",
        flops // 16,
        2**16,
    )
    made = [made[:3], made[3:]]

    carriers_shape = jax.ShapeDtypeStruct((slabs * orbitals, 2 * orbitals), BF16)
    double_shape = jax.ShapeDtypeStruct((2 * orbitals, 2 * orbitals), BF16)

    def carriers_of(slot):
        couple, _, entry = made[slot]
        return vmem_call(
            carrier_kernel,
            (carriers_shape, double_shape),
            (couple, entry),
            [vmem] * 2,
            [],
            f"carriers_{slot}",
            flops // 16,
            2**16,
        )

    def local_of(slot):
        return vmem_call(
            local_kernel,
            (jax.ShapeDtypeStruct((scale_rows(parts), LANE), F32), density_shape),
            made[slot],
            [vmem] * 3,
            work,
            f"local_{slot}",
            flops // 16,
            2**16,
        )

    def pass_on(stage, slot, block):
        return vmem_call(
            functools.partial(pass_kernel, stage),
            (block_shape,),
            (local[slot][0], *carried[slot], block),
            [vmem] * 4,
            [
                pltpu.VMEM(double_shape.shape, BF16),
                pltpu.VMEM((orbitals, 2 * orbitals), BF16),
            ],
            f"pass_{stage}_{slot}",
            2 * flops,
        )[0]

    def densities(slot, density, came):
        return vmem_call(
            density_kernel,
            (density_shape,),
            (carried[slot][0], made[slot][2], local[slot][1], density, *came),
            [vmem] * (4 + len(came)),
            [
                pltpu.VMEM(double_shape.shape, BF16),
                pltpu.VMEM((slabs * orbitals, LANE), F32),
            ],
            f"density_{slot}",
            4 * flops,
            input_output_aliases={3: 0},
        )[0]

    came = [[arrived[0]], [arrived[1]]]
    carried, local = [carriers_of(0)], [local_of(0)]
    made[1], _ = lax.optimization_barrier((made[1], local[0][1]))
    carried.append(carriers_of(1))
    came[0][0], _ = lax.optimization_barrier((came[0][0], carried[1]))
    for stage in range(1, en_size - 1):
        for slot in range(2):
            if stage == 1 and slot == 1:
                made[1], _ = lax.optimization_barrier((made[1], block))
                local.append(local_of(1))
            block = pass_on(stage, slot, came[slot][-1])
            came[slot].append(forward(block, stage))
    for slot in range(2):
        density = densities(slot, density, came[slot])
    part_shape = jax.ShapeDtypeStruct(poisson_inverse.shape, BF16)
    inverse, _ = lax.optimization_barrier((poisson_inverse, block))
    split = vmem_call(
        split_kernel, (part_shape,) * 3, (inverse,), [vmem], [], "split_inverse", 2 * flops
    )
    density, *split = lax.optimization_barrier((density, *split))
    return vmem_call(
        last_kernel,
        (density_shape, density_shape),
        (gather_over(density, "kt"), doping, *split),
        [vmem] * 5,
        [],
        "last",
        flops // slabs,
    )


def solution(mesh):
    return jax.shard_map(
        body,
        mesh=mesh,
        in_specs=(
            P("kt"),
            P(),
            P("en", None),
            P("en", None),
            P("en", None),
            P("en", None, None),
            P("en", None, None),
            P("en", None),
            P(),
        ),
        out_specs=(P("en", None), P("en", None)),
        check_vma=False,
    )
```

```python
import functools

import jax
import jax.numpy as jnp
import numpy as np
from jax import lax
from jax.experimental import pallas as pl
from jax.experimental.pallas import tpu as pltpu
from jax.sharding import PartitionSpec as P

EMAX = 4
LANE = 128
F32 = jnp.float32
BF16 = jnp.bfloat16

bottom_sample_mark = -1.0
sample_gap = 0.25
electrode_filling = -0.5
boltzmann_spread = 0.1
broadening = 1.0
contact_width = 0.5


def item_constants(impulse_count):
    wave = np.float32(np.pi) * (np.arange(impulse_count, dtype=np.float32) + np.float32(0.5))
    cosine = np.cos(wave / np.float32(impulse_count))
    energy = bottom_sample_mark + sample_gap * np.arange(EMAX)
    weight = sample_gap / (1.0 + np.exp((energy - electrode_filling) / boltzmann_spread)) / np.pi
    return np.concatenate([cosine, weight]).astype(np.float32)


def span(k):
    return slice(k * LANE, (k + 1) * LANE)


def place(parts, half, c):
    if c == parts - 1:
        return parts - 1 + half
    return c if half == 0 else parts + 1 + c


def blocks_on_or_below(parts):
    return [(r, c) for r in range(parts) for c in range(r + 1)]


def packed_rows(orbitals):
    parts = orbitals // LANE
    return parts * parts * LANE + 16


def pairs_below(parts):
    return [(r, c) for r in range(parts) for c in range(r)]


def pair_slot(parts, r, c, half):
    return 2 * pairs_below(parts).index((r, c)) + half


def middle_slot(parts, r):
    return parts * (parts - 1) + r


def tile_indices():
    rows = lax.broadcasted_iota(jnp.int32, (LANE, LANE), 0)
    cols = lax.broadcasted_iota(jnp.int32, (LANE, LANE), 1)
    return rows, cols


def unpack_blocks(packed, put, parts):
    rows, cols = tile_indices()
    for r, c in pairs_below(parts):
        for half in range(2):
            block = packed[span(pair_slot(parts, r, c, half)), :]
            put(half, r, c, block)
            put(half, c, r, block.T)
    at = parts * parts * LANE
    for r in range(parts):
        block = packed[span(middle_slot(parts, r)), :]
        turned = block.T
        middle = packed[at : at + 16, :][r : r + 1, :]
        put(0, r, r, jnp.where(rows <= cols, block, turned))
        put(1, r, r, jnp.where(rows > cols, block, jnp.where(rows == cols, middle, turned)))


def pack_block(packed, r, c, green_real, green_imag, parts):
    rows, cols = tile_indices()
    if r == c:
        packed[span(middle_slot(parts, r)), :] = jnp.where(
            rows <= cols, green_real, green_imag
        ).astype(BF16)
    else:
        packed[span(pair_slot(parts, r, c, 0)), :] = green_real.astype(BF16)
        packed[span(pair_slot(parts, r, c, 1)), :] = green_imag.astype(BF16)


def pack_middles(packed, middles, parts):
    rest = jnp.zeros((16 - parts, LANE), F32)
    at = parts * parts * LANE
    packed[at : at + 16, :] = jnp.concatenate(middles + [rest], axis=0).astype(BF16)


def diagonal_row(block):
    rows, cols = tile_indices()
    return jnp.sum(jnp.where(rows == cols, block, 0.0), axis=0, keepdims=True)


def takes_first_levels():
    return lax.axis_index("kt") % 2 == 1


def first_level_item(slot):
    return lax.axis_index("kt") - 1 + slot, jnp.int32(0)


def item_of(counts, slot):
    wanted = lax.axis_index("kt") + slot

    def one(k, state):
        momentum, before = state
        extra = counts[k] - 1
        take = jnp.logical_and(momentum == k, before + extra <= wanted)
        return (jnp.where(take, k + 1, momentum), jnp.where(take, before + extra, before))

    momentum, before = lax.fori_loop(0, counts.shape[0], one, (jnp.int32(0), jnp.int32(0)))
    momentum = jnp.minimum(momentum, counts.shape[0] - 1)
    level = jnp.clip(1 + wanted - before, 0, EMAX - 1)
    own_momentum, own_level = first_level_item(slot)
    own = takes_first_levels()
    return jnp.where(own, own_momentum, momentum), jnp.where(own, own_level, level)


def entry_amounts(constants, impulse_count, momentum, level):
    energy = bottom_sample_mark + sample_gap * level.astype(F32)
    return constants[momentum], energy, constants[impulse_count + level]


def inverse_diagonal(position, cosine, energy, contact, onsite, hopping, potential):
    slabs, orbitals = onsite.shape
    diag_real = energy + (-onsite[...] - potential[...]) - cosine * hopping[...]
    slab_in = lax.broadcasted_iota(jnp.int32, (slabs, orbitals), 0) + position * slabs
    at_contact = jnp.logical_or(slab_in == contact[0], slab_in == contact[1])
    diag_imag = broadening + contact_width * at_contact.astype(F32)
    magnitude = diag_real * diag_real + diag_imag * diag_imag
    inv_real = diag_real / magnitude
    inv_imag = -diag_imag / magnitude
    return inv_real, inv_imag


def scale_rows(parts):
    return 2 * len(blocks_on_or_below(parts)) * LANE


def form_scales(slabs_wanted, inv_real, inv_imag, scales, parts):
    slabs = inv_real.shape[0]
    down = jnp.concatenate([inv_real, inv_imag], axis=0).T
    for s in slabs_wanted:
        for k, (r, c) in enumerate(blocks_on_or_below(parts)):
            real_col = down[span(r), s : s + 1]
            imag_col = down[span(r), slabs + s : slabs + s + 1]
            rr = inv_real[s : s + 1, span(c)]
            ri = inv_imag[s : s + 1, span(c)]
            scales[s, span(2 * k), :] = real_col * rr - imag_col * ri
            scales[s, span(2 * k + 1), :] = real_col * ri + imag_col * rr


def store_left(left, piece, half, c, parts):
    last = (parts - 1) * LANE
    left[half * last : (half + 1) * last, span(c)] = piece[:last]
    bottom = 2 * last + half * LANE
    left[bottom : bottom + LANE, span(c)] = piece[last:]


def times_carried(coupled, g, left, parts):
    product = jnp.dot(coupled, g[...], preferred_element_type=F32).astype(BF16)
    for column in range(2 * parts):
        half, c = (
            (0, column)
            if column < parts
            else (1, parts - 1 if column == parts else column - parts - 1)
        )
        store_left(left, product[:, span(column)], half, c, parts)


def finish_slab(
    s, times_turned, left, g, packed, real_row, imag_row, scales, note, parts, local=None
):
    last = (parts - 1) * LANE
    rows, cols = tile_indices()
    diagonal = rows == cols
    numbers = {block: k for k, block in enumerate(blocks_on_or_below(parts))}
    middles = {}

    def finish(r, c, sr, si):
        k = numbers[r, c]
        scale_real = scales[s, span(2 * k), :]
        scale_imag = scales[s, span(2 * k + 1), :]
        green_real = scale_real * sr - scale_imag * si
        green_imag = scale_real * si + scale_imag * sr
        if r == c:
            green_real = green_real + jnp.where(diagonal, real_row[:, span(c)], 0.0)
            green_imag = green_imag + jnp.where(diagonal, imag_row[:, span(c)], 0.0)
            if note is not None:
                middles[r] = diagonal_row(green_imag)
                note(r, middles[r])
        if packed is not None:
            pack_block(packed, r, c, green_real, green_imag, parts)
        if local is not None:
            local[span(2 * k), :] = green_real
            local[span(2 * k + 1), :] = green_imag
        if g is None:
            return
        for half, green in ((0, green_real), (1, green_imag)):
            rounded = green.astype(BF16)
            g[span(r), span(place(parts, half, c))] = rounded
            if r != c:
                g[span(c), span(place(parts, half, r))] = rounded.T

    turned = times_turned(left[...])
    far = turned[2 * last :, :]
    near = turned[: 2 * last, :]
    for c in range(parts):
        finish(parts - 1, c, far[:LANE, span(c)], far[LANE:, span(c)])
    for r in range(parts - 1):
        for c in range(r + 1):
            finish(r, c, near[span(r), span(c)], near[last:, :][span(r), span(c)])
    if packed is not None:
        pack_middles(packed, [middles[r] for r in range(parts)], parts)


def coupling_of(base, wave, cosine):
    return (base.astype(F32) + cosine * wave.astype(F32)).astype(BF16)


def first_segment(
    coupled_of, inv_real, inv_imag, scales, weight, g, left, sent, density, local=None
):
    slabs, orbitals = inv_real.shape
    parts = orbitals // LANE
    if density is not None:
        density[0:1, :] += -weight * inv_imag[0:1, :]
    for s in range(1, slabs):
        coupled = coupled_of(s)
        if s == 1:
            wide = coupled.astype(F32)
            for half, inv in ((0, inv_real), (1, inv_imag)):
                piece = (wide * inv[0:1, :].astype(BF16).astype(F32)).astype(BF16)
                for c in range(parts):
                    store_left(left, piece[:, span(c)], half, c, parts)
        else:
            times_carried(coupled, g, left, parts)

        def times_turned(rows):
            return lax.dot_general(
                rows, coupled, (((1,), (1,)), ((), ())), preferred_element_type=F32
            )

        def note(r, middle):
            density[s : s + 1, span(r)] += -weight * middle

        final = s == slabs - 1
        finish_slab(
            s, times_turned, left, None if final else g, sent if final else None,
            inv_real[s : s + 1, :], inv_imag[s : s + 1, :], scales, None if density is None else note, parts,
            local if final else None,
        )


def copies_of_constants(constants_hbm, contact_hbm, constants, contact, sem):
    return [
        pltpu.make_async_copy(constants_hbm, constants, sem.at[0]),
        pltpu.make_async_copy(contact_hbm, contact, sem.at[1]),
    ]


def copies_of_couplings(base_hbm, wave_hbm, base, wave, sem, slabs_wanted):
    return {
        s: (
            pltpu.make_async_copy(base_hbm.at[s], base.at[s], sem.at[0, s]),
            pltpu.make_async_copy(wave_hbm.at[s], wave.at[s], sem.at[1, s]),
        )
        for s in slabs_wanted
    }


def lead_kernel(
    impulse_count,
    constants_hbm, contact_hbm, onsite_hbm, hopping_hbm, potential_hbm, base_hbm, wave_hbm,
    sent, density, base, wave,
    constants, contact, tables, scales, g, left, small_sem, table_sem, couple_sem,
):
    slabs, orbitals = onsite_hbm.shape
    parts = orbitals // LANE
    position = lax.axis_index("en")
    density[...] = jnp.zeros_like(density)

    @pl.when(position == 0)
    def _():
        small_copies = copies_of_constants(
            constants_hbm, contact_hbm, constants, contact, small_sem
        ) + [
            pltpu.make_async_copy(source, tables.at[k], table_sem.at[k])
            for k, source in enumerate((onsite_hbm, hopping_hbm, potential_hbm))
        ]
        couple_copies = copies_of_couplings(
            base_hbm, wave_hbm, base, wave, couple_sem, range(1, slabs)
        )
        for copy in small_copies:
            copy.start()
        for s in couple_copies:
            for copy in couple_copies[s]:
                copy.start()
        for copy in small_copies:
            copy.wait()

        @pl.when(takes_first_levels())
        def _():
            momentum, level = first_level_item(0)
            cosine, energy, weight = entry_amounts(
                constants, impulse_count, momentum, level
            )
            inv_real, inv_imag = inverse_diagonal(
                position, cosine, energy, contact, tables.at[0], tables.at[1], tables.at[2]
            )
            form_scales(range(1, slabs), inv_real, inv_imag, scales, parts)

            def coupled_of(s):
                for copy in couple_copies[s]:
                    copy.wait()
                return coupling_of(base[s], wave[s], cosine)

            first_segment(
                coupled_of, inv_real, inv_imag, scales, weight, g, left, sent, density
            )

        @pl.when(jnp.logical_not(takes_first_levels()))
        def _():
            for s in couple_copies:
                for copy in couple_copies[s]:
                    copy.wait()


    @pl.when(position > 0)
    def _():
        couple_copies = copies_of_couplings(
            base_hbm, wave_hbm, base, wave, couple_sem, range(slabs)
        )
        for s in couple_copies:
            for copy in couple_copies[s]:
                copy.start()
        for s in couple_copies:
            for copy in couple_copies[s]:
                copy.wait()


def with_scalars(refs, scratch, sem):
    copies = [
        pltpu.make_async_copy(source, target, sem.at[k])
        for k, (source, target) in enumerate(zip(refs, scratch))
    ]
    for copy in copies:
        copy.start()
    for copy in copies:
        copy.wait()


def begin_kernel(
    impulse_count, slot,
    constants_ref, contact_ref, counts_ref,
    onsite, hopping, potential, base, wave, so_far, *refs,
):
    held, refs = refs[:-9], refs[-9:]
    density, sent, constants, contact, counts, scalar_sem, scales, g, left = refs
    slabs, orbitals = onsite.shape
    parts = orbitals // LANE
    position = lax.axis_index("en")
    density[...] = so_far[...]
    active = position == 0
    if slot == 0:

        @pl.when(jnp.logical_and(active, takes_first_levels()))
        def _():
            sent[...] = held[0][...]

        active = jnp.logical_and(active, jnp.logical_not(takes_first_levels()))

    @pl.when(active)
    def _():
        with_scalars(
            (constants_ref, contact_ref, counts_ref), (constants, contact, counts), scalar_sem
        )
        momentum, level = item_of(counts, slot)
        cosine, energy, weight = entry_amounts(constants, impulse_count, momentum, level)
        inv_real, inv_imag = inverse_diagonal(
            position, cosine, energy, contact, onsite, hopping, potential
        )
        form_scales(range(1, slabs), inv_real, inv_imag, scales, parts)

        def coupled_of(s):
            return coupling_of(base[s], wave[s], cosine)

        first_segment(coupled_of, inv_real, inv_imag, scales, weight, g, left, sent, density)


def prepare(cosine, weight, inv_real, inv_imag, base, wave, couple, scales, entry):
    slabs, orbitals = inv_real.shape
    parts = orbitals // LANE
    form_scales(range(slabs), inv_real, inv_imag, scales, parts)
    for s in range(slabs):
        entry[s] = jnp.broadcast_to(inv_real[s : s + 1, :], entry.shape[1:])
        entry[slabs + s] = jnp.broadcast_to(inv_imag[s : s + 1, :], entry.shape[1:])
    entry[2 * slabs] = jnp.full(entry.shape[1:], weight, F32)

    def one(s, carry):
        couple[s] = coupling_of(base[s], wave[s], cosine)
        return carry

    lax.fori_loop(0, slabs, one, 0)


def prepare_kernel(
    impulse_count,
    constants_ref, contact_ref, counts_ref, onsite, hopping, potential, base, wave,
    couple_0, scales_0, entry_0,
    couple_1, scales_1, entry_1,
    constants, contact, counts, scalar_sem,
):
    position = lax.axis_index("en")

    @pl.when(position > 0)
    def _():
        with_scalars(
            (constants_ref, contact_ref, counts_ref), (constants, contact, counts), scalar_sem
        )
        for slot, made in (
            (0, (couple_0, scales_0, entry_0)),
            (1, (couple_1, scales_1, entry_1)),
        ):
            momentum, level = item_of(counts, slot)
            cosine, energy, weight = entry_amounts(constants, impulse_count, momentum, level)
            inv_real, inv_imag = inverse_diagonal(
                position, cosine, energy, contact, onsite, hopping, potential
            )
            prepare(cosine, weight, inv_real, inv_imag, base, wave, *made)


def rows_of_entry(entry, slabs):
    inv_real = jnp.concatenate([entry[s, 0:1, :] for s in range(slabs)], axis=0)
    inv_imag = jnp.concatenate([entry[slabs + s, 0:1, :] for s in range(slabs)], axis=0)
    return inv_real, inv_imag, entry[2 * slabs, 0:1, 0:1]


def carrier_kernel(couple, entry, carriers, cross):
    slabs, orbitals, _ = couple.shape
    parts = orbitals // LANE

    @pl.when(lax.axis_index("en") > 0)
    def _():
        inv_real, inv_imag, _ = rows_of_entry(entry, slabs)
        down = jnp.concatenate([inv_real, inv_imag], axis=0).T
        for s in range(slabs):
            here = slice(s * orbitals, (s + 1) * orbitals)
            real_col = down[:, s : s + 1]
            imag_col = down[:, slabs + s : slabs + s + 1]
            if s == 0:
                wide = couple[0].astype(F32)
                real, imag = real_col * wide, imag_col * wide
            else:
                ahead = slice((s - 1) * orbitals, s * orbitals)
                product = jnp.dot(couple[s], carriers[ahead, :], preferred_element_type=F32)
                from_real, from_imag = product[:, :orbitals], product[:, orbitals:]
                real = real_col * from_real - imag_col * from_imag
                imag = real_col * from_imag + imag_col * from_real
            carriers[here, :orbitals] = real.astype(BF16)
            carriers[here, orbitals:] = imag.astype(BF16)
        top = (slabs - 1) * parts
        for r in range(parts):
            for c in range(parts):
                real = carriers[span(top + r), span(c)].T
                imag = carriers[span(top + r), span(parts + c)].T
                cross[span(c), span(r)] = real
                cross[span(parts + c), span(parts + r)] = real
                cross[span(c), span(parts + r)] = imag
                cross[span(parts + c), span(r)] = -imag


def local_kernel(couple, scales, entry, local, densities, g, left):
    slabs = couple.shape[0]

    @pl.when(lax.axis_index("en") > 0)
    def _():
        inv_real, inv_imag, weight = rows_of_entry(entry, slabs)
        densities[...] = jnp.zeros_like(densities)
        first_segment(
            lambda s: couple[s], inv_real, inv_imag, scales, weight, g, left, None, densities, local
        )


def pass_kernel(stage, local, carriers, cross, arrived, sent, wide, half_way):
    orbitals = carriers.shape[1] // 2
    parts = orbitals // LANE

    @pl.when(lax.axis_index("en") == stage)
    def _():
        def put(half, r, c, block):
            if half == 0:
                wide[span(r), span(c)] = block
                wide[span(parts + r), span(parts + c)] = block
            else:
                wide[span(r), span(parts + c)] = block
                wide[span(parts + r), span(c)] = -block

        unpack_blocks(arrived, put, parts)
        half_way[...] = jnp.dot(
            carriers[carriers.shape[0] - orbitals :, :], wide[...], preferred_element_type=F32
        ).astype(BF16)
        out = jnp.dot(half_way[...], cross[...], preferred_element_type=F32)
        middles = []
        for k, (r, c) in enumerate(blocks_on_or_below(parts)):
            green_real = local[span(2 * k), :] + out[span(r), span(c)]
            green_imag = local[span(2 * k + 1), :] + out[span(r), span(parts + c)]
            pack_block(sent, r, c, green_real, green_imag, parts)
            if r == c:
                middles.append(diagonal_row(green_imag))
        pack_middles(sent, middles, parts)


def density_kernel(carriers, entry, local_densities, so_far, *refs):
    arrived, (density, wide, total) = refs[:-3], refs[-3:]
    slabs, orbitals = so_far.shape
    parts = orbitals // LANE
    position = lax.axis_index("en")
    density[...] = so_far[...]

    def put(half, r, c, block):
        if half == 0:
            wide[span(r), span(2 * c)] = block
            wide[span(parts + r), span(2 * c + 1)] = block
        else:
            wide[span(r), span(2 * c + 1)] = block
            wide[span(parts + r), span(2 * c)] = -block

    for stage, block in enumerate(arrived, 1):

        @pl.when(position == stage)
        def _():
            unpack_blocks(block, put, parts)

    @pl.when(position > 0)
    def _():
        for c in range(parts):
            product = jnp.dot(
                carriers[...],
                wide[:, 2 * c * LANE : 2 * (c + 1) * LANE],
                preferred_element_type=F32,
            )
            term = product[:, :LANE] * carriers[:, span(parts + c)].astype(F32) + product[
                :, LANE:
            ] * carriers[:, span(c)].astype(F32)
            if c == 0:
                total[...] = term
            else:
                total[...] += term
        weight = entry[2 * slabs, 0:1, :LANE]
        for s in range(slabs):
            for r in range(parts):
                row = jnp.sum(total[span(s * parts + r), :].T, axis=0, keepdims=True)
                density[s : s + 1, span(r)] += (
                    local_densities[s : s + 1, span(r)] - weight * row
                )


def vmem_call(kernel, outs, operands, in_specs, scratch, name, flops, traffic=2**21, **more):
    vmem = pl.BlockSpec(memory_space=pltpu.VMEM)
    return pl.pallas_call(
        kernel,
        out_shape=tuple(outs),
        in_specs=in_specs,
        out_specs=(vmem,) * len(outs),
        scratch_shapes=scratch,
        compiler_params=pltpu.CompilerParams(vmem_limit_bytes=16 * 2**20),
        cost_estimate=pl.CostEstimate(flops=flops, bytes_accessed=traffic, transcendentals=0),
        name=name,
        **more,
    )(*operands)


def split_kernel(inverse, high, middle, low):
    for r in range(inverse.shape[0] // LANE):
        for c in range(inverse.shape[1] // LANE):
            block = inverse[span(r), span(c)].T
            for part in (high, middle, low):
                rounded = block.astype(BF16)
                part[span(c), span(r)] = rounded
                block = block - rounded.astype(F32)


def last_kernel(gathered, doping, high, middle, low, summed, potential):
    total = jnp.sum(gathered[...], axis=0)
    summed[...] = total
    rest = total - doping[...]
    pieces = []
    for _ in range(3):
        pieces.append(rest.astype(BF16).astype(F32))
        rest = rest - pieces[-1]
    rows = total.shape[0]
    answer = jnp.zeros_like(total)
    for count, part in ((1, low), (2, middle), (3, high)):
        padded = -(-3 * rows // 16) * 16 - count * rows
        stacked = jnp.concatenate(
            pieces[:count] + [jnp.zeros((padded, total.shape[1]), F32)], axis=0
        ).astype(BF16)
        product = jnp.dot(stacked, part[...], preferred_element_type=F32)
        for k in reversed(range(count)):
            answer = answer + product[k * rows : (k + 1) * rows]
    potential[...] = answer


def gather_over(values, axis):
    copies = jnp.broadcast_to(values[None], (lax.axis_size(axis),) + values.shape)
    return lax.all_to_all(copies, axis, 0, 0)


def body(
    counts,
    contact_slabs,
    onsite,
    hopping,
    potential_in,
    couple_base,
    couple_wave,
    doping,
    poisson_inverse,
):
    kt_size = lax.axis_size("kt")
    en_size = lax.axis_size("en")
    slabs, orbitals = onsite.shape
    parts = orbitals // LANE
    impulse_count = counts.shape[0] * kt_size
    constants = jnp.asarray(item_constants(impulse_count))
    smem = pl.BlockSpec(memory_space=pltpu.SMEM)
    hbm = pl.BlockSpec(memory_space=pltpu.HBM)
    vmem = pl.BlockSpec(memory_space=pltpu.VMEM)
    flops = 2 * slabs * orbitals**3

    def forward(block, stage):
        return lax.ppermute(block, "en", [(stage, stage + 1)])

    block_shape = jax.ShapeDtypeStruct((packed_rows(orbitals), LANE), BF16)
    density_shape = jax.ShapeDtypeStruct((slabs, orbitals), F32)
    couple_shape = jax.ShapeDtypeStruct((slabs, orbitals, orbitals), BF16)
    scales_shape = jax.ShapeDtypeStruct((slabs, scale_rows(parts), LANE), F32)
    entry_shape = jax.ShapeDtypeStruct((2 * slabs + 1, 8, orbitals), F32)
    scales_scratch = pltpu.VMEM(scales_shape.shape, F32)
    work = [
        pltpu.VMEM((orbitals, 2 * orbitals), BF16),
        pltpu.VMEM((2 * orbitals, orbitals), BF16),
    ]

    counts_all = lax.all_to_all(jnp.tile(counts, kt_size), "kt", 0, 0, tiled=True)
    given = (constants, contact_slabs, onsite, hopping, potential_in, couple_base, couple_wave)
    pinned = [pltpu.with_memory_space_constraint(t, pltpu.HBM) for t in given]
    block, density, *loaded = vmem_call(
        functools.partial(lead_kernel, impulse_count),
        (block_shape, density_shape, couple_shape, couple_shape),
        pinned,
        [hbm] * len(pinned),
        [
            pltpu.SMEM(constants.shape, F32),
            pltpu.SMEM(contact_slabs.shape, jnp.int32),
            pltpu.VMEM((3, slabs, orbitals), F32),
            scales_scratch,
        ]
        + work
        + [
            pltpu.SemaphoreType.DMA((2,)),
            pltpu.SemaphoreType.DMA((3,)),
            pltpu.SemaphoreType.DMA((2, slabs)),
        ],
        "lead",
        3 * flops,
    )
    block, counts_all = lax.optimization_barrier((block, counts_all))
    small = (constants, contact_slabs, counts_all, onsite, hopping, potential_in)

    anywhere = pl.BlockSpec(memory_space=pl.ANY)
    scalar_scratch = [
        pltpu.SMEM(constants.shape, F32),
        pltpu.SMEM(contact_slabs.shape, jnp.int32),
        pltpu.SMEM(counts_all.shape, jnp.int32),
        pltpu.SemaphoreType.DMA((3,)),
    ]

    def begin(slot, density, *held):
        return vmem_call(
            functools.partial(begin_kernel, impulse_count, slot),
            (density_shape, block_shape),
            (*small, *loaded, density, *held),
            [anywhere] * 3 + [vmem] * (6 + len(held)),
            scalar_scratch + [scales_scratch] + work,
            f"begin_{slot}",
            3 * flops,
            input_output_aliases={8: 0, 9: 1} if held else {8: 0},
        )

    density, block = begin(0, density, block)
    arrived = [forward(block, 0)]
    density, block = begin(1, density)
    arrived.append(forward(block, 0))
    small, _ = lax.optimization_barrier((small, block))
    made = vmem_call(
        functools.partial(prepare_kernel, impulse_count),
        (couple_shape, scales_shape, entry_shape) * 2,
        (*small, *loaded),
        [anywhere] * 3 + [vmem] * 5,
        scalar_scratch,
        "prepare",
        flops // 16,
        2**16,
    )
    made = [made[:3], made[3:]]

    carriers_shape = jax.ShapeDtypeStruct((slabs * orbitals, 2 * orbitals), BF16)
    double_shape = jax.ShapeDtypeStruct((2 * orbitals, 2 * orbitals), BF16)

    def carriers_of(slot):
        couple, _, entry = made[slot]
        return vmem_call(
            carrier_kernel,
            (carriers_shape, double_shape),
            (couple, entry),
            [vmem] * 2,
            [],
            f"carriers_{slot}",
            flops // 16,
            2**16,
        )

    def local_of(slot):
        return vmem_call(
            local_kernel,
            (jax.ShapeDtypeStruct((scale_rows(parts), LANE), F32), density_shape),
            made[slot],
            [vmem] * 3,
            work,
            f"local_{slot}",
            flops // 16,
            2**16,
        )

    def pass_on(stage, slot, block):
        return vmem_call(
            functools.partial(pass_kernel, stage),
            (block_shape,),
            (local[slot][0], *carried[slot], block),
            [vmem] * 4,
            [
                pltpu.VMEM(double_shape.shape, BF16),
                pltpu.VMEM((orbitals, 2 * orbitals), BF16),
            ],
            f"pass_{stage}_{slot}",
            2 * flops,
        )[0]

    def densities(slot, density, came):
        return vmem_call(
            density_kernel,
            (density_shape,),
            (carried[slot][0], made[slot][2], local[slot][1], density, *came),
            [vmem] * (4 + len(came)),
            [
                pltpu.VMEM(double_shape.shape, BF16),
                pltpu.VMEM((slabs * orbitals, LANE), F32),
            ],
            f"density_{slot}",
            4 * flops,
            input_output_aliases={3: 0},
        )[0]

    came = [[arrived[0]], [arrived[1]]]
    carried, local = [carriers_of(0)], [local_of(0)]
    for stage in range(1, en_size - 1):
        for slot in range(2):
            if stage == 1 and slot == 1:
                made[1], _ = lax.optimization_barrier((made[1], block))
                carried.append(carriers_of(1))
                local.append(local_of(1))
            block = pass_on(stage, slot, came[slot][-1])
            came[slot].append(forward(block, stage))
    for slot in range(2):
        density = densities(slot, density, came[slot])
    part_shape = jax.ShapeDtypeStruct(poisson_inverse.shape, BF16)
    inverse, _ = lax.optimization_barrier((poisson_inverse, block))
    split = vmem_call(
        split_kernel, (part_shape,) * 3, (inverse,), [vmem], [], "split_inverse", 2 * flops
    )
    density, *split = lax.optimization_barrier((density, *split))
    return vmem_call(
        last_kernel,
        (density_shape, density_shape),
        (gather_over(density, "kt"), doping, *split),
        [vmem] * 5,
        [],
        "last",
        flops // slabs,
    )


def solution(mesh):
    return jax.shard_map(
        body,
        mesh=mesh,
        in_specs=(
            P("kt"),
            P(),
            P("en", None),
            P("en", None),
            P("en", None),
            P("en", None, None),
            P("en", None, None),
            P("en", None),
            P(),
        ),
        out_specs=(P("en", None), P("en", None)),
        check_vma=False,
    )
```

```python
import functools

import jax
import jax.numpy as jnp
import numpy as np
from jax import lax
from jax.experimental import pallas as pl
from jax.experimental.pallas import tpu as pltpu
from jax.sharding import PartitionSpec as P

EMAX = 4
LANE = 128
F32 = jnp.float32
BF16 = jnp.bfloat16

bottom_sample_mark = -1.0
sample_gap = 0.25
electrode_filling = -0.5
boltzmann_spread = 0.1
broadening = 1.0
contact_width = 0.5


def item_constants(impulse_count):
    wave = np.float32(np.pi) * (np.arange(impulse_count, dtype=np.float32) + np.float32(0.5))
    cosine = np.cos(wave / np.float32(impulse_count))
    energy = bottom_sample_mark + sample_gap * np.arange(EMAX)
    weight = sample_gap / (1.0 + np.exp((energy - electrode_filling) / boltzmann_spread)) / np.pi
    return np.concatenate([cosine, weight]).astype(np.float32)


def span(k):
    return slice(k * LANE, (k + 1) * LANE)


def place(parts, half, c):
    if c == parts - 1:
        return parts - 1 + half
    return c if half == 0 else parts + 1 + c


def blocks_on_or_below(parts):
    return [(r, c) for r in range(parts) for c in range(r + 1)]


def packed_rows(orbitals):
    parts = orbitals // LANE
    return parts * parts * LANE + 16


def pairs_below(parts):
    return [(r, c) for r in range(parts) for c in range(r)]


def pair_slot(parts, r, c, half):
    return 2 * pairs_below(parts).index((r, c)) + half


def middle_slot(parts, r):
    return parts * (parts - 1) + r


def tile_indices():
    rows = lax.broadcasted_iota(jnp.int32, (LANE, LANE), 0)
    cols = lax.broadcasted_iota(jnp.int32, (LANE, LANE), 1)
    return rows, cols


def unpack_blocks(packed, put, parts):
    rows, cols = tile_indices()
    for r, c in pairs_below(parts):
        for half in range(2):
            block = packed[span(pair_slot(parts, r, c, half)), :]
            put(half, r, c, block)
            put(half, c, r, block.T)
    at = parts * parts * LANE
    for r in range(parts):
        block = packed[span(middle_slot(parts, r)), :]
        turned = block.T
        middle = packed[at : at + 16, :][r : r + 1, :]
        put(0, r, r, jnp.where(rows <= cols, block, turned))
        put(1, r, r, jnp.where(rows > cols, block, jnp.where(rows == cols, middle, turned)))


def pack_block(packed, r, c, green_real, green_imag, parts):
    rows, cols = tile_indices()
    if r == c:
        packed[span(middle_slot(parts, r)), :] = jnp.where(
            rows <= cols, green_real, green_imag
        ).astype(BF16)
    else:
        packed[span(pair_slot(parts, r, c, 0)), :] = green_real.astype(BF16)
        packed[span(pair_slot(parts, r, c, 1)), :] = green_imag.astype(BF16)


def pack_middles(packed, middles, parts):
    rest = jnp.zeros((16 - parts, LANE), F32)
    at = parts * parts * LANE
    packed[at : at + 16, :] = jnp.concatenate(middles + [rest], axis=0).astype(BF16)


def diagonal_row(block):
    rows, cols = tile_indices()
    return jnp.sum(jnp.where(rows == cols, block, 0.0), axis=0, keepdims=True)


def takes_first_levels():
    return lax.axis_index("kt") % 2 == 1


class Either:
    def __init__(self, refs):
        self.refs = refs
        self.shape = refs[0].shape

    def __getitem__(self, index):
        if len(self.refs) == 1:
            return self.refs[0][index]
        return jnp.where(takes_first_levels(), self.refs[1][index], self.refs[0][index])


def first_level_item(slot):
    return lax.axis_index("kt") - 1 + slot, jnp.int32(0)


def item_of(counts, slot):
    wanted = lax.axis_index("kt") + slot

    def one(k, state):
        momentum, before = state
        extra = counts[k] - 1
        take = jnp.logical_and(momentum == k, before + extra <= wanted)
        return (jnp.where(take, k + 1, momentum), jnp.where(take, before + extra, before))

    momentum, before = lax.fori_loop(0, counts.shape[0], one, (jnp.int32(0), jnp.int32(0)))
    momentum = jnp.minimum(momentum, counts.shape[0] - 1)
    level = jnp.clip(1 + wanted - before, 0, EMAX - 1)
    own_momentum, own_level = first_level_item(slot)
    own = takes_first_levels()
    return jnp.where(own, own_momentum, momentum), jnp.where(own, own_level, level)


def entry_amounts(constants, impulse_count, momentum, level):
    energy = bottom_sample_mark + sample_gap * level.astype(F32)
    return constants[momentum], energy, constants[impulse_count + level]


def inverse_diagonal(position, cosine, energy, contact, onsite, hopping, potential):
    slabs, orbitals = onsite.shape
    diag_real = energy + (-onsite[...] - potential[...]) - cosine * hopping[...]
    slab_in = lax.broadcasted_iota(jnp.int32, (slabs, orbitals), 0) + position * slabs
    at_contact = jnp.logical_or(slab_in == contact[0], slab_in == contact[1])
    diag_imag = broadening + contact_width * at_contact.astype(F32)
    magnitude = diag_real * diag_real + diag_imag * diag_imag
    inv_real = diag_real / magnitude
    inv_imag = -diag_imag / magnitude
    return inv_real, inv_imag


def local_rows(parts):
    return 2 * len(blocks_on_or_below(parts)) * LANE


def columns_of(inv_real, inv_imag):
    return jnp.concatenate([inv_real, inv_imag], axis=0).T


def store_left(left, piece, half, c, parts):
    last = (parts - 1) * LANE
    left[half * last : (half + 1) * last, span(c)] = piece[:last]
    bottom = 2 * last + half * LANE
    left[bottom : bottom + LANE, span(c)] = piece[last:]


def times_carried(coupled, g, left, parts):
    product = jnp.dot(coupled, g[...], preferred_element_type=F32).astype(BF16)
    for column in range(2 * parts):
        half, c = (
            (0, column)
            if column < parts
            else (1, parts - 1 if column == parts else column - parts - 1)
        )
        store_left(left, product[:, span(column)], half, c, parts)


def finish_slab(
    s, times_turned, left, g, packed, columns, real_row, imag_row, note, parts, local=None
):
    last = (parts - 1) * LANE
    rows, cols = tile_indices()
    diagonal = rows == cols
    numbers = {block: k for k, block in enumerate(blocks_on_or_below(parts))}
    middles = {}

    def finish(r, c, sr, si):
        k = numbers[r, c]
        real_col, imag_col = columns[0][span(r)], columns[1][span(r)]
        half_real = real_col * sr - imag_col * si
        half_imag = real_col * si + imag_col * sr
        rr, ri = real_row[:, span(c)], imag_row[:, span(c)]
        green_real = half_real * rr - half_imag * ri
        green_imag = half_real * ri + half_imag * rr
        if r == c:
            green_real = green_real + jnp.where(diagonal, real_row[:, span(c)], 0.0)
            green_imag = green_imag + jnp.where(diagonal, imag_row[:, span(c)], 0.0)
            if note is not None:
                middles[r] = diagonal_row(green_imag)
                note(r, middles[r])
        if packed is not None:
            pack_block(packed, r, c, green_real, green_imag, parts)
        if local is not None:
            local[span(2 * k), :] = green_real
            local[span(2 * k + 1), :] = green_imag
        if g is None:
            return
        for half, green in ((0, green_real), (1, green_imag)):
            rounded = green.astype(BF16)
            g[span(r), span(place(parts, half, c))] = rounded
            if r != c:
                g[span(c), span(place(parts, half, r))] = rounded.T

    turned = times_turned(left[...])
    far = turned[2 * last :, :]
    near = turned[: 2 * last, :]
    for c in range(parts):
        finish(parts - 1, c, far[:LANE, span(c)], far[LANE:, span(c)])
    for r in range(parts - 1):
        for c in range(r + 1):
            finish(r, c, near[span(r), span(c)], near[last:, :][span(r), span(c)])
    if packed is not None:
        pack_middles(packed, [middles[r] for r in range(parts)], parts)


def coupling_of(base, wave, cosine):
    return (base.astype(F32) + cosine * wave.astype(F32)).astype(BF16)


def first_segment(
    coupled_of, inv_real, inv_imag, weight, g, left, sent, density, local=None
):
    slabs, orbitals = inv_real.shape
    parts = orbitals // LANE
    down = columns_of(inv_real, inv_imag)
    if density is not None:
        density[0:1, :] += -weight * inv_imag[0:1, :]
    for s in range(1, slabs):
        coupled = coupled_of(s)
        if s == 1:
            wide = coupled.astype(F32)
            for half, inv in ((0, inv_real), (1, inv_imag)):
                piece = (wide * inv[0:1, :].astype(BF16).astype(F32)).astype(BF16)
                for c in range(parts):
                    store_left(left, piece[:, span(c)], half, c, parts)
        else:
            times_carried(coupled, g, left, parts)

        def times_turned(rows):
            return lax.dot_general(
                rows, coupled, (((1,), (1,)), ((), ())), preferred_element_type=F32
            )

        def note(r, middle):
            density[s : s + 1, span(r)] += -weight * middle

        final = s == slabs - 1
        finish_slab(
            s, times_turned, left, None if final else g, sent if final else None,
            (down[:, s : s + 1], down[:, slabs + s : slabs + s + 1]),
            inv_real[s : s + 1, :], inv_imag[s : s + 1, :],
            None if density is None else note, parts, local if final else None,
        )


def copies_of_constants(constants_hbm, contact_hbm, constants, contact, sem):
    return [
        pltpu.make_async_copy(constants_hbm, constants, sem.at[0]),
        pltpu.make_async_copy(contact_hbm, contact, sem.at[1]),
    ]


def copies_of_couplings(base_hbm, wave_hbm, base, wave, sem, slabs_wanted):
    return {
        s: (
            pltpu.make_async_copy(base_hbm.at[s], base.at[s], sem.at[0, s]),
            pltpu.make_async_copy(wave_hbm.at[s], wave.at[s], sem.at[1, s]),
        )
        for s in slabs_wanted
    }


def lead_kernel(
    impulse_count,
    constants_hbm, contact_hbm, onsite_hbm, hopping_hbm, potential_hbm, base_hbm, wave_hbm,
    sent, density, base, wave, couple_0, entry_0,
    constants, contact, tables, g, left, small_sem, table_sem, couple_sem,
):
    slabs, orbitals = onsite_hbm.shape
    parts = orbitals // LANE
    position = lax.axis_index("en")
    density[...] = jnp.zeros_like(density)
    small_copies = copies_of_constants(
        constants_hbm, contact_hbm, constants, contact, small_sem
    ) + [
        pltpu.make_async_copy(source, tables.at[k], table_sem.at[k])
        for k, source in enumerate((onsite_hbm, hopping_hbm, potential_hbm))
    ]
    for copy in small_copies:
        copy.start()

    def first_level_amounts():
        momentum, level = first_level_item(0)
        cosine, energy, weight = entry_amounts(constants, impulse_count, momentum, level)
        inv_real, inv_imag = inverse_diagonal(
            position, cosine, energy, contact, tables.at[0], tables.at[1], tables.at[2]
        )
        return cosine, weight, inv_real, inv_imag

    @pl.when(position == 0)
    def _():
        couple_copies = copies_of_couplings(
            base_hbm, wave_hbm, base, wave, couple_sem, range(1, slabs)
        )
        for s in couple_copies:
            for copy in couple_copies[s]:
                copy.start()
        for copy in small_copies:
            copy.wait()

        @pl.when(takes_first_levels())
        def _():
            cosine, weight, inv_real, inv_imag = first_level_amounts()

            def coupled_of(s):
                for copy in couple_copies[s]:
                    copy.wait()
                return coupling_of(base[s], wave[s], cosine)

            first_segment(
                coupled_of, inv_real, inv_imag, weight, g, left, sent, density
            )

        @pl.when(jnp.logical_not(takes_first_levels()))
        def _():
            for s in couple_copies:
                for copy in couple_copies[s]:
                    copy.wait()


    @pl.when(position > 0)
    def _():
        couple_copies = copies_of_couplings(
            base_hbm, wave_hbm, base, wave, couple_sem, range(slabs)
        )
        for s in couple_copies:
            for copy in couple_copies[s]:
                copy.start()
        for copy in small_copies:
            copy.wait()
        for s in couple_copies:
            for copy in couple_copies[s]:
                copy.wait()

        @pl.when(takes_first_levels())
        def _():
            cosine, weight, inv_real, inv_imag = first_level_amounts()
            prepare(
                cosine, weight, inv_real, inv_imag, base, wave, couple_0, entry_0
            )


def with_scalars(refs, scratch, sem):
    copies = [
        pltpu.make_async_copy(source, target, sem.at[k])
        for k, (source, target) in enumerate(zip(refs, scratch))
    ]
    for copy in copies:
        copy.start()
    for copy in copies:
        copy.wait()


def begin_kernel(
    impulse_count, slot,
    constants_ref, contact_ref, counts_ref,
    onsite, hopping, potential, base, wave, so_far, *refs,
):
    held, refs = refs[:-8], refs[-8:]
    density, sent, constants, contact, counts, scalar_sem, g, left = refs
    slabs, orbitals = onsite.shape
    parts = orbitals // LANE
    position = lax.axis_index("en")
    density[...] = so_far[...]
    active = position == 0
    if slot == 0:

        @pl.when(jnp.logical_and(active, takes_first_levels()))
        def _():
            sent[...] = held[0][...]

        active = jnp.logical_and(active, jnp.logical_not(takes_first_levels()))

    @pl.when(active)
    def _():
        with_scalars(
            (constants_ref, contact_ref, counts_ref), (constants, contact, counts), scalar_sem
        )
        momentum, level = item_of(counts, slot)
        cosine, energy, weight = entry_amounts(constants, impulse_count, momentum, level)
        inv_real, inv_imag = inverse_diagonal(
            position, cosine, energy, contact, onsite, hopping, potential
        )

        def coupled_of(s):
            return coupling_of(base[s], wave[s], cosine)

        first_segment(coupled_of, inv_real, inv_imag, weight, g, left, sent, density)


def prepare(cosine, weight, inv_real, inv_imag, base, wave, couple, entry):
    slabs, orbitals = inv_real.shape
    parts = orbitals // LANE
    for s in range(slabs):
        entry[s] = jnp.broadcast_to(inv_real[s : s + 1, :], entry.shape[1:])
        entry[slabs + s] = jnp.broadcast_to(inv_imag[s : s + 1, :], entry.shape[1:])
    entry[2 * slabs] = jnp.full(entry.shape[1:], weight, F32)

    def one(s, carry):
        couple[s] = coupling_of(base[s], wave[s], cosine)
        return carry

    lax.fori_loop(0, slabs, one, 0)


def prepare_kernel(
    impulse_count,
    constants_ref, contact_ref, counts_ref, onsite, hopping, potential, base, wave,
    couple_0, entry_0,
    couple_1, entry_1,
    constants, contact, counts, scalar_sem,
):
    position = lax.axis_index("en")

    def prepare_slot(slot, made):
        momentum, level = item_of(counts, slot)
        cosine, energy, weight = entry_amounts(constants, impulse_count, momentum, level)
        inv_real, inv_imag = inverse_diagonal(
            position, cosine, energy, contact, onsite, hopping, potential
        )
        prepare(cosine, weight, inv_real, inv_imag, base, wave, *made)

    @pl.when(position > 0)
    def _():
        with_scalars(
            (constants_ref, contact_ref, counts_ref), (constants, contact, counts), scalar_sem
        )

        @pl.when(jnp.logical_not(takes_first_levels()))
        def _():
            prepare_slot(0, (couple_0, entry_0))

        prepare_slot(1, (couple_1, entry_1))


def rows_of_entry(entry, slabs):
    inv_real = jnp.concatenate([entry[s, 0:1, :] for s in range(slabs)], axis=0)
    inv_imag = jnp.concatenate([entry[slabs + s, 0:1, :] for s in range(slabs)], axis=0)
    return inv_real, inv_imag, entry[2 * slabs, 0:1, 0:1]


def carrier_kernel(calls, *refs):
    couple, entry = Either(refs[:calls]), Either(refs[calls : 2 * calls])
    carriers, cross = refs[2 * calls :]
    slabs, orbitals, _ = couple.shape
    parts = orbitals // LANE

    @pl.when(lax.axis_index("en") > 0)
    def _():
        inv_real, inv_imag, _ = rows_of_entry(entry, slabs)
        down = jnp.concatenate([inv_real, inv_imag], axis=0).T
        for s in range(slabs):
            here = slice(s * orbitals, (s + 1) * orbitals)
            real_col = down[:, s : s + 1]
            imag_col = down[:, slabs + s : slabs + s + 1]
            if s == 0:
                wide = couple[0].astype(F32)
                real, imag = real_col * wide, imag_col * wide
            else:
                ahead = slice((s - 1) * orbitals, s * orbitals)
                product = jnp.dot(couple[s], carriers[ahead, :], preferred_element_type=F32)
                from_real, from_imag = product[:, :orbitals], product[:, orbitals:]
                real = real_col * from_real - imag_col * from_imag
                imag = real_col * from_imag + imag_col * from_real
            carriers[here, :orbitals] = real.astype(BF16)
            carriers[here, orbitals:] = imag.astype(BF16)
        top = (slabs - 1) * parts
        for r in range(parts):
            for c in range(parts):
                real = carriers[span(top + r), span(c)].T
                imag = carriers[span(top + r), span(parts + c)].T
                cross[span(c), span(r)] = real
                cross[span(parts + c), span(parts + r)] = real
                cross[span(c), span(parts + r)] = imag
                cross[span(parts + c), span(r)] = -imag


def local_kernel(calls, odd_too, even_too, *refs):
    couple, entry = Either(refs[:calls]), Either(refs[calls : 2 * calls])
    local, densities, g, left = refs[2 * calls :]
    slabs = couple.shape[0]
    active = lax.axis_index("en") > 0
    if not odd_too:
        active = jnp.logical_and(active, jnp.logical_not(takes_first_levels()))
    if not even_too:
        active = jnp.logical_and(active, takes_first_levels())

    @pl.when(active)
    def _():
        inv_real, inv_imag, weight = rows_of_entry(entry, slabs)
        densities[...] = jnp.zeros_like(densities)
        first_segment(
            lambda s: couple[s], inv_real, inv_imag, weight, g, left, None, densities, local
        )


def pass_kernel(stage, calls, *refs):
    local = Either(refs[:calls])
    carriers, cross, arrived, sent, wide, half_way = refs[calls:]
    orbitals = carriers.shape[1] // 2
    parts = orbitals // LANE

    @pl.when(lax.axis_index("en") == stage)
    def _():
        def put(half, r, c, block):
            if half == 0:
                wide[span(r), span(c)] = block
                wide[span(parts + r), span(parts + c)] = block
            else:
                wide[span(r), span(parts + c)] = block
                wide[span(parts + r), span(c)] = -block

        unpack_blocks(arrived, put, parts)
        half_way[...] = jnp.dot(
            carriers[carriers.shape[0] - orbitals :, :], wide[...], preferred_element_type=F32
        ).astype(BF16)
        out = jnp.dot(half_way[...], cross[...], preferred_element_type=F32)
        middles = []
        for k, (r, c) in enumerate(blocks_on_or_below(parts)):
            green_real = local[span(2 * k), :] + out[span(r), span(c)]
            green_imag = local[span(2 * k + 1), :] + out[span(r), span(parts + c)]
            pack_block(sent, r, c, green_real, green_imag, parts)
            if r == c:
                middles.append(diagonal_row(green_imag))
        pack_middles(sent, middles, parts)


def density_kernel(calls, carriers, *refs):
    entry, refs = Either(refs[: calls[0]]), refs[calls[0] :]
    local_densities, refs = Either(refs[: calls[1]]), refs[calls[1] :]
    so_far, arrived, (density, wide, total) = refs[0], refs[1:-3], refs[-3:]
    slabs, orbitals = so_far.shape
    parts = orbitals // LANE
    position = lax.axis_index("en")
    density[...] = so_far[...]

    def put(half, r, c, block):
        if half == 0:
            wide[span(r), span(2 * c)] = block
            wide[span(parts + r), span(2 * c + 1)] = block
        else:
            wide[span(r), span(2 * c + 1)] = block
            wide[span(parts + r), span(2 * c)] = -block

    for stage, block in enumerate(arrived, 1):

        @pl.when(position == stage)
        def _():
            unpack_blocks(block, put, parts)

    @pl.when(position > 0)
    def _():
        for c in range(parts):
            product = jnp.dot(
                carriers[...],
                wide[:, 2 * c * LANE : 2 * (c + 1) * LANE],
                preferred_element_type=F32,
            )
            term = product[:, :LANE] * carriers[:, span(parts + c)].astype(F32) + product[
                :, LANE:
            ] * carriers[:, span(c)].astype(F32)
            if c == 0:
                total[...] = term
            else:
                total[...] += term
        weight = entry[2 * slabs, 0:1, :LANE]
        for s in range(slabs):
            for r in range(parts):
                row = jnp.sum(total[span(s * parts + r), :].T, axis=0, keepdims=True)
                density[s : s + 1, span(r)] += (
                    local_densities[s : s + 1, span(r)] - weight * row
                )


def vmem_call(kernel, outs, operands, in_specs, scratch, name, flops, traffic=2**21, **more):
    vmem = pl.BlockSpec(memory_space=pltpu.VMEM)
    return pl.pallas_call(
        kernel,
        out_shape=tuple(outs),
        in_specs=in_specs,
        out_specs=(vmem,) * len(outs),
        scratch_shapes=scratch,
        compiler_params=pltpu.CompilerParams(vmem_limit_bytes=16 * 2**20),
        cost_estimate=pl.CostEstimate(flops=flops, bytes_accessed=traffic, transcendentals=0),
        name=name,
        **more,
    )(*operands)


def split_kernel(inverse, high, middle, low):
    for r in range(inverse.shape[0] // LANE):
        for c in range(inverse.shape[1] // LANE):
            block = inverse[span(r), span(c)].T
            for part in (high, middle, low):
                rounded = block.astype(BF16)
                part[span(c), span(r)] = rounded
                block = block - rounded.astype(F32)


def last_kernel(gathered, doping, high, middle, low, summed, potential):
    total = jnp.sum(gathered[...], axis=0)
    summed[...] = total
    rest = total - doping[...]
    pieces = []
    for _ in range(3):
        pieces.append(rest.astype(BF16).astype(F32))
        rest = rest - pieces[-1]
    rows = total.shape[0]
    answer = jnp.zeros_like(total)
    for count, part in ((1, low), (2, middle), (3, high)):
        padded = -(-3 * rows // 16) * 16 - count * rows
        stacked = jnp.concatenate(
            pieces[:count] + [jnp.zeros((padded, total.shape[1]), F32)], axis=0
        ).astype(BF16)
        product = jnp.dot(stacked, part[...], preferred_element_type=F32)
        for k in reversed(range(count)):
            answer = answer + product[k * rows : (k + 1) * rows]
    potential[...] = answer


def gather_over(values, axis):
    copies = jnp.broadcast_to(values[None], (lax.axis_size(axis),) + values.shape)
    return lax.all_to_all(copies, axis, 0, 0)


def body(
    counts,
    contact_slabs,
    onsite,
    hopping,
    potential_in,
    couple_base,
    couple_wave,
    doping,
    poisson_inverse,
):
    kt_size = lax.axis_size("kt")
    en_size = lax.axis_size("en")
    slabs, orbitals = onsite.shape
    parts = orbitals // LANE
    impulse_count = counts.shape[0] * kt_size
    constants = jnp.asarray(item_constants(impulse_count))
    smem = pl.BlockSpec(memory_space=pltpu.SMEM)
    hbm = pl.BlockSpec(memory_space=pltpu.HBM)
    vmem = pl.BlockSpec(memory_space=pltpu.VMEM)
    flops = 2 * slabs * orbitals**3

    def forward(block, stage):
        return lax.ppermute(block, "en", [(stage, stage + 1)])

    block_shape = jax.ShapeDtypeStruct((packed_rows(orbitals), LANE), BF16)
    density_shape = jax.ShapeDtypeStruct((slabs, orbitals), F32)
    couple_shape = jax.ShapeDtypeStruct((slabs, orbitals, orbitals), BF16)
    entry_shape = jax.ShapeDtypeStruct((2 * slabs + 1, 8, orbitals), F32)
    work = [
        pltpu.VMEM((orbitals, 2 * orbitals), BF16),
        pltpu.VMEM((2 * orbitals, orbitals), BF16),
    ]

    counts_all = lax.all_to_all(jnp.tile(counts, kt_size), "kt", 0, 0, tiled=True)
    given = (constants, contact_slabs, onsite, hopping, potential_in, couple_base, couple_wave)
    pinned = [pltpu.with_memory_space_constraint(t, pltpu.HBM) for t in given]
    block, density, *rest = vmem_call(
        functools.partial(lead_kernel, impulse_count),
        (block_shape, density_shape) + (couple_shape,) * 3 + (entry_shape,),
        pinned,
        [hbm] * len(pinned),
        [
            pltpu.SMEM(constants.shape, F32),
            pltpu.SMEM(contact_slabs.shape, jnp.int32),
            pltpu.VMEM((3, slabs, orbitals), F32),
        ]
        + work
        + [
            pltpu.SemaphoreType.DMA((2,)),
            pltpu.SemaphoreType.DMA((3,)),
            pltpu.SemaphoreType.DMA((2, slabs)),
        ],
        "lead",
        3 * flops,
    )
    loaded, made_first = rest[:2], rest[2:]
    block, counts_all = lax.optimization_barrier((block, counts_all))
    small = (constants, contact_slabs, counts_all, onsite, hopping, potential_in)

    anywhere = pl.BlockSpec(memory_space=pl.ANY)
    scalar_scratch = [
        pltpu.SMEM(constants.shape, F32),
        pltpu.SMEM(contact_slabs.shape, jnp.int32),
        pltpu.SMEM(counts_all.shape, jnp.int32),
        pltpu.SemaphoreType.DMA((3,)),
    ]

    def begin(slot, density, *held):
        return vmem_call(
            functools.partial(begin_kernel, impulse_count, slot),
            (density_shape, block_shape),
            (*small, *loaded, density, *held),
            [anywhere] * 3 + [vmem] * (6 + len(held)),
            scalar_scratch + work,
            f"begin_{slot}",
            3 * flops,
            input_output_aliases={8: 0, 9: 1} if held else {8: 0},
        )

    density, block = begin(0, density, block)
    arrived = [forward(block, 0)]
    density, block = begin(1, density)
    arrived.append(forward(block, 0))
    small, _ = lax.optimization_barrier((small, block))
    made = vmem_call(
        functools.partial(prepare_kernel, impulse_count),
        (couple_shape, entry_shape) * 2,
        (*small, *loaded),
        [anywhere] * 3 + [vmem] * 5,
        scalar_scratch,
        "prepare",
        flops // 16,
        2**16,
    )
    made = [list(zip(made[:2], made_first)), [(one,) for one in made[2:]]]

    carriers_shape = jax.ShapeDtypeStruct((slabs * orbitals, 2 * orbitals), BF16)
    double_shape = jax.ShapeDtypeStruct((2 * orbitals, 2 * orbitals), BF16)

    def carriers_of(slot):
        couple, entry = made[slot]
        return vmem_call(
            functools.partial(carrier_kernel, len(couple)),
            (carriers_shape, double_shape),
            (*couple, *entry),
            [vmem] * (2 * len(couple)),
            [],
            f"carriers_{slot}",
            flops // 16,
            2**16,
        )

    def local_of(slot, odd_too=True, even_too=True):
        couple, entry = made[slot]
        return vmem_call(
            functools.partial(local_kernel, len(couple), odd_too, even_too),
            (jax.ShapeDtypeStruct((local_rows(parts), LANE), F32), density_shape),
            (*couple, *entry),
            [vmem] * (2 * len(couple)),
            work,
            f"local_{slot}{int(even_too)}{int(odd_too)}",
            flops // 16,
            2**16,
        )

    def pass_on(stage, slot, block):
        calls = [one[0] for one in local[slot]]
        return vmem_call(
            functools.partial(pass_kernel, stage, len(calls)),
            (block_shape,),
            (*calls, *carried[slot], block),
            [vmem] * (3 + len(calls)),
            [
                pltpu.VMEM(double_shape.shape, BF16),
                pltpu.VMEM((orbitals, 2 * orbitals), BF16),
            ],
            f"pass_{stage}_{slot}",
            2 * flops,
        )[0]

    def densities(slot, density, came):
        entry = made[slot][1]
        calls = [one[1] for one in local[slot]]
        before = 1 + len(entry) + len(calls)
        return vmem_call(
            functools.partial(density_kernel, (len(entry), len(calls))),
            (density_shape,),
            (carried[slot][0], *entry, *calls, density, *came),
            [vmem] * (before + 1 + len(came)),
            [
                pltpu.VMEM(double_shape.shape, BF16),
                pltpu.VMEM((slabs * orbitals, LANE), F32),
            ],
            f"density_{slot}",
            4 * flops,
            input_output_aliases={before: 0},
        )[0]

    came = [[arrived[0]], [arrived[1]]]
    carried, local = [carriers_of(0)], [[local_of(0)]]
    made[1], _ = lax.optimization_barrier((made[1], local[0][0][1]))
    local.append([local_of(1, odd_too=False)])
    came[0][0], local[1][0] = lax.optimization_barrier((came[0][0], local[1][0]))
    for stage in range(1, en_size - 1):
        for slot in range(2):
            if stage == 1 and slot == 1:
                made[1], _ = lax.optimization_barrier((made[1], block))
                carried.append(carriers_of(1))
                made[1], _ = lax.optimization_barrier((made[1], carried[1][1]))
                local[1].append(local_of(1, even_too=False))
            block = pass_on(stage, slot, came[slot][-1])
            came[slot].append(forward(block, stage))
    for slot in range(2):
        density = densities(slot, density, came[slot])
    part_shape = jax.ShapeDtypeStruct(poisson_inverse.shape, BF16)
    inverse, _ = lax.optimization_barrier((poisson_inverse, block))
    split = vmem_call(
        split_kernel, (part_shape,) * 3, (inverse,), [vmem], [], "split_inverse", 2 * flops
    )
    density, *split = lax.optimization_barrier((density, *split))
    return vmem_call(
        last_kernel,
        (density_shape, density_shape),
        (gather_over(density, "kt"), doping, *split),
        [vmem] * 5,
        [],
        "last",
        flops // slabs,
    )


def solution(mesh):
    return jax.shard_map(
        body,
        mesh=mesh,
        in_specs=(
            P("kt"),
            P(),
            P("en", None),
            P("en", None),
            P("en", None),
            P("en", None, None),
            P("en", None, None),
            P("en", None),
            P(),
        ),
        out_specs=(P("en", None), P("en", None)),
        check_vma=False,
    )
```

```python
import functools

import jax
import jax.numpy as jnp
import numpy as np
from jax import lax
from jax.experimental import pallas as pl
from jax.experimental.pallas import tpu as pltpu
from jax.sharding import PartitionSpec as P

EMAX = 4
LANE = 128
F32 = jnp.float32
BF16 = jnp.bfloat16

bottom_sample_mark = -1.0
sample_gap = 0.25
electrode_filling = -0.5
boltzmann_spread = 0.1
broadening = 1.0
contact_width = 0.5


def item_constants(impulse_count):
    wave = np.float32(np.pi) * (np.arange(impulse_count, dtype=np.float32) + np.float32(0.5))
    cosine = np.cos(wave / np.float32(impulse_count))
    energy = bottom_sample_mark + sample_gap * np.arange(EMAX)
    weight = sample_gap / (1.0 + np.exp((energy - electrode_filling) / boltzmann_spread)) / np.pi
    return np.concatenate([cosine, weight]).astype(np.float32)


def span(k):
    return slice(k * LANE, (k + 1) * LANE)


def place(parts, half, c):
    if c == parts - 1:
        return parts - 1 + half
    return c if half == 0 else parts + 1 + c


def blocks_on_or_below(parts):
    return [(r, c) for r in range(parts) for c in range(r + 1)]


def packed_rows(orbitals):
    parts = orbitals // LANE
    return parts * parts * LANE + 16


def pairs_below(parts):
    return [(r, c) for r in range(parts) for c in range(r)]


def pair_slot(parts, r, c, half):
    return 2 * pairs_below(parts).index((r, c)) + half


def middle_slot(parts, r):
    return parts * (parts - 1) + r


def tile_indices():
    rows = lax.broadcasted_iota(jnp.int32, (LANE, LANE), 0)
    cols = lax.broadcasted_iota(jnp.int32, (LANE, LANE), 1)
    return rows, cols


def unpack_blocks(packed, put, parts):
    rows, cols = tile_indices()
    for r, c in pairs_below(parts):
        for half in range(2):
            block = packed[span(pair_slot(parts, r, c, half)), :]
            put(half, r, c, block)
            put(half, c, r, block.T)
    at = parts * parts * LANE
    for r in range(parts):
        block = packed[span(middle_slot(parts, r)), :]
        turned = block.T
        middle = packed[at : at + 16, :][r : r + 1, :]
        put(0, r, r, jnp.where(rows <= cols, block, turned))
        put(1, r, r, jnp.where(rows > cols, block, jnp.where(rows == cols, middle, turned)))


def pack_block(packed, r, c, green_real, green_imag, parts):
    rows, cols = tile_indices()
    if r == c:
        packed[span(middle_slot(parts, r)), :] = jnp.where(
            rows <= cols, green_real, green_imag
        ).astype(BF16)
    else:
        packed[span(pair_slot(parts, r, c, 0)), :] = green_real.astype(BF16)
        packed[span(pair_slot(parts, r, c, 1)), :] = green_imag.astype(BF16)


def pack_middles(packed, middles, parts):
    rest = jnp.zeros((16 - parts, LANE), F32)
    at = parts * parts * LANE
    packed[at : at + 16, :] = jnp.concatenate(middles + [rest], axis=0).astype(BF16)


def diagonal_row(block):
    rows, cols = tile_indices()
    return jnp.sum(jnp.where(rows == cols, block, 0.0), axis=0, keepdims=True)


def takes_first_levels():
    return lax.axis_index("kt") % 2 == 1


class Either:
    def __init__(self, refs):
        self.refs = refs
        self.shape = refs[0].shape

    def __getitem__(self, index):
        if len(self.refs) == 1:
            return self.refs[0][index]
        return jnp.where(takes_first_levels(), self.refs[1][index], self.refs[0][index])


def first_level_item(slot):
    return lax.axis_index("kt") - 1 + slot, jnp.int32(0)


def item_of(counts, slot):
    wanted = lax.axis_index("kt") + slot

    def one(k, state):
        momentum, before = state
        extra = counts[k] - 1
        take = jnp.logical_and(momentum == k, before + extra <= wanted)
        return (jnp.where(take, k + 1, momentum), jnp.where(take, before + extra, before))

    momentum, before = lax.fori_loop(0, counts.shape[0], one, (jnp.int32(0), jnp.int32(0)))
    momentum = jnp.minimum(momentum, counts.shape[0] - 1)
    level = jnp.clip(1 + wanted - before, 0, EMAX - 1)
    own_momentum, own_level = first_level_item(slot)
    own = takes_first_levels()
    return jnp.where(own, own_momentum, momentum), jnp.where(own, own_level, level)


def entry_amounts(constants, impulse_count, momentum, level):
    energy = bottom_sample_mark + sample_gap * level.astype(F32)
    return constants[momentum], energy, constants[impulse_count + level]


def inverse_diagonal(position, cosine, energy, contact, onsite, hopping, potential):
    slabs, orbitals = onsite.shape
    diag_real = energy + (-onsite[...] - potential[...]) - cosine * hopping[...]
    slab_in = lax.broadcasted_iota(jnp.int32, (slabs, orbitals), 0) + position * slabs
    at_contact = jnp.logical_or(slab_in == contact[0], slab_in == contact[1])
    diag_imag = broadening + contact_width * at_contact.astype(F32)
    magnitude = diag_real * diag_real + diag_imag * diag_imag
    inv_real = diag_real / magnitude
    inv_imag = -diag_imag / magnitude
    return inv_real, inv_imag


def local_rows(parts):
    return 2 * len(blocks_on_or_below(parts)) * LANE


def columns_of(inv_real, inv_imag):
    return jnp.concatenate([inv_real, inv_imag], axis=0).T


def store_left(left, piece, half, c, parts):
    last = (parts - 1) * LANE
    left[half * last : (half + 1) * last, span(c)] = piece[:last]
    bottom = 2 * last + half * LANE
    left[bottom : bottom + LANE, span(c)] = piece[last:]


def times_carried(coupled, g, left, parts):
    product = jnp.dot(coupled, g[...], preferred_element_type=F32).astype(BF16)
    for column in range(2 * parts):
        half, c = (
            (0, column)
            if column < parts
            else (1, parts - 1 if column == parts else column - parts - 1)
        )
        store_left(left, product[:, span(column)], half, c, parts)


def finish_slab(
    s, times_turned, left, g, packed, columns, real_row, imag_row, note, parts, local=None
):
    last = (parts - 1) * LANE
    rows, cols = tile_indices()
    diagonal = rows == cols
    numbers = {block: k for k, block in enumerate(blocks_on_or_below(parts))}
    middles = {}

    def finish(r, c, sr, si):
        k = numbers[r, c]
        real_col, imag_col = columns[0][span(r)], columns[1][span(r)]
        half_real = real_col * sr - imag_col * si
        half_imag = real_col * si + imag_col * sr
        rr, ri = real_row[:, span(c)], imag_row[:, span(c)]
        green_real = half_real * rr - half_imag * ri
        green_imag = half_real * ri + half_imag * rr
        if r == c:
            green_real = green_real + jnp.where(diagonal, real_row[:, span(c)], 0.0)
            green_imag = green_imag + jnp.where(diagonal, imag_row[:, span(c)], 0.0)
            if note is not None:
                middles[r] = diagonal_row(green_imag)
                note(r, middles[r])
        if packed is not None:
            pack_block(packed, r, c, green_real, green_imag, parts)
        if local is not None:
            local[span(2 * k), :] = green_real
            local[span(2 * k + 1), :] = green_imag
        if g is None:
            return
        for half, green in ((0, green_real), (1, green_imag)):
            rounded = green.astype(BF16)
            g[span(r), span(place(parts, half, c))] = rounded
            if r != c:
                g[span(c), span(place(parts, half, r))] = rounded.T

    turned = times_turned(left[...])
    far = turned[2 * last :, :]
    near = turned[: 2 * last, :]
    for c in range(parts):
        finish(parts - 1, c, far[:LANE, span(c)], far[LANE:, span(c)])
    for r in range(parts - 1):
        for c in range(r + 1):
            finish(r, c, near[span(r), span(c)], near[last:, :][span(r), span(c)])
    if packed is not None:
        pack_middles(packed, [middles[r] for r in range(parts)], parts)


def coupling_of(base, wave, cosine):
    return (base.astype(F32) + cosine * wave.astype(F32)).astype(BF16)


def first_segment(
    coupled_of, inv_real, inv_imag, weight, g, left, sent, density, local=None
):
    slabs, orbitals = inv_real.shape
    parts = orbitals // LANE
    down = columns_of(inv_real, inv_imag)
    if density is not None:
        density[0:1, :] += -weight * inv_imag[0:1, :]
    for s in range(1, slabs):
        coupled = coupled_of(s)
        if s == 1:
            wide = coupled.astype(F32)
            for half, inv in ((0, inv_real), (1, inv_imag)):
                piece = (wide * inv[0:1, :].astype(BF16).astype(F32)).astype(BF16)
                for c in range(parts):
                    store_left(left, piece[:, span(c)], half, c, parts)
        else:
            times_carried(coupled, g, left, parts)

        def times_turned(rows):
            return lax.dot_general(
                rows, coupled, (((1,), (1,)), ((), ())), preferred_element_type=F32
            )

        def note(r, middle):
            density[s : s + 1, span(r)] += -weight * middle

        final = s == slabs - 1
        finish_slab(
            s, times_turned, left, None if final else g, sent if final else None,
            (down[:, s : s + 1], down[:, slabs + s : slabs + s + 1]),
            inv_real[s : s + 1, :], inv_imag[s : s + 1, :],
            None if density is None else note, parts, local if final else None,
        )


def copies_of_constants(constants_hbm, contact_hbm, constants, contact, sem):
    return [
        pltpu.make_async_copy(constants_hbm, constants, sem.at[0]),
        pltpu.make_async_copy(contact_hbm, contact, sem.at[1]),
    ]


def copies_of_couplings(base_hbm, wave_hbm, base, wave, sem, slabs_wanted):
    return {
        s: (
            pltpu.make_async_copy(base_hbm.at[s], base.at[s], sem.at[0, s]),
            pltpu.make_async_copy(wave_hbm.at[s], wave.at[s], sem.at[1, s]),
        )
        for s in slabs_wanted
    }


def lead_kernel(
    impulse_count,
    constants_hbm, contact_hbm, onsite_hbm, hopping_hbm, potential_hbm, base_hbm, wave_hbm,
    sent, density, base, wave,
    constants, contact, tables, g, left, small_sem, table_sem, couple_sem,
):
    slabs, orbitals = onsite_hbm.shape
    parts = orbitals // LANE
    position = lax.axis_index("en")
    density[...] = jnp.zeros_like(density)
    small_copies = copies_of_constants(
        constants_hbm, contact_hbm, constants, contact, small_sem
    ) + [
        pltpu.make_async_copy(source, tables.at[k], table_sem.at[k])
        for k, source in enumerate((onsite_hbm, hopping_hbm, potential_hbm))
    ]
    for copy in small_copies:
        copy.start()

    def first_level_amounts():
        momentum, level = first_level_item(0)
        cosine, energy, weight = entry_amounts(constants, impulse_count, momentum, level)
        inv_real, inv_imag = inverse_diagonal(
            position, cosine, energy, contact, tables.at[0], tables.at[1], tables.at[2]
        )
        return cosine, weight, inv_real, inv_imag

    @pl.when(position == 0)
    def _():
        couple_copies = copies_of_couplings(
            base_hbm, wave_hbm, base, wave, couple_sem, range(1, slabs)
        )
        for s in couple_copies:
            for copy in couple_copies[s]:
                copy.start()
        for copy in small_copies:
            copy.wait()

        @pl.when(takes_first_levels())
        def _():
            cosine, weight, inv_real, inv_imag = first_level_amounts()

            def coupled_of(s):
                for copy in couple_copies[s]:
                    copy.wait()
                return coupling_of(base[s], wave[s], cosine)

            first_segment(
                coupled_of, inv_real, inv_imag, weight, g, left, sent, density
            )

        @pl.when(jnp.logical_not(takes_first_levels()))
        def _():
            for s in couple_copies:
                for copy in couple_copies[s]:
                    copy.wait()


    @pl.when(position > 0)
    def _():
        couple_copies = copies_of_couplings(
            base_hbm, wave_hbm, base, wave, couple_sem, range(slabs)
        )
        for s in couple_copies:
            for copy in couple_copies[s]:
                copy.start()
        for copy in small_copies:
            copy.wait()
        for s in couple_copies:
            for copy in couple_copies[s]:
                copy.wait()


def with_scalars(refs, scratch, sem):
    copies = [
        pltpu.make_async_copy(source, target, sem.at[k])
        for k, (source, target) in enumerate(zip(refs, scratch))
    ]
    for copy in copies:
        copy.start()
    for copy in copies:
        copy.wait()


def begin_kernel(
    impulse_count, slot,
    constants_ref, contact_ref, counts_ref,
    onsite, hopping, potential, base, wave, so_far, *refs,
):
    held, refs = refs[:-8], refs[-8:]
    density, sent, constants, contact, counts, scalar_sem, g, left = refs
    slabs, orbitals = onsite.shape
    parts = orbitals // LANE
    position = lax.axis_index("en")
    density[...] = so_far[...]
    active = position == 0
    if slot == 0:

        @pl.when(jnp.logical_and(active, takes_first_levels()))
        def _():
            sent[...] = held[0][...]

        active = jnp.logical_and(active, jnp.logical_not(takes_first_levels()))

    @pl.when(active)
    def _():
        with_scalars(
            (constants_ref, contact_ref, counts_ref), (constants, contact, counts), scalar_sem
        )
        momentum, level = item_of(counts, slot)
        cosine, energy, weight = entry_amounts(constants, impulse_count, momentum, level)
        inv_real, inv_imag = inverse_diagonal(
            position, cosine, energy, contact, onsite, hopping, potential
        )

        def coupled_of(s):
            return coupling_of(base[s], wave[s], cosine)

        first_segment(coupled_of, inv_real, inv_imag, weight, g, left, sent, density)


def prepare(cosine, weight, inv_real, inv_imag, base, wave, couple, entry):
    slabs, orbitals = inv_real.shape
    parts = orbitals // LANE
    for s in range(slabs):
        entry[s] = jnp.broadcast_to(inv_real[s : s + 1, :], entry.shape[1:])
        entry[slabs + s] = jnp.broadcast_to(inv_imag[s : s + 1, :], entry.shape[1:])
    entry[2 * slabs] = jnp.full(entry.shape[1:], weight, F32)

    def one(s, carry):
        couple[s] = coupling_of(base[s], wave[s], cosine)
        return carry

    lax.fori_loop(0, slabs, one, 0)


def prepare_kernel(
    impulse_count,
    constants_ref, contact_ref, counts_ref, onsite, hopping, potential, base, wave,
    couple_0, entry_0,
    couple_1, entry_1,
    constants, contact, counts, scalar_sem,
):
    position = lax.axis_index("en")

    def prepare_slot(slot, made):
        momentum, level = item_of(counts, slot)
        cosine, energy, weight = entry_amounts(constants, impulse_count, momentum, level)
        inv_real, inv_imag = inverse_diagonal(
            position, cosine, energy, contact, onsite, hopping, potential
        )
        prepare(cosine, weight, inv_real, inv_imag, base, wave, *made)

    @pl.when(position > 0)
    def _():
        with_scalars(
            (constants_ref, contact_ref, counts_ref), (constants, contact, counts), scalar_sem
        )
        prepare_slot(0, (couple_0, entry_0))
        prepare_slot(1, (couple_1, entry_1))


def rows_of_entry(entry, slabs):
    inv_real = jnp.concatenate([entry[s, 0:1, :] for s in range(slabs)], axis=0)
    inv_imag = jnp.concatenate([entry[slabs + s, 0:1, :] for s in range(slabs)], axis=0)
    return inv_real, inv_imag, entry[2 * slabs, 0:1, 0:1]


def carrier_kernel(calls, *refs):
    couple, entry = Either(refs[:calls]), Either(refs[calls : 2 * calls])
    carriers, cross = refs[2 * calls :]
    slabs, orbitals, _ = couple.shape
    parts = orbitals // LANE

    @pl.when(lax.axis_index("en") > 0)
    def _():
        inv_real, inv_imag, _ = rows_of_entry(entry, slabs)
        down = jnp.concatenate([inv_real, inv_imag], axis=0).T
        for s in range(slabs):
            here = slice(s * orbitals, (s + 1) * orbitals)
            real_col = down[:, s : s + 1]
            imag_col = down[:, slabs + s : slabs + s + 1]
            if s == 0:
                wide = couple[0].astype(F32)
                real, imag = real_col * wide, imag_col * wide
            else:
                ahead = slice((s - 1) * orbitals, s * orbitals)
                product = jnp.dot(couple[s], carriers[ahead, :], preferred_element_type=F32)
                from_real, from_imag = product[:, :orbitals], product[:, orbitals:]
                real = real_col * from_real - imag_col * from_imag
                imag = real_col * from_imag + imag_col * from_real
            carriers[here, :orbitals] = real.astype(BF16)
            carriers[here, orbitals:] = imag.astype(BF16)
        top = (slabs - 1) * parts
        for r in range(parts):
            for c in range(parts):
                real = carriers[span(top + r), span(c)].T
                imag = carriers[span(top + r), span(parts + c)].T
                cross[span(c), span(r)] = real
                cross[span(parts + c), span(parts + r)] = real
                cross[span(c), span(parts + r)] = imag
                cross[span(parts + c), span(r)] = -imag


def local_kernel(calls, odd_too, even_too, *refs):
    couple, entry = Either(refs[:calls]), Either(refs[calls : 2 * calls])
    local, densities, g, left = refs[2 * calls :]
    slabs = couple.shape[0]
    active = lax.axis_index("en") > 0
    if not odd_too:
        active = jnp.logical_and(active, jnp.logical_not(takes_first_levels()))
    if not even_too:
        active = jnp.logical_and(active, takes_first_levels())

    @pl.when(active)
    def _():
        inv_real, inv_imag, weight = rows_of_entry(entry, slabs)
        densities[...] = jnp.zeros_like(densities)
        first_segment(
            lambda s: couple[s], inv_real, inv_imag, weight, g, left, None, densities, local
        )


def pass_kernel(stage, calls, *refs):
    local = Either(refs[:calls])
    carriers, cross, arrived, sent, wide, half_way = refs[calls:]
    orbitals = carriers.shape[1] // 2
    parts = orbitals // LANE

    @pl.when(lax.axis_index("en") == stage)
    def _():
        def put(half, r, c, block):
            if half == 0:
                wide[span(r), span(c)] = block
                wide[span(parts + r), span(parts + c)] = block
            else:
                wide[span(r), span(parts + c)] = block
                wide[span(parts + r), span(c)] = -block

        unpack_blocks(arrived, put, parts)
        half_way[...] = jnp.dot(
            carriers[carriers.shape[0] - orbitals :, :], wide[...], preferred_element_type=F32
        ).astype(BF16)
        out = jnp.dot(half_way[...], cross[...], preferred_element_type=F32)
        middles = []
        for k, (r, c) in enumerate(blocks_on_or_below(parts)):
            green_real = local[span(2 * k), :] + out[span(r), span(c)]
            green_imag = local[span(2 * k + 1), :] + out[span(r), span(parts + c)]
            pack_block(sent, r, c, green_real, green_imag, parts)
            if r == c:
                middles.append(diagonal_row(green_imag))
        pack_middles(sent, middles, parts)


def density_kernel(calls, carriers, *refs):
    entry, refs = Either(refs[: calls[0]]), refs[calls[0] :]
    local_densities, refs = Either(refs[: calls[1]]), refs[calls[1] :]
    so_far, arrived, (density, wide, total) = refs[0], refs[1:-3], refs[-3:]
    slabs, orbitals = so_far.shape
    parts = orbitals // LANE
    position = lax.axis_index("en")
    density[...] = so_far[...]

    def put(half, r, c, block):
        if half == 0:
            wide[span(r), span(2 * c)] = block
            wide[span(parts + r), span(2 * c + 1)] = block
        else:
            wide[span(r), span(2 * c + 1)] = block
            wide[span(parts + r), span(2 * c)] = -block

    for stage, block in enumerate(arrived, 1):

        @pl.when(position == stage)
        def _():
            unpack_blocks(block, put, parts)

    @pl.when(position > 0)
    def _():
        for c in range(parts):
            product = jnp.dot(
                carriers[...],
                wide[:, 2 * c * LANE : 2 * (c + 1) * LANE],
                preferred_element_type=F32,
            )
            term = product[:, :LANE] * carriers[:, span(parts + c)].astype(F32) + product[
                :, LANE:
            ] * carriers[:, span(c)].astype(F32)
            if c == 0:
                total[...] = term
            else:
                total[...] += term
        weight = entry[2 * slabs, 0:1, :LANE]
        for s in range(slabs):
            for r in range(parts):
                row = jnp.sum(total[span(s * parts + r), :].T, axis=0, keepdims=True)
                density[s : s + 1, span(r)] += (
                    local_densities[s : s + 1, span(r)] - weight * row
                )


def vmem_call(kernel, outs, operands, in_specs, scratch, name, flops, traffic=2**21, **more):
    vmem = pl.BlockSpec(memory_space=pltpu.VMEM)
    return pl.pallas_call(
        kernel,
        out_shape=tuple(outs),
        in_specs=in_specs,
        out_specs=(vmem,) * len(outs),
        scratch_shapes=scratch,
        compiler_params=pltpu.CompilerParams(vmem_limit_bytes=16 * 2**20),
        cost_estimate=pl.CostEstimate(flops=flops, bytes_accessed=traffic, transcendentals=0),
        name=name,
        **more,
    )(*operands)


def split_kernel(inverse, high, middle, low):
    for r in range(inverse.shape[0] // LANE):
        for c in range(inverse.shape[1] // LANE):
            block = inverse[span(r), span(c)].T
            for part in (high, middle, low):
                rounded = block.astype(BF16)
                part[span(c), span(r)] = rounded
                block = block - rounded.astype(F32)


def last_kernel(gathered, doping, high, middle, low, summed, potential):
    total = jnp.sum(gathered[...], axis=0)
    summed[...] = total
    rest = total - doping[...]
    pieces = []
    for _ in range(3):
        pieces.append(rest.astype(BF16).astype(F32))
        rest = rest - pieces[-1]
    rows = total.shape[0]
    answer = jnp.zeros_like(total)
    for count, part in ((1, low), (2, middle), (3, high)):
        padded = -(-3 * rows // 16) * 16 - count * rows
        stacked = jnp.concatenate(
            pieces[:count] + [jnp.zeros((padded, total.shape[1]), F32)], axis=0
        ).astype(BF16)
        product = jnp.dot(stacked, part[...], preferred_element_type=F32)
        for k in reversed(range(count)):
            answer = answer + product[k * rows : (k + 1) * rows]
    potential[...] = answer


def gather_over(values, axis):
    copies = jnp.broadcast_to(values[None], (lax.axis_size(axis),) + values.shape)
    return lax.all_to_all(copies, axis, 0, 0)


def body(
    counts,
    contact_slabs,
    onsite,
    hopping,
    potential_in,
    couple_base,
    couple_wave,
    doping,
    poisson_inverse,
):
    kt_size = lax.axis_size("kt")
    en_size = lax.axis_size("en")
    slabs, orbitals = onsite.shape
    parts = orbitals // LANE
    impulse_count = counts.shape[0] * kt_size
    constants = jnp.asarray(item_constants(impulse_count))
    smem = pl.BlockSpec(memory_space=pltpu.SMEM)
    hbm = pl.BlockSpec(memory_space=pltpu.HBM)
    vmem = pl.BlockSpec(memory_space=pltpu.VMEM)
    flops = 2 * slabs * orbitals**3

    def forward(block, stage):
        return lax.ppermute(block, "en", [(stage, stage + 1)])

    block_shape = jax.ShapeDtypeStruct((packed_rows(orbitals), LANE), BF16)
    density_shape = jax.ShapeDtypeStruct((slabs, orbitals), F32)
    couple_shape = jax.ShapeDtypeStruct((slabs, orbitals, orbitals), BF16)
    entry_shape = jax.ShapeDtypeStruct((2 * slabs + 1, 8, orbitals), F32)
    work = [
        pltpu.VMEM((orbitals, 2 * orbitals), BF16),
        pltpu.VMEM((2 * orbitals, orbitals), BF16),
    ]

    counts_all = lax.all_to_all(jnp.tile(counts, kt_size), "kt", 0, 0, tiled=True)
    given = (constants, contact_slabs, onsite, hopping, potential_in, couple_base, couple_wave)
    pinned = [pltpu.with_memory_space_constraint(t, pltpu.HBM) for t in given]
    block, density, *loaded = vmem_call(
        functools.partial(lead_kernel, impulse_count),
        (block_shape, density_shape, couple_shape, couple_shape),
        pinned,
        [hbm] * len(pinned),
        [
            pltpu.SMEM(constants.shape, F32),
            pltpu.SMEM(contact_slabs.shape, jnp.int32),
            pltpu.VMEM((3, slabs, orbitals), F32),
        ]
        + work
        + [
            pltpu.SemaphoreType.DMA((2,)),
            pltpu.SemaphoreType.DMA((3,)),
            pltpu.SemaphoreType.DMA((2, slabs)),
        ],
        "lead",
        3 * flops,
    )
    block, counts_all = lax.optimization_barrier((block, counts_all))
    small = (constants, contact_slabs, counts_all, onsite, hopping, potential_in)

    anywhere = pl.BlockSpec(memory_space=pl.ANY)
    scalar_scratch = [
        pltpu.SMEM(constants.shape, F32),
        pltpu.SMEM(contact_slabs.shape, jnp.int32),
        pltpu.SMEM(counts_all.shape, jnp.int32),
        pltpu.SemaphoreType.DMA((3,)),
    ]

    def begin(slot, density, *held):
        return vmem_call(
            functools.partial(begin_kernel, impulse_count, slot),
            (density_shape, block_shape),
            (*small, *loaded, density, *held),
            [anywhere] * 3 + [vmem] * (6 + len(held)),
            scalar_scratch + work,
            f"begin_{slot}",
            3 * flops,
            input_output_aliases={8: 0, 9: 1} if held else {8: 0},
        )

    density, block = begin(0, density, block)
    arrived = [forward(block, 0)]
    density, block = begin(1, density)
    arrived.append(forward(block, 0))
    small, _ = lax.optimization_barrier((small, block))
    made = vmem_call(
        functools.partial(prepare_kernel, impulse_count),
        (couple_shape, entry_shape) * 2,
        (*small, *loaded),
        [anywhere] * 3 + [vmem] * 5,
        scalar_scratch,
        "prepare",
        flops // 16,
        2**16,
    )
    made = [[(one,) for one in made[:2]], [(one,) for one in made[2:]]]

    carriers_shape = jax.ShapeDtypeStruct((slabs * orbitals, 2 * orbitals), BF16)
    double_shape = jax.ShapeDtypeStruct((2 * orbitals, 2 * orbitals), BF16)

    def carriers_of(slot):
        couple, entry = made[slot]
        return vmem_call(
            functools.partial(carrier_kernel, len(couple)),
            (carriers_shape, double_shape),
            (*couple, *entry),
            [vmem] * (2 * len(couple)),
            [],
            f"carriers_{slot}",
            flops // 16,
            2**16,
        )

    def local_of(slot, odd_too=True, even_too=True):
        couple, entry = made[slot]
        return vmem_call(
            functools.partial(local_kernel, len(couple), odd_too, even_too),
            (jax.ShapeDtypeStruct((local_rows(parts), LANE), F32), density_shape),
            (*couple, *entry),
            [vmem] * (2 * len(couple)),
            work,
            f"local_{slot}{int(even_too)}{int(odd_too)}",
            flops // 16,
            2**16,
        )

    def pass_on(stage, slot, block):
        calls = [one[0] for one in local[slot]]
        return vmem_call(
            functools.partial(pass_kernel, stage, len(calls)),
            (block_shape,),
            (*calls, *carried[slot], block),
            [vmem] * (3 + len(calls)),
            [
                pltpu.VMEM(double_shape.shape, BF16),
                pltpu.VMEM((orbitals, 2 * orbitals), BF16),
            ],
            f"pass_{stage}_{slot}",
            2 * flops,
        )[0]

    def densities(slot, density, came):
        entry = made[slot][1]
        calls = [one[1] for one in local[slot]]
        before = 1 + len(entry) + len(calls)
        return vmem_call(
            functools.partial(density_kernel, (len(entry), len(calls))),
            (density_shape,),
            (carried[slot][0], *entry, *calls, density, *came),
            [vmem] * (before + 1 + len(came)),
            [
                pltpu.VMEM(double_shape.shape, BF16),
                pltpu.VMEM((slabs * orbitals, LANE), F32),
            ],
            f"density_{slot}",
            4 * flops,
            input_output_aliases={before: 0},
        )[0]

    came = [[arrived[0]], [arrived[1]]]
    carried, local = [carriers_of(0)], [[local_of(0)]]
    made[1], _ = lax.optimization_barrier((made[1], local[0][0][1]))
    local.append([local_of(1, odd_too=False)])
    came[0][0], local[1][0] = lax.optimization_barrier((came[0][0], local[1][0]))
    for stage in range(1, en_size - 1):
        for slot in range(2):
            if stage == 1 and slot == 1:
                made[1], _ = lax.optimization_barrier((made[1], block))
                carried.append(carriers_of(1))
                made[1], _ = lax.optimization_barrier((made[1], carried[1][1]))
                local[1].append(local_of(1, even_too=False))
            block = pass_on(stage, slot, came[slot][-1])
            came[slot].append(forward(block, stage))
    for slot in range(2):
        density = densities(slot, density, came[slot])
    part_shape = jax.ShapeDtypeStruct(poisson_inverse.shape, BF16)
    inverse, _ = lax.optimization_barrier((poisson_inverse, block))
    split = vmem_call(
        split_kernel, (part_shape,) * 3, (inverse,), [vmem], [], "split_inverse", 2 * flops
    )
    density, *split = lax.optimization_barrier((density, *split))
    return vmem_call(
        last_kernel,
        (density_shape, density_shape),
        (gather_over(density, "kt"), doping, *split),
        [vmem] * 5,
        [],
        "last",
        flops // slabs,
    )


def solution(mesh):
    return jax.shard_map(
        body,
        mesh=mesh,
        in_specs=(
            P("kt"),
            P(),
            P("en", None),
            P("en", None),
            P("en", None),
            P("en", None, None),
            P("en", None, None),
            P("en", None),
            P(),
        ),
        out_specs=(P("en", None), P("en", None)),
        check_vma=False,
    )
```

```python
import functools

import jax
import jax.numpy as jnp
import numpy as np
from jax import lax
from jax.experimental import pallas as pl
from jax.experimental.pallas import tpu as pltpu
from jax.sharding import PartitionSpec as P

EMAX = 4
LANE = 128
F32 = jnp.float32
BF16 = jnp.bfloat16

bottom_sample_mark = -1.0
sample_gap = 0.25
electrode_filling = -0.5
boltzmann_spread = 0.1
broadening = 1.0
contact_width = 0.5


def item_constants(impulse_count):
    wave = np.float32(np.pi) * (np.arange(impulse_count, dtype=np.float32) + np.float32(0.5))
    cosine = np.cos(wave / np.float32(impulse_count))
    energy = bottom_sample_mark + sample_gap * np.arange(EMAX)
    weight = sample_gap / (1.0 + np.exp((energy - electrode_filling) / boltzmann_spread)) / np.pi
    return np.concatenate([cosine, weight]).astype(np.float32)


def span(k):
    return slice(k * LANE, (k + 1) * LANE)


def place(parts, half, c):
    if c == parts - 1:
        return parts - 1 + half
    return c if half == 0 else parts + 1 + c


def blocks_on_or_below(parts):
    return [(r, c) for r in range(parts) for c in range(r + 1)]


def packed_rows(orbitals):
    parts = orbitals // LANE
    return parts * parts * LANE + 16


def pairs_below(parts):
    return [(r, c) for r in range(parts) for c in range(r)]


def pair_slot(parts, r, c, half):
    return 2 * pairs_below(parts).index((r, c)) + half


def middle_slot(parts, r):
    return parts * (parts - 1) + r


def tile_indices():
    rows = lax.broadcasted_iota(jnp.int32, (LANE, LANE), 0)
    cols = lax.broadcasted_iota(jnp.int32, (LANE, LANE), 1)
    return rows, cols


def unpack_blocks(packed, put, parts):
    rows, cols = tile_indices()
    for r, c in pairs_below(parts):
        for half in range(2):
            block = packed[span(pair_slot(parts, r, c, half)), :]
            put(half, r, c, block)
            put(half, c, r, block.T)
    at = parts * parts * LANE
    for r in range(parts):
        block = packed[span(middle_slot(parts, r)), :]
        turned = block.T
        middle = packed[at : at + 16, :][r : r + 1, :]
        put(0, r, r, jnp.where(rows <= cols, block, turned))
        put(1, r, r, jnp.where(rows > cols, block, jnp.where(rows == cols, middle, turned)))


def pack_block(packed, r, c, green_real, green_imag, parts):
    rows, cols = tile_indices()
    if r == c:
        packed[span(middle_slot(parts, r)), :] = jnp.where(
            rows <= cols, green_real, green_imag
        ).astype(BF16)
    else:
        packed[span(pair_slot(parts, r, c, 0)), :] = green_real.astype(BF16)
        packed[span(pair_slot(parts, r, c, 1)), :] = green_imag.astype(BF16)


def pack_middles(packed, middles, parts):
    rest = jnp.zeros((16 - parts, LANE), F32)
    at = parts * parts * LANE
    packed[at : at + 16, :] = jnp.concatenate(middles + [rest], axis=0).astype(BF16)


def diagonal_row(block):
    rows, cols = tile_indices()
    return jnp.sum(jnp.where(rows == cols, block, 0.0), axis=0, keepdims=True)


def takes_first_levels():
    return lax.axis_index("kt") % 2 == 1


class Either:
    def __init__(self, refs):
        self.refs = refs
        self.shape = refs[0].shape

    def __getitem__(self, index):
        if len(self.refs) == 1:
            return self.refs[0][index]
        return jnp.where(takes_first_levels(), self.refs[1][index], self.refs[0][index])


def first_level_item(slot):
    return lax.axis_index("kt") - 1 + slot, jnp.int32(0)


def item_of(counts, slot):
    wanted = lax.axis_index("kt") + slot

    def one(k, state):
        momentum, before = state
        extra = counts[k] - 1
        take = jnp.logical_and(momentum == k, before + extra <= wanted)
        return (jnp.where(take, k + 1, momentum), jnp.where(take, before + extra, before))

    momentum, before = lax.fori_loop(0, counts.shape[0], one, (jnp.int32(0), jnp.int32(0)))
    momentum = jnp.minimum(momentum, counts.shape[0] - 1)
    level = jnp.clip(1 + wanted - before, 0, EMAX - 1)
    own_momentum, own_level = first_level_item(slot)
    own = takes_first_levels()
    return jnp.where(own, own_momentum, momentum), jnp.where(own, own_level, level)


def entry_amounts(constants, impulse_count, momentum, level):
    energy = bottom_sample_mark + sample_gap * level.astype(F32)
    return constants[momentum], energy, constants[impulse_count + level]


def inverse_diagonal(position, cosine, energy, contact, onsite, hopping, potential):
    slabs, orbitals = onsite.shape
    diag_real = energy + (-onsite[...] - potential[...]) - cosine * hopping[...]
    slab_in = lax.broadcasted_iota(jnp.int32, (slabs, orbitals), 0) + position * slabs
    at_contact = jnp.logical_or(slab_in == contact[0], slab_in == contact[1])
    diag_imag = broadening + contact_width * at_contact.astype(F32)
    magnitude = diag_real * diag_real + diag_imag * diag_imag
    inv_real = diag_real / magnitude
    inv_imag = -diag_imag / magnitude
    return inv_real, inv_imag


def local_rows(parts):
    return 2 * len(blocks_on_or_below(parts)) * LANE


def columns_of(inv_real, inv_imag):
    return jnp.concatenate([inv_real, inv_imag], axis=0).T


def store_left(left, piece, half, c, parts):
    last = (parts - 1) * LANE
    left[half * last : (half + 1) * last, span(c)] = piece[:last]
    bottom = 2 * last + half * LANE
    left[bottom : bottom + LANE, span(c)] = piece[last:]


def times_carried(coupled, g, left, parts):
    product = jnp.dot(coupled, g[...], preferred_element_type=F32).astype(BF16)
    for column in range(2 * parts):
        half, c = (
            (0, column)
            if column < parts
            else (1, parts - 1 if column == parts else column - parts - 1)
        )
        store_left(left, product[:, span(column)], half, c, parts)


def finish_slab(
    s, times_turned, left, g, packed, columns, real_row, imag_row, note, parts, local=None
):
    last = (parts - 1) * LANE
    rows, cols = tile_indices()
    diagonal = rows == cols
    numbers = {block: k for k, block in enumerate(blocks_on_or_below(parts))}
    middles = {}

    def finish(r, c, sr, si):
        k = numbers[r, c]
        real_col, imag_col = columns[0][span(r)], columns[1][span(r)]
        half_real = real_col * sr - imag_col * si
        half_imag = real_col * si + imag_col * sr
        rr, ri = real_row[:, span(c)], imag_row[:, span(c)]
        green_real = half_real * rr - half_imag * ri
        green_imag = half_real * ri + half_imag * rr
        if r == c:
            green_real = green_real + jnp.where(diagonal, real_row[:, span(c)], 0.0)
            green_imag = green_imag + jnp.where(diagonal, imag_row[:, span(c)], 0.0)
            if note is not None:
                middles[r] = diagonal_row(green_imag)
                note(r, middles[r])
        if packed is not None:
            pack_block(packed, r, c, green_real, green_imag, parts)
        if local is not None:
            local[span(2 * k), :] = green_real
            local[span(2 * k + 1), :] = green_imag
        if g is None:
            return
        for half, green in ((0, green_real), (1, green_imag)):
            rounded = green.astype(BF16)
            g[span(r), span(place(parts, half, c))] = rounded
            if r != c:
                g[span(c), span(place(parts, half, r))] = rounded.T

    turned = times_turned(left[...])
    far = turned[2 * last :, :]
    near = turned[: 2 * last, :]
    for c in range(parts):
        finish(parts - 1, c, far[:LANE, span(c)], far[LANE:, span(c)])
    for r in range(parts - 1):
        for c in range(r + 1):
            finish(r, c, near[span(r), span(c)], near[last:, :][span(r), span(c)])
    if packed is not None:
        pack_middles(packed, [middles[r] for r in range(parts)], parts)


def coupling_of(base, wave, cosine):
    return (base.astype(F32) + cosine * wave.astype(F32)).astype(BF16)


def first_segment(
    coupled_of, inv_real, inv_imag, weight, g, left, sent, density, local=None
):
    slabs, orbitals = inv_real.shape
    parts = orbitals // LANE
    down = columns_of(inv_real, inv_imag)
    if density is not None:
        density[0:1, :] += -weight * inv_imag[0:1, :]
    for s in range(1, slabs):
        coupled = coupled_of(s)
        if s == 1:
            wide = coupled.astype(F32)
            for half, inv in ((0, inv_real), (1, inv_imag)):
                piece = (wide * inv[0:1, :].astype(BF16).astype(F32)).astype(BF16)
                for c in range(parts):
                    store_left(left, piece[:, span(c)], half, c, parts)
        else:
            times_carried(coupled, g, left, parts)

        def times_turned(rows):
            return lax.dot_general(
                rows, coupled, (((1,), (1,)), ((), ())), preferred_element_type=F32
            )

        def note(r, middle):
            density[s : s + 1, span(r)] += -weight * middle

        final = s == slabs - 1
        finish_slab(
            s, times_turned, left, None if final else g, sent if final else None,
            (down[:, s : s + 1], down[:, slabs + s : slabs + s + 1]),
            inv_real[s : s + 1, :], inv_imag[s : s + 1, :],
            None if density is None else note, parts, local if final else None,
        )


def copies_of_constants(constants_hbm, contact_hbm, constants, contact, sem):
    return [
        pltpu.make_async_copy(constants_hbm, constants, sem.at[0]),
        pltpu.make_async_copy(contact_hbm, contact, sem.at[1]),
    ]


def copies_of_couplings(base_hbm, wave_hbm, base, wave, sem, slabs_wanted):
    return {
        s: (
            pltpu.make_async_copy(base_hbm.at[s], base.at[s], sem.at[0, s]),
            pltpu.make_async_copy(wave_hbm.at[s], wave.at[s], sem.at[1, s]),
        )
        for s in slabs_wanted
    }


def lead_kernel(
    impulse_count,
    constants_hbm, contact_hbm, onsite_hbm, hopping_hbm, potential_hbm, base_hbm, wave_hbm,
    sent, density, base, wave,
    constants, contact, tables, g, left, small_sem, table_sem, couple_sem,
):
    slabs, orbitals = onsite_hbm.shape
    parts = orbitals // LANE
    position = lax.axis_index("en")
    density[...] = jnp.zeros_like(density)
    small_copies = copies_of_constants(
        constants_hbm, contact_hbm, constants, contact, small_sem
    ) + [
        pltpu.make_async_copy(source, tables.at[k], table_sem.at[k])
        for k, source in enumerate((onsite_hbm, hopping_hbm, potential_hbm))
    ]
    for copy in small_copies:
        copy.start()

    def first_level_amounts():
        momentum, level = first_level_item(0)
        cosine, energy, weight = entry_amounts(constants, impulse_count, momentum, level)
        inv_real, inv_imag = inverse_diagonal(
            position, cosine, energy, contact, tables.at[0], tables.at[1], tables.at[2]
        )
        return cosine, weight, inv_real, inv_imag

    @pl.when(position == 0)
    def _():
        couple_copies = copies_of_couplings(
            base_hbm, wave_hbm, base, wave, couple_sem, range(1, slabs)
        )
        for s in couple_copies:
            for copy in couple_copies[s]:
                copy.start()
        for copy in small_copies:
            copy.wait()

        @pl.when(takes_first_levels())
        def _():
            cosine, weight, inv_real, inv_imag = first_level_amounts()

            def coupled_of(s):
                for copy in couple_copies[s]:
                    copy.wait()
                return coupling_of(base[s], wave[s], cosine)

            first_segment(
                coupled_of, inv_real, inv_imag, weight, g, left, sent, density
            )

        @pl.when(jnp.logical_not(takes_first_levels()))
        def _():
            for s in couple_copies:
                for copy in couple_copies[s]:
                    copy.wait()


    @pl.when(position > 0)
    def _():
        couple_copies = copies_of_couplings(
            base_hbm, wave_hbm, base, wave, couple_sem, range(slabs)
        )
        for s in couple_copies:
            for copy in couple_copies[s]:
                copy.start()
        for copy in small_copies:
            copy.wait()
        for s in couple_copies:
            for copy in couple_copies[s]:
                copy.wait()


def with_scalars(refs, scratch, sem):
    copies = [
        pltpu.make_async_copy(source, target, sem.at[k])
        for k, (source, target) in enumerate(zip(refs, scratch))
    ]
    for copy in copies:
        copy.start()
    for copy in copies:
        copy.wait()


def begin_kernel(
    impulse_count, slot,
    constants_ref, contact_ref, counts_ref,
    onsite, hopping, potential, base, wave, so_far, *refs,
):
    held, refs = refs[:-8], refs[-8:]
    density, sent, constants, contact, counts, scalar_sem, g, left = refs
    slabs, orbitals = onsite.shape
    parts = orbitals // LANE
    position = lax.axis_index("en")
    density[...] = so_far[...]
    active = position == 0
    if slot == 0:

        @pl.when(jnp.logical_and(active, takes_first_levels()))
        def _():
            sent[...] = held[0][...]

        active = jnp.logical_and(active, jnp.logical_not(takes_first_levels()))

    @pl.when(active)
    def _():
        with_scalars(
            (constants_ref, contact_ref, counts_ref), (constants, contact, counts), scalar_sem
        )
        momentum, level = item_of(counts, slot)
        cosine, energy, weight = entry_amounts(constants, impulse_count, momentum, level)
        inv_real, inv_imag = inverse_diagonal(
            position, cosine, energy, contact, onsite, hopping, potential
        )

        def coupled_of(s):
            return coupling_of(base[s], wave[s], cosine)

        first_segment(coupled_of, inv_real, inv_imag, weight, g, left, sent, density)


def prepare(cosine, weight, inv_real, inv_imag, base, wave, couple, entry):
    slabs, orbitals = inv_real.shape
    parts = orbitals // LANE
    for s in range(slabs):
        entry[s] = jnp.broadcast_to(inv_real[s : s + 1, :], entry.shape[1:])
        entry[slabs + s] = jnp.broadcast_to(inv_imag[s : s + 1, :], entry.shape[1:])
    entry[2 * slabs] = jnp.full(entry.shape[1:], weight, F32)

    def one(s, carry):
        couple[s] = coupling_of(base[s], wave[s], cosine)
        return carry

    lax.fori_loop(0, slabs, one, 0)


def prepare_kernel(
    impulse_count,
    constants_ref, contact_ref, counts_ref, onsite, hopping, potential, base, wave,
    couple_0, entry_0,
    couple_1, entry_1,
    constants, contact, counts, scalar_sem,
):
    position = lax.axis_index("en")

    def prepare_slot(slot, made):
        momentum, level = item_of(counts, slot)
        cosine, energy, weight = entry_amounts(constants, impulse_count, momentum, level)
        inv_real, inv_imag = inverse_diagonal(
            position, cosine, energy, contact, onsite, hopping, potential
        )
        prepare(cosine, weight, inv_real, inv_imag, base, wave, *made)

    @pl.when(position > 0)
    def _():
        with_scalars(
            (constants_ref, contact_ref, counts_ref), (constants, contact, counts), scalar_sem
        )
        prepare_slot(0, (couple_0, entry_0))
        prepare_slot(1, (couple_1, entry_1))


def rows_of_entry(entry, slabs):
    inv_real = jnp.concatenate([entry[s, 0:1, :] for s in range(slabs)], axis=0)
    inv_imag = jnp.concatenate([entry[slabs + s, 0:1, :] for s in range(slabs)], axis=0)
    return inv_real, inv_imag, entry[2 * slabs, 0:1, 0:1]


def carrier_kernel(calls, *refs):
    couple, entry = Either(refs[:calls]), Either(refs[calls : 2 * calls])
    carriers, cross = refs[2 * calls :]
    slabs, orbitals, _ = couple.shape
    parts = orbitals // LANE

    @pl.when(lax.axis_index("en") > 0)
    def _():
        inv_real, inv_imag, _ = rows_of_entry(entry, slabs)
        down = jnp.concatenate([inv_real, inv_imag], axis=0).T
        for s in range(slabs):
            here = slice(s * orbitals, (s + 1) * orbitals)
            real_col = down[:, s : s + 1]
            imag_col = down[:, slabs + s : slabs + s + 1]
            if s == 0:
                wide = couple[0].astype(F32)
                real, imag = real_col * wide, imag_col * wide
            else:
                ahead = slice((s - 1) * orbitals, s * orbitals)
                product = jnp.dot(couple[s], carriers[ahead, :], preferred_element_type=F32)
                from_real, from_imag = product[:, :orbitals], product[:, orbitals:]
                real = real_col * from_real - imag_col * from_imag
                imag = real_col * from_imag + imag_col * from_real
            carriers[here, :orbitals] = real.astype(BF16)
            carriers[here, orbitals:] = imag.astype(BF16)
        top = (slabs - 1) * parts
        for r in range(parts):
            for c in range(parts):
                real = carriers[span(top + r), span(c)].T
                imag = carriers[span(top + r), span(parts + c)].T
                cross[span(c), span(r)] = real
                cross[span(parts + c), span(parts + r)] = real
                cross[span(c), span(parts + r)] = imag
                cross[span(parts + c), span(r)] = -imag


def local_kernel(calls, *refs):
    couple, entry = Either(refs[:calls]), Either(refs[calls : 2 * calls])
    local, densities, g, left = refs[2 * calls :]
    slabs = couple.shape[0]

    @pl.when(lax.axis_index("en") > 0)
    def _():
        inv_real, inv_imag, weight = rows_of_entry(entry, slabs)
        densities[...] = jnp.zeros_like(densities)
        first_segment(
            lambda s: couple[s], inv_real, inv_imag, weight, g, left, None, densities, local
        )


def pass_kernel(stage, calls, *refs):
    local = Either(refs[:calls])
    carriers, cross, arrived, sent, wide, half_way = refs[calls:]
    orbitals = carriers.shape[1] // 2
    parts = orbitals // LANE

    @pl.when(lax.axis_index("en") == stage)
    def _():
        def put(half, r, c, block):
            if half == 0:
                wide[span(r), span(c)] = block
                wide[span(parts + r), span(parts + c)] = block
            else:
                wide[span(r), span(parts + c)] = block
                wide[span(parts + r), span(c)] = -block

        unpack_blocks(arrived, put, parts)
        half_way[...] = jnp.dot(
            carriers[carriers.shape[0] - orbitals :, :], wide[...], preferred_element_type=F32
        ).astype(BF16)
        out = jnp.dot(half_way[...], cross[...], preferred_element_type=F32)
        middles = []
        for k, (r, c) in enumerate(blocks_on_or_below(parts)):
            green_real = local[span(2 * k), :] + out[span(r), span(c)]
            green_imag = local[span(2 * k + 1), :] + out[span(r), span(parts + c)]
            pack_block(sent, r, c, green_real, green_imag, parts)
            if r == c:
                middles.append(diagonal_row(green_imag))
        pack_middles(sent, middles, parts)


def density_kernel(calls, carriers, *refs):
    entry, refs = Either(refs[: calls[0]]), refs[calls[0] :]
    local_densities, refs = Either(refs[: calls[1]]), refs[calls[1] :]
    so_far, arrived, (density, wide, total) = refs[0], refs[1:-3], refs[-3:]
    slabs, orbitals = so_far.shape
    parts = orbitals // LANE
    position = lax.axis_index("en")
    density[...] = so_far[...]

    def put(half, r, c, block):
        if half == 0:
            wide[span(r), span(2 * c)] = block
            wide[span(parts + r), span(2 * c + 1)] = block
        else:
            wide[span(r), span(2 * c + 1)] = block
            wide[span(parts + r), span(2 * c)] = -block

    for stage, block in enumerate(arrived, 1):

        @pl.when(position == stage)
        def _():
            unpack_blocks(block, put, parts)

    @pl.when(position > 0)
    def _():
        for c in range(parts):
            product = jnp.dot(
                carriers[...],
                wide[:, 2 * c * LANE : 2 * (c + 1) * LANE],
                preferred_element_type=F32,
            )
            term = product[:, :LANE] * carriers[:, span(parts + c)].astype(F32) + product[
                :, LANE:
            ] * carriers[:, span(c)].astype(F32)
            if c == 0:
                total[...] = term
            else:
                total[...] += term
        weight = entry[2 * slabs, 0:1, :LANE]
        for s in range(slabs):
            for r in range(parts):
                row = jnp.sum(total[span(s * parts + r), :].T, axis=0, keepdims=True)
                density[s : s + 1, span(r)] += (
                    local_densities[s : s + 1, span(r)] - weight * row
                )


def vmem_call(kernel, outs, operands, in_specs, scratch, name, flops, traffic=2**21, **more):
    vmem = pl.BlockSpec(memory_space=pltpu.VMEM)
    return pl.pallas_call(
        kernel,
        out_shape=tuple(outs),
        in_specs=in_specs,
        out_specs=(vmem,) * len(outs),
        scratch_shapes=scratch,
        compiler_params=pltpu.CompilerParams(vmem_limit_bytes=16 * 2**20),
        cost_estimate=pl.CostEstimate(flops=flops, bytes_accessed=traffic, transcendentals=0),
        name=name,
        **more,
    )(*operands)


def split_kernel(inverse, high, middle, low):
    for r in range(inverse.shape[0] // LANE):
        for c in range(inverse.shape[1] // LANE):
            block = inverse[span(r), span(c)].T
            for part in (high, middle, low):
                rounded = block.astype(BF16)
                part[span(c), span(r)] = rounded
                block = block - rounded.astype(F32)


def last_kernel(gathered, doping, high, middle, low, summed, potential):
    total = jnp.sum(gathered[...], axis=0)
    summed[...] = total
    rest = total - doping[...]
    pieces = []
    for _ in range(3):
        pieces.append(rest.astype(BF16).astype(F32))
        rest = rest - pieces[-1]
    rows = total.shape[0]
    answer = jnp.zeros_like(total)
    for count, part in ((1, low), (2, middle), (3, high)):
        padded = -(-3 * rows // 16) * 16 - count * rows
        stacked = jnp.concatenate(
            pieces[:count] + [jnp.zeros((padded, total.shape[1]), F32)], axis=0
        ).astype(BF16)
        product = jnp.dot(stacked, part[...], preferred_element_type=F32)
        for k in reversed(range(count)):
            answer = answer + product[k * rows : (k + 1) * rows]
    potential[...] = answer


def gather_over(values, axis):
    copies = jnp.broadcast_to(values[None], (lax.axis_size(axis),) + values.shape)
    return lax.all_to_all(copies, axis, 0, 0)


def body(
    counts,
    contact_slabs,
    onsite,
    hopping,
    potential_in,
    couple_base,
    couple_wave,
    doping,
    poisson_inverse,
):
    kt_size = lax.axis_size("kt")
    en_size = lax.axis_size("en")
    slabs, orbitals = onsite.shape
    parts = orbitals // LANE
    impulse_count = counts.shape[0] * kt_size
    constants = jnp.asarray(item_constants(impulse_count))
    smem = pl.BlockSpec(memory_space=pltpu.SMEM)
    hbm = pl.BlockSpec(memory_space=pltpu.HBM)
    vmem = pl.BlockSpec(memory_space=pltpu.VMEM)
    flops = 2 * slabs * orbitals**3

    def forward(block, stage):
        return lax.ppermute(block, "en", [(stage, stage + 1)])

    block_shape = jax.ShapeDtypeStruct((packed_rows(orbitals), LANE), BF16)
    density_shape = jax.ShapeDtypeStruct((slabs, orbitals), F32)
    couple_shape = jax.ShapeDtypeStruct((slabs, orbitals, orbitals), BF16)
    entry_shape = jax.ShapeDtypeStruct((2 * slabs + 1, 8, orbitals), F32)
    work = [
        pltpu.VMEM((orbitals, 2 * orbitals), BF16),
        pltpu.VMEM((2 * orbitals, orbitals), BF16),
    ]

    counts_all = lax.all_to_all(jnp.tile(counts, kt_size), "kt", 0, 0, tiled=True)
    given = (constants, contact_slabs, onsite, hopping, potential_in, couple_base, couple_wave)
    pinned = [pltpu.with_memory_space_constraint(t, pltpu.HBM) for t in given]
    block, density, *loaded = vmem_call(
        functools.partial(lead_kernel, impulse_count),
        (block_shape, density_shape, couple_shape, couple_shape),
        pinned,
        [hbm] * len(pinned),
        [
            pltpu.SMEM(constants.shape, F32),
            pltpu.SMEM(contact_slabs.shape, jnp.int32),
            pltpu.VMEM((3, slabs, orbitals), F32),
        ]
        + work
        + [
            pltpu.SemaphoreType.DMA((2,)),
            pltpu.SemaphoreType.DMA((3,)),
            pltpu.SemaphoreType.DMA((2, slabs)),
        ],
        "lead",
        3 * flops,
    )
    block, counts_all = lax.optimization_barrier((block, counts_all))
    small = (constants, contact_slabs, counts_all, onsite, hopping, potential_in)

    anywhere = pl.BlockSpec(memory_space=pl.ANY)
    scalar_scratch = [
        pltpu.SMEM(constants.shape, F32),
        pltpu.SMEM(contact_slabs.shape, jnp.int32),
        pltpu.SMEM(counts_all.shape, jnp.int32),
        pltpu.SemaphoreType.DMA((3,)),
    ]

    def begin(slot, density, *held):
        return vmem_call(
            functools.partial(begin_kernel, impulse_count, slot),
            (density_shape, block_shape),
            (*small, *loaded, density, *held),
            [anywhere] * 3 + [vmem] * (6 + len(held)),
            scalar_scratch + work,
            f"begin_{slot}",
            3 * flops,
            input_output_aliases={8: 0, 9: 1} if held else {8: 0},
        )

    density, block = begin(0, density, block)
    arrived = [forward(block, 0)]
    density, block = begin(1, density)
    arrived.append(forward(block, 0))
    small, _ = lax.optimization_barrier((small, block))
    made = vmem_call(
        functools.partial(prepare_kernel, impulse_count),
        (couple_shape, entry_shape) * 2,
        (*small, *loaded),
        [anywhere] * 3 + [vmem] * 5,
        scalar_scratch,
        "prepare",
        flops // 16,
        2**16,
    )
    made = [[(one,) for one in made[:2]], [(one,) for one in made[2:]]]

    carriers_shape = jax.ShapeDtypeStruct((slabs * orbitals, 2 * orbitals), BF16)
    double_shape = jax.ShapeDtypeStruct((2 * orbitals, 2 * orbitals), BF16)

    def carriers_of(slot):
        couple, entry = made[slot]
        return vmem_call(
            functools.partial(carrier_kernel, len(couple)),
            (carriers_shape, double_shape),
            (*couple, *entry),
            [vmem] * (2 * len(couple)),
            [],
            f"carriers_{slot}",
            flops // 16,
            2**16,
        )

    def local_of(slot):
        couple, entry = made[slot]
        return vmem_call(
            functools.partial(local_kernel, len(couple)),
            (jax.ShapeDtypeStruct((local_rows(parts), LANE), F32), density_shape),
            (*couple, *entry),
            [vmem] * (2 * len(couple)),
            work,
            f"local_{slot}",
            flops // 16,
            2**16,
        )

    def pass_on(stage, slot, block):
        calls = [one[0] for one in local[slot]]
        return vmem_call(
            functools.partial(pass_kernel, stage, len(calls)),
            (block_shape,),
            (*calls, *carried[slot], block),
            [vmem] * (3 + len(calls)),
            [
                pltpu.VMEM(double_shape.shape, BF16),
                pltpu.VMEM((orbitals, 2 * orbitals), BF16),
            ],
            f"pass_{stage}_{slot}",
            2 * flops,
        )[0]

    def densities(slot, density, came):
        entry = made[slot][1]
        calls = [one[1] for one in local[slot]]
        before = 1 + len(entry) + len(calls)
        return vmem_call(
            functools.partial(density_kernel, (len(entry), len(calls))),
            (density_shape,),
            (carried[slot][0], *entry, *calls, density, *came),
            [vmem] * (before + 1 + len(came)),
            [
                pltpu.VMEM(double_shape.shape, BF16),
                pltpu.VMEM((slabs * orbitals, LANE), F32),
            ],
            f"density_{slot}",
            4 * flops,
            input_output_aliases={before: 0},
        )[0]

    came = [[arrived[0]], [arrived[1]]]
    carried, local = [carriers_of(0)], [[local_of(0)]]
    for stage in range(1, en_size - 1):
        for slot in range(2):
            if stage == 1 and slot == 1:
                made[1], _ = lax.optimization_barrier((made[1], block))
                carried.append(carriers_of(1))
                local.append([local_of(1)])
            block = pass_on(stage, slot, came[slot][-1])
            came[slot].append(forward(block, stage))
    for slot in range(2):
        density = densities(slot, density, came[slot])
    part_shape = jax.ShapeDtypeStruct(poisson_inverse.shape, BF16)
    inverse, _ = lax.optimization_barrier((poisson_inverse, block))
    split = vmem_call(
        split_kernel, (part_shape,) * 3, (inverse,), [vmem], [], "split_inverse", 2 * flops
    )
    density, *split = lax.optimization_barrier((density, *split))
    return vmem_call(
        last_kernel,
        (density_shape, density_shape),
        (gather_over(density, "kt"), doping, *split),
        [vmem] * 5,
        [],
        "last",
        flops // slabs,
    )


def solution(mesh):
    return jax.shard_map(
        body,
        mesh=mesh,
        in_specs=(
            P("kt"),
            P(),
            P("en", None),
            P("en", None),
            P("en", None),
            P("en", None, None),
            P("en", None, None),
            P("en", None),
            P(),
        ),
        out_specs=(P("en", None), P("en", None)),
        check_vma=False,
    )
```

```python
import functools

import jax
import jax.numpy as jnp
import numpy as np
from jax import lax
from jax.experimental import pallas as pl
from jax.experimental.pallas import tpu as pltpu
from jax.sharding import PartitionSpec as P

EMAX = 4
LANE = 128
F32 = jnp.float32
BF16 = jnp.bfloat16

bottom_sample_mark = -1.0
sample_gap = 0.25
electrode_filling = -0.5
boltzmann_spread = 0.1
broadening = 1.0
contact_width = 0.5


def item_constants(impulse_count):
    wave = np.float32(np.pi) * (np.arange(impulse_count, dtype=np.float32) + np.float32(0.5))
    cosine = np.cos(wave / np.float32(impulse_count))
    energy = bottom_sample_mark + sample_gap * np.arange(EMAX)
    weight = sample_gap / (1.0 + np.exp((energy - electrode_filling) / boltzmann_spread)) / np.pi
    return np.concatenate([cosine, weight]).astype(np.float32)


def span(k):
    return slice(k * LANE, (k + 1) * LANE)


def place(parts, half, c):
    if c == parts - 1:
        return parts - 1 + half
    return c if half == 0 else parts + 1 + c


def blocks_on_or_below(parts):
    return [(r, c) for r in range(parts) for c in range(r + 1)]


def packed_rows(orbitals):
    parts = orbitals // LANE
    return parts * parts * LANE + 16


def pairs_below(parts):
    return [(r, c) for r in range(parts) for c in range(r)]


def pair_slot(parts, r, c, half):
    return 2 * pairs_below(parts).index((r, c)) + half


def middle_slot(parts, r):
    return parts * (parts - 1) + r


def tile_indices():
    rows = lax.broadcasted_iota(jnp.int32, (LANE, LANE), 0)
    cols = lax.broadcasted_iota(jnp.int32, (LANE, LANE), 1)
    return rows, cols


def unpack_blocks(packed, put, parts):
    rows, cols = tile_indices()
    for r, c in pairs_below(parts):
        for half in range(2):
            block = packed[span(pair_slot(parts, r, c, half)), :]
            put(half, r, c, block)
            put(half, c, r, block.T)
    at = parts * parts * LANE
    for r in range(parts):
        block = packed[span(middle_slot(parts, r)), :]
        turned = block.T
        middle = packed[at : at + 16, :][r : r + 1, :]
        put(0, r, r, jnp.where(rows <= cols, block, turned))
        put(1, r, r, jnp.where(rows > cols, block, jnp.where(rows == cols, middle, turned)))


def pack_block(packed, r, c, green_real, green_imag, parts):
    rows, cols = tile_indices()
    if r == c:
        packed[span(middle_slot(parts, r)), :] = jnp.where(
            rows <= cols, green_real, green_imag
        ).astype(BF16)
    else:
        packed[span(pair_slot(parts, r, c, 0)), :] = green_real.astype(BF16)
        packed[span(pair_slot(parts, r, c, 1)), :] = green_imag.astype(BF16)


def pack_middles(packed, middles, parts):
    rest = jnp.zeros((16 - parts, LANE), F32)
    at = parts * parts * LANE
    packed[at : at + 16, :] = jnp.concatenate(middles + [rest], axis=0).astype(BF16)


def diagonal_row(block):
    rows, cols = tile_indices()
    return jnp.sum(jnp.where(rows == cols, block, 0.0), axis=0, keepdims=True)


def takes_first_levels():
    return lax.axis_index("kt") % 2 == 1


class Either:
    def __init__(self, refs):
        self.refs = refs
        self.shape = refs[0].shape

    def __getitem__(self, index):
        if len(self.refs) == 1:
            return self.refs[0][index]
        return jnp.where(takes_first_levels(), self.refs[1][index], self.refs[0][index])


def first_level_item(slot):
    return lax.axis_index("kt") - 1 + slot, jnp.int32(0)


def item_of(counts, slot):
    wanted = lax.axis_index("kt") + slot

    def one(k, state):
        momentum, before = state
        extra = counts[k] - 1
        take = jnp.logical_and(momentum == k, before + extra <= wanted)
        return (jnp.where(take, k + 1, momentum), jnp.where(take, before + extra, before))

    momentum, before = lax.fori_loop(0, counts.shape[0], one, (jnp.int32(0), jnp.int32(0)))
    momentum = jnp.minimum(momentum, counts.shape[0] - 1)
    level = jnp.clip(1 + wanted - before, 0, EMAX - 1)
    own_momentum, own_level = first_level_item(slot)
    own = takes_first_levels()
    return jnp.where(own, own_momentum, momentum), jnp.where(own, own_level, level)


def entry_amounts(constants, impulse_count, momentum, level):
    energy = bottom_sample_mark + sample_gap * level.astype(F32)
    return constants[momentum], energy, constants[impulse_count + level]


def inverse_diagonal(position, cosine, energy, contact, onsite, hopping, potential):
    slabs, orbitals = onsite.shape
    diag_real = energy + (-onsite[...] - potential[...]) - cosine * hopping[...]
    slab_in = lax.broadcasted_iota(jnp.int32, (slabs, orbitals), 0) + position * slabs
    at_contact = jnp.logical_or(slab_in == contact[0], slab_in == contact[1])
    diag_imag = broadening + contact_width * at_contact.astype(F32)
    magnitude = diag_real * diag_real + diag_imag * diag_imag
    inv_real = diag_real / magnitude
    inv_imag = -diag_imag / magnitude
    return inv_real, inv_imag


def local_rows(parts):
    return 2 * len(blocks_on_or_below(parts)) * LANE


def columns_of(inv_real, inv_imag):
    return jnp.concatenate([inv_real, inv_imag], axis=0).T


def store_left(left, piece, half, c, parts):
    last = (parts - 1) * LANE
    left[half * last : (half + 1) * last, span(c)] = piece[:last]
    bottom = 2 * last + half * LANE
    left[bottom : bottom + LANE, span(c)] = piece[last:]


def times_carried(coupled, g, left, parts):
    product = jnp.dot(coupled, g[...], preferred_element_type=F32)
    keep_product(product.astype(BF16), left, parts)


def keep_product(product, left, parts):
    for column in range(2 * parts):
        half, c = (
            (0, column)
            if column < parts
            else (1, parts - 1 if column == parts else column - parts - 1)
        )
        store_left(left, product[:, span(column)], half, c, parts)


def finish_slab(
    s, times_turned, left, g, packed, columns, real_row, imag_row, note, parts, local=None, offset=0
):
    last = (parts - 1) * LANE
    rows, cols = tile_indices()
    diagonal = rows == cols
    numbers = {block: k for k, block in enumerate(blocks_on_or_below(parts))}
    middles = {}

    def finish(r, c, sr, si):
        k = numbers[r, c]
        real_col, imag_col = columns[0][span(r)], columns[1][span(r)]
        half_real = real_col * sr - imag_col * si
        half_imag = real_col * si + imag_col * sr
        rr, ri = real_row[:, span(c)], imag_row[:, span(c)]
        green_real = half_real * rr - half_imag * ri
        green_imag = half_real * ri + half_imag * rr
        if r == c:
            green_real = green_real + jnp.where(diagonal, real_row[:, span(c)], 0.0)
            green_imag = green_imag + jnp.where(diagonal, imag_row[:, span(c)], 0.0)
            if note is not None:
                middles[r] = diagonal_row(green_imag)
                note(r, middles[r])
        if packed is not None:
            pack_block(packed, r, c, green_real, green_imag, parts)
        if local is not None:
            local[span(2 * k), :] = green_real
            local[span(2 * k + 1), :] = green_imag
        if g is None:
            return
        for half, green in ((0, green_real), (1, green_imag)):
            rounded = green.astype(BF16)
            g[span(r), span(offset + place(parts, half, c))] = rounded
            if r != c:
                g[span(c), span(offset + place(parts, half, r))] = rounded.T

    turned = times_turned(left[...])
    far = turned[2 * last :, :]
    near = turned[: 2 * last, :]
    for c in range(parts):
        finish(parts - 1, c, far[:LANE, span(c)], far[LANE:, span(c)])
    for r in range(parts - 1):
        for c in range(r + 1):
            finish(r, c, near[span(r), span(c)], near[last:, :][span(r), span(c)])
    if packed is not None:
        pack_middles(packed, [middles[r] for r in range(parts)], parts)


def coupling_of(base, wave, cosine):
    return (base.astype(F32) + cosine * wave.astype(F32)).astype(BF16)


def first_segment(
    coupled_of, inv_real, inv_imag, weight, g, left, sent, density, local=None
):
    slabs, orbitals = inv_real.shape
    parts = orbitals // LANE
    down = columns_of(inv_real, inv_imag)
    if density is not None:
        density[0:1, :] += -weight * inv_imag[0:1, :]
    for s in range(1, slabs):
        coupled = coupled_of(s)
        if s == 1:
            wide = coupled.astype(F32)
            for half, inv in ((0, inv_real), (1, inv_imag)):
                piece = (wide * inv[0:1, :].astype(BF16).astype(F32)).astype(BF16)
                for c in range(parts):
                    store_left(left, piece[:, span(c)], half, c, parts)
        else:
            times_carried(coupled, g, left, parts)

        def times_turned(rows):
            return lax.dot_general(
                rows, coupled, (((1,), (1,)), ((), ())), preferred_element_type=F32
            )

        def note(r, middle):
            density[s : s + 1, span(r)] += -weight * middle

        final = s == slabs - 1
        finish_slab(
            s, times_turned, left, None if final else g, sent if final else None,
            (down[:, s : s + 1], down[:, slabs + s : slabs + s + 1]),
            inv_real[s : s + 1, :], inv_imag[s : s + 1, :],
            None if density is None else note, parts, local if final else None,
        )


def copies_of_constants(constants_hbm, contact_hbm, constants, contact, sem):
    return [
        pltpu.make_async_copy(constants_hbm, constants, sem.at[0]),
        pltpu.make_async_copy(contact_hbm, contact, sem.at[1]),
    ]


def copies_of_couplings(base_hbm, wave_hbm, base, wave, sem, slabs_wanted):
    return {
        s: (
            pltpu.make_async_copy(base_hbm.at[s], base.at[s], sem.at[0, s]),
            pltpu.make_async_copy(wave_hbm.at[s], wave.at[s], sem.at[1, s]),
        )
        for s in slabs_wanted
    }


def lead_kernel(
    impulse_count,
    constants_hbm, contact_hbm, onsite_hbm, hopping_hbm, potential_hbm, base_hbm, wave_hbm,
    sent, density, base, wave,
    constants, contact, tables, g, left, small_sem, table_sem, couple_sem,
):
    slabs, orbitals = onsite_hbm.shape
    parts = orbitals // LANE
    position = lax.axis_index("en")
    density[...] = jnp.zeros_like(density)
    small_copies = copies_of_constants(
        constants_hbm, contact_hbm, constants, contact, small_sem
    ) + [
        pltpu.make_async_copy(source, tables.at[k], table_sem.at[k])
        for k, source in enumerate((onsite_hbm, hopping_hbm, potential_hbm))
    ]
    for copy in small_copies:
        copy.start()

    def first_level_amounts():
        momentum, level = first_level_item(0)
        cosine, energy, weight = entry_amounts(constants, impulse_count, momentum, level)
        inv_real, inv_imag = inverse_diagonal(
            position, cosine, energy, contact, tables.at[0], tables.at[1], tables.at[2]
        )
        return cosine, weight, inv_real, inv_imag

    @pl.when(position == 0)
    def _():
        couple_copies = copies_of_couplings(
            base_hbm, wave_hbm, base, wave, couple_sem, range(1, slabs)
        )
        for s in couple_copies:
            for copy in couple_copies[s]:
                copy.start()
        for copy in small_copies:
            copy.wait()

        @pl.when(takes_first_levels())
        def _():
            cosine, weight, inv_real, inv_imag = first_level_amounts()

            def coupled_of(s):
                for copy in couple_copies[s]:
                    copy.wait()
                return coupling_of(base[s], wave[s], cosine)

            first_segment(
                coupled_of, inv_real, inv_imag, weight, g, left, sent, density
            )

        @pl.when(jnp.logical_not(takes_first_levels()))
        def _():
            for s in couple_copies:
                for copy in couple_copies[s]:
                    copy.wait()


    @pl.when(position > 0)
    def _():
        couple_copies = copies_of_couplings(
            base_hbm, wave_hbm, base, wave, couple_sem, range(slabs)
        )
        for s in couple_copies:
            for copy in couple_copies[s]:
                copy.start()
        for copy in small_copies:
            copy.wait()
        for s in couple_copies:
            for copy in couple_copies[s]:
                copy.wait()


def with_scalars(refs, scratch, sem):
    copies = [
        pltpu.make_async_copy(source, target, sem.at[k])
        for k, (source, target) in enumerate(zip(refs, scratch))
    ]
    for copy in copies:
        copy.start()
    for copy in copies:
        copy.wait()


def begin_kernel(
    impulse_count, slot,
    constants_ref, contact_ref, counts_ref,
    onsite, hopping, potential, base, wave, so_far, *refs,
):
    held, refs = refs[:-8], refs[-8:]
    density, sent, constants, contact, counts, scalar_sem, g, left = refs
    slabs, orbitals = onsite.shape
    parts = orbitals // LANE
    position = lax.axis_index("en")
    density[...] = so_far[...]
    active = position == 0
    if slot == 0:

        @pl.when(jnp.logical_and(active, takes_first_levels()))
        def _():
            sent[...] = held[0][...]

        active = jnp.logical_and(active, jnp.logical_not(takes_first_levels()))

    @pl.when(active)
    def _():
        with_scalars(
            (constants_ref, contact_ref, counts_ref), (constants, contact, counts), scalar_sem
        )
        momentum, level = item_of(counts, slot)
        cosine, energy, weight = entry_amounts(constants, impulse_count, momentum, level)
        inv_real, inv_imag = inverse_diagonal(
            position, cosine, energy, contact, onsite, hopping, potential
        )

        def coupled_of(s):
            return coupling_of(base[s], wave[s], cosine)

        first_segment(coupled_of, inv_real, inv_imag, weight, g, left, sent, density)


def prepare(cosine, weight, inv_real, inv_imag, base, wave, couple, entry):
    slabs, orbitals = inv_real.shape
    parts = orbitals // LANE
    for s in range(slabs):
        entry[s] = jnp.broadcast_to(inv_real[s : s + 1, :], entry.shape[1:])
        entry[slabs + s] = jnp.broadcast_to(inv_imag[s : s + 1, :], entry.shape[1:])
    entry[2 * slabs] = jnp.full(entry.shape[1:], weight, F32)

    def one(s, carry):
        couple[s] = coupling_of(base[s], wave[s], cosine)
        return carry

    lax.fori_loop(0, slabs, one, 0)


def prepare_kernel(
    impulse_count,
    constants_ref, contact_ref, counts_ref, onsite, hopping, potential, base, wave,
    couple_0, entry_0,
    couple_1, entry_1,
    constants, contact, counts, scalar_sem,
):
    position = lax.axis_index("en")

    def prepare_slot(slot, made):
        momentum, level = item_of(counts, slot)
        cosine, energy, weight = entry_amounts(constants, impulse_count, momentum, level)
        inv_real, inv_imag = inverse_diagonal(
            position, cosine, energy, contact, onsite, hopping, potential
        )
        prepare(cosine, weight, inv_real, inv_imag, base, wave, *made)

    @pl.when(position > 0)
    def _():
        with_scalars(
            (constants_ref, contact_ref, counts_ref), (constants, contact, counts), scalar_sem
        )
        prepare_slot(0, (couple_0, entry_0))
        prepare_slot(1, (couple_1, entry_1))


def rows_of_entry(entry, slabs):
    inv_real = jnp.concatenate([entry[s, 0:1, :] for s in range(slabs)], axis=0)
    inv_imag = jnp.concatenate([entry[slabs + s, 0:1, :] for s in range(slabs)], axis=0)
    return inv_real, inv_imag, entry[2 * slabs, 0:1, 0:1]


def operator_kernel(couple, entry, carriers, cross, local, densities, both, left):
    slabs, orbitals, _ = couple.shape
    parts = orbitals // LANE

    @pl.when(lax.axis_index("en") > 0)
    def _():
        inv_real, inv_imag, weight = rows_of_entry(entry, slabs)
        down = columns_of(inv_real, inv_imag)
        for s in range(slabs):
            coupled = couple[s]
            real_col = down[:, s : s + 1]
            imag_col = down[:, slabs + s : slabs + s + 1]
            real_row, imag_row = inv_real[s : s + 1, :], inv_imag[s : s + 1, :]
            if s == 0:
                wide = coupled.astype(F32)
                real, imag = real_col * wide, imag_col * wide
                densities[0:1, :] = -weight * imag_row
            else:
                width = 2 * orbitals if s == 1 else 4 * orbitals
                product = jnp.dot(coupled, both[:, :width], preferred_element_type=F32)
                from_real, from_imag = product[:, :orbitals], product[:, orbitals : 2 * orbitals]
                real = real_col * from_real - imag_col * from_imag
                imag = real_col * from_imag + imag_col * from_real
                if s == 1:
                    wide = coupled.astype(F32)
                    for half, inv in ((0, inv_real), (1, inv_imag)):
                        piece = (wide * inv[0:1, :].astype(BF16).astype(F32)).astype(BF16)
                        for c in range(parts):
                            store_left(left, piece[:, span(c)], half, c, parts)
                else:
                    keep_product(product[:, 2 * orbitals :].astype(BF16), left, parts)
            real, imag = real.astype(BF16), imag.astype(BF16)
            here = slice(s * orbitals, (s + 1) * orbitals)
            carriers[here, :orbitals] = real
            carriers[here, orbitals:] = imag
            if s < slabs - 1:
                both[:, :orbitals] = real
                both[:, orbitals : 2 * orbitals] = imag
            if s == 0:
                continue

            def times_turned(rows):
                return lax.dot_general(
                    rows, coupled, (((1,), (1,)), ((), ())), preferred_element_type=F32
                )

            def note(r, middle):
                densities[s : s + 1, span(r)] = -weight * middle

            final = s == slabs - 1
            finish_slab(
                s, times_turned, left, None if final else both, None,
                (real_col, imag_col), real_row, imag_row, note, parts,
                local if final else None, 2 * parts,
            )
        top = (slabs - 1) * parts
        for r in range(parts):
            for c in range(parts):
                real = carriers[span(top + r), span(c)].T
                imag = carriers[span(top + r), span(parts + c)].T
                cross[span(c), span(r)] = real
                cross[span(parts + c), span(parts + r)] = real
                cross[span(c), span(parts + r)] = imag
                cross[span(parts + c), span(r)] = -imag


def pass_kernel(stage, calls, *refs):
    local = Either(refs[:calls])
    carriers, cross, arrived, sent, wide, half_way = refs[calls:]
    orbitals = carriers.shape[1] // 2
    parts = orbitals // LANE

    @pl.when(lax.axis_index("en") == stage)
    def _():
        def put(half, r, c, block):
            if half == 0:
                wide[span(r), span(c)] = block
                wide[span(parts + r), span(parts + c)] = block
            else:
                wide[span(r), span(parts + c)] = block
                wide[span(parts + r), span(c)] = -block

        unpack_blocks(arrived, put, parts)
        half_way[...] = jnp.dot(
            carriers[carriers.shape[0] - orbitals :, :], wide[...], preferred_element_type=F32
        ).astype(BF16)
        out = jnp.dot(half_way[...], cross[...], preferred_element_type=F32)
        middles = []
        for k, (r, c) in enumerate(blocks_on_or_below(parts)):
            green_real = local[span(2 * k), :] + out[span(r), span(c)]
            green_imag = local[span(2 * k + 1), :] + out[span(r), span(parts + c)]
            pack_block(sent, r, c, green_real, green_imag, parts)
            if r == c:
                middles.append(diagonal_row(green_imag))
        pack_middles(sent, middles, parts)


def density_kernel(calls, carriers, *refs):
    entry, refs = Either(refs[: calls[0]]), refs[calls[0] :]
    local_densities, refs = Either(refs[: calls[1]]), refs[calls[1] :]
    so_far, arrived, (density, wide, total) = refs[0], refs[1:-3], refs[-3:]
    slabs, orbitals = so_far.shape
    parts = orbitals // LANE
    position = lax.axis_index("en")
    density[...] = so_far[...]

    def put(half, r, c, block):
        if half == 0:
            wide[span(r), span(2 * c)] = block
            wide[span(parts + r), span(2 * c + 1)] = block
        else:
            wide[span(r), span(2 * c + 1)] = block
            wide[span(parts + r), span(2 * c)] = -block

    for stage, block in enumerate(arrived, 1):

        @pl.when(position == stage)
        def _():
            unpack_blocks(block, put, parts)

    @pl.when(position > 0)
    def _():
        for c in range(parts):
            product = jnp.dot(
                carriers[...],
                wide[:, 2 * c * LANE : 2 * (c + 1) * LANE],
                preferred_element_type=F32,
            )
            term = product[:, :LANE] * carriers[:, span(parts + c)].astype(F32) + product[
                :, LANE:
            ] * carriers[:, span(c)].astype(F32)
            if c == 0:
                total[...] = term
            else:
                total[...] += term
        weight = entry[2 * slabs, 0:1, :LANE]
        for s in range(slabs):
            for r in range(parts):
                row = jnp.sum(total[span(s * parts + r), :].T, axis=0, keepdims=True)
                density[s : s + 1, span(r)] += (
                    local_densities[s : s + 1, span(r)] - weight * row
                )


def vmem_call(kernel, outs, operands, in_specs, scratch, name, flops, traffic=2**21, **more):
    vmem = pl.BlockSpec(memory_space=pltpu.VMEM)
    return pl.pallas_call(
        kernel,
        out_shape=tuple(outs),
        in_specs=in_specs,
        out_specs=(vmem,) * len(outs),
        scratch_shapes=scratch,
        compiler_params=pltpu.CompilerParams(vmem_limit_bytes=16 * 2**20),
        cost_estimate=pl.CostEstimate(flops=flops, bytes_accessed=traffic, transcendentals=0),
        name=name,
        **more,
    )(*operands)


def split_kernel(inverse, high, middle, low):
    for r in range(inverse.shape[0] // LANE):
        for c in range(inverse.shape[1] // LANE):
            block = inverse[span(r), span(c)].T
            for part in (high, middle, low):
                rounded = block.astype(BF16)
                part[span(c), span(r)] = rounded
                block = block - rounded.astype(F32)


def last_kernel(gathered, doping, high, middle, low, summed, potential):
    total = jnp.sum(gathered[...], axis=0)
    summed[...] = total
    rest = total - doping[...]
    pieces = []
    for _ in range(3):
        pieces.append(rest.astype(BF16).astype(F32))
        rest = rest - pieces[-1]
    rows = total.shape[0]
    answer = jnp.zeros_like(total)
    for count, part in ((1, low), (2, middle), (3, high)):
        padded = -(-3 * rows // 16) * 16 - count * rows
        stacked = jnp.concatenate(
            pieces[:count] + [jnp.zeros((padded, total.shape[1]), F32)], axis=0
        ).astype(BF16)
        product = jnp.dot(stacked, part[...], preferred_element_type=F32)
        for k in reversed(range(count)):
            answer = answer + product[k * rows : (k + 1) * rows]
    potential[...] = answer


def gather_over(values, axis):
    copies = jnp.broadcast_to(values[None], (lax.axis_size(axis),) + values.shape)
    return lax.all_to_all(copies, axis, 0, 0)


def body(
    counts,
    contact_slabs,
    onsite,
    hopping,
    potential_in,
    couple_base,
    couple_wave,
    doping,
    poisson_inverse,
):
    kt_size = lax.axis_size("kt")
    en_size = lax.axis_size("en")
    slabs, orbitals = onsite.shape
    parts = orbitals // LANE
    impulse_count = counts.shape[0] * kt_size
    constants = jnp.asarray(item_constants(impulse_count))
    smem = pl.BlockSpec(memory_space=pltpu.SMEM)
    hbm = pl.BlockSpec(memory_space=pltpu.HBM)
    vmem = pl.BlockSpec(memory_space=pltpu.VMEM)
    flops = 2 * slabs * orbitals**3

    def forward(block, stage):
        return lax.ppermute(block, "en", [(stage, stage + 1)])

    block_shape = jax.ShapeDtypeStruct((packed_rows(orbitals), LANE), BF16)
    density_shape = jax.ShapeDtypeStruct((slabs, orbitals), F32)
    couple_shape = jax.ShapeDtypeStruct((slabs, orbitals, orbitals), BF16)
    entry_shape = jax.ShapeDtypeStruct((2 * slabs + 1, 8, orbitals), F32)
    work = [
        pltpu.VMEM((orbitals, 2 * orbitals), BF16),
        pltpu.VMEM((2 * orbitals, orbitals), BF16),
    ]

    counts_all = lax.all_to_all(jnp.tile(counts, kt_size), "kt", 0, 0, tiled=True)
    given = (constants, contact_slabs, onsite, hopping, potential_in, couple_base, couple_wave)
    pinned = [pltpu.with_memory_space_constraint(t, pltpu.HBM) for t in given]
    block, density, *loaded = vmem_call(
        functools.partial(lead_kernel, impulse_count),
        (block_shape, density_shape, couple_shape, couple_shape),
        pinned,
        [hbm] * len(pinned),
        [
            pltpu.SMEM(constants.shape, F32),
            pltpu.SMEM(contact_slabs.shape, jnp.int32),
            pltpu.VMEM((3, slabs, orbitals), F32),
        ]
        + work
        + [
            pltpu.SemaphoreType.DMA((2,)),
            pltpu.SemaphoreType.DMA((3,)),
            pltpu.SemaphoreType.DMA((2, slabs)),
        ],
        "lead",
        3 * flops,
    )
    block, counts_all = lax.optimization_barrier((block, counts_all))
    small = (constants, contact_slabs, counts_all, onsite, hopping, potential_in)

    anywhere = pl.BlockSpec(memory_space=pl.ANY)
    scalar_scratch = [
        pltpu.SMEM(constants.shape, F32),
        pltpu.SMEM(contact_slabs.shape, jnp.int32),
        pltpu.SMEM(counts_all.shape, jnp.int32),
        pltpu.SemaphoreType.DMA((3,)),
    ]

    def begin(slot, density, *held):
        return vmem_call(
            functools.partial(begin_kernel, impulse_count, slot),
            (density_shape, block_shape),
            (*small, *loaded, density, *held),
            [anywhere] * 3 + [vmem] * (6 + len(held)),
            scalar_scratch + work,
            f"begin_{slot}",
            3 * flops,
            input_output_aliases={8: 0, 9: 1} if held else {8: 0},
        )

    density, block = begin(0, density, block)
    arrived = [forward(block, 0)]
    density, block = begin(1, density)
    arrived.append(forward(block, 0))
    small, _ = lax.optimization_barrier((small, block))
    made = vmem_call(
        functools.partial(prepare_kernel, impulse_count),
        (couple_shape, entry_shape) * 2,
        (*small, *loaded),
        [anywhere] * 3 + [vmem] * 5,
        scalar_scratch,
        "prepare",
        flops // 16,
        2**16,
    )
    made = [[(one,) for one in made[:2]], [(one,) for one in made[2:]]]

    carriers_shape = jax.ShapeDtypeStruct((slabs * orbitals, 2 * orbitals), BF16)
    double_shape = jax.ShapeDtypeStruct((2 * orbitals, 2 * orbitals), BF16)

    def operator_of(slot):
        (couple,), (entry,) = made[slot]
        results = vmem_call(
            operator_kernel,
            (
                carriers_shape,
                double_shape,
                jax.ShapeDtypeStruct((local_rows(parts), LANE), F32),
                density_shape,
            ),
            (couple, entry),
            [vmem] * 2,
            [
                pltpu.VMEM((orbitals, 4 * orbitals), BF16),
                pltpu.VMEM((2 * orbitals, orbitals), BF16),
            ],
            f"operator_{slot}",
            flops // 16,
            2**16,
        )
        carried.append(results[:2])
        local.append([results[2:]])

    def pass_on(stage, slot, block):
        calls = [one[0] for one in local[slot]]
        return vmem_call(
            functools.partial(pass_kernel, stage, len(calls)),
            (block_shape,),
            (*calls, *carried[slot], block),
            [vmem] * (3 + len(calls)),
            [
                pltpu.VMEM(double_shape.shape, BF16),
                pltpu.VMEM((orbitals, 2 * orbitals), BF16),
            ],
            f"pass_{stage}_{slot}",
            2 * flops,
        )[0]

    def densities(slot, density, came):
        entry = made[slot][1]
        calls = [one[1] for one in local[slot]]
        before = 1 + len(entry) + len(calls)
        return vmem_call(
            functools.partial(density_kernel, (len(entry), len(calls))),
            (density_shape,),
            (carried[slot][0], *entry, *calls, density, *came),
            [vmem] * (before + 1 + len(came)),
            [
                pltpu.VMEM(double_shape.shape, BF16),
                pltpu.VMEM((slabs * orbitals, LANE), F32),
            ],
            f"density_{slot}",
            4 * flops,
            input_output_aliases={before: 0},
        )[0]

    came = [[arrived[0]], [arrived[1]]]
    carried, local = [], []
    operator_of(0)
    for stage in range(1, en_size - 1):
        for slot in range(2):
            if stage == 1 and slot == 1:
                made[1], _ = lax.optimization_barrier((made[1], block))
                operator_of(1)
            block = pass_on(stage, slot, came[slot][-1])
            came[slot].append(forward(block, stage))
    for slot in range(2):
        density = densities(slot, density, came[slot])
    part_shape = jax.ShapeDtypeStruct(poisson_inverse.shape, BF16)
    inverse, _ = lax.optimization_barrier((poisson_inverse, block))
    split = vmem_call(
        split_kernel, (part_shape,) * 3, (inverse,), [vmem], [], "split_inverse", 2 * flops
    )
    density, *split = lax.optimization_barrier((density, *split))
    return vmem_call(
        last_kernel,
        (density_shape, density_shape),
        (gather_over(density, "kt"), doping, *split),
        [vmem] * 5,
        [],
        "last",
        flops // slabs,
    )


def solution(mesh):
    return jax.shard_map(
        body,
        mesh=mesh,
        in_specs=(
            P("kt"),
            P(),
            P("en", None),
            P("en", None),
            P("en", None),
            P("en", None, None),
            P("en", None, None),
            P("en", None),
            P(),
        ),
        out_specs=(P("en", None), P("en", None)),
        check_vma=False,
    )
```

```python
import functools

import jax
import jax.numpy as jnp
import numpy as np
from jax import lax
from jax.experimental import pallas as pl
from jax.experimental.pallas import tpu as pltpu
from jax.sharding import PartitionSpec as P

EMAX = 4
LANE = 128
F32 = jnp.float32
BF16 = jnp.bfloat16

bottom_sample_mark = -1.0
sample_gap = 0.25
electrode_filling = -0.5
boltzmann_spread = 0.1
broadening = 1.0
contact_width = 0.5


def item_constants(impulse_count):
    wave = np.float32(np.pi) * (np.arange(impulse_count, dtype=np.float32) + np.float32(0.5))
    cosine = np.cos(wave / np.float32(impulse_count))
    energy = bottom_sample_mark + sample_gap * np.arange(EMAX)
    weight = sample_gap / (1.0 + np.exp((energy - electrode_filling) / boltzmann_spread)) / np.pi
    return np.concatenate([cosine, weight]).astype(np.float32)


def span(k):
    return slice(k * LANE, (k + 1) * LANE)


def place(parts, half, c):
    if c == parts - 1:
        return parts - 1 + half
    return c if half == 0 else parts + 1 + c


def blocks_on_or_below(parts):
    return [(r, c) for r in range(parts) for c in range(r + 1)]


def packed_rows(orbitals):
    parts = orbitals // LANE
    return parts * parts * LANE + 16


def pairs_below(parts):
    return [(r, c) for r in range(parts) for c in range(r)]


def pair_slot(parts, r, c, half):
    return 2 * pairs_below(parts).index((r, c)) + half


def middle_slot(parts, r):
    return parts * (parts - 1) + r


def tile_indices():
    rows = lax.broadcasted_iota(jnp.int32, (LANE, LANE), 0)
    cols = lax.broadcasted_iota(jnp.int32, (LANE, LANE), 1)
    return rows, cols


def unpack_blocks(packed, put, parts):
    rows, cols = tile_indices()
    for r, c in pairs_below(parts):
        for half in range(2):
            block = packed[span(pair_slot(parts, r, c, half)), :]
            put(half, r, c, block)
            put(half, c, r, block.T)
    at = parts * parts * LANE
    for r in range(parts):
        block = packed[span(middle_slot(parts, r)), :]
        turned = block.T
        middle = packed[at : at + 16, :][r : r + 1, :]
        put(0, r, r, jnp.where(rows <= cols, block, turned))
        put(1, r, r, jnp.where(rows > cols, block, jnp.where(rows == cols, middle, turned)))


def pack_block(packed, r, c, green_real, green_imag, parts):
    rows, cols = tile_indices()
    if r == c:
        packed[span(middle_slot(parts, r)), :] = jnp.where(
            rows <= cols, green_real, green_imag
        ).astype(BF16)
    else:
        packed[span(pair_slot(parts, r, c, 0)), :] = green_real.astype(BF16)
        packed[span(pair_slot(parts, r, c, 1)), :] = green_imag.astype(BF16)


def pack_middles(packed, middles, parts):
    rest = jnp.zeros((16 - parts, LANE), F32)
    at = parts * parts * LANE
    packed[at : at + 16, :] = jnp.concatenate(middles + [rest], axis=0).astype(BF16)


def diagonal_row(block):
    rows, cols = tile_indices()
    return jnp.sum(jnp.where(rows == cols, block, 0.0), axis=0, keepdims=True)


def takes_first_levels():
    return lax.axis_index("kt") % 2 == 1


class Either:
    def __init__(self, refs):
        self.refs = refs
        self.shape = refs[0].shape

    def __getitem__(self, index):
        if len(self.refs) == 1:
            return self.refs[0][index]
        return jnp.where(takes_first_levels(), self.refs[1][index], self.refs[0][index])


def first_level_item(slot):
    return lax.axis_index("kt") - 1 + slot, jnp.int32(0)


def item_of(counts, slot):
    wanted = lax.axis_index("kt") + slot

    def one(k, state):
        momentum, before = state
        extra = counts[k, 0, 0] - 1
        take = jnp.logical_and(momentum == k, before + extra <= wanted)
        return (jnp.where(take, k + 1, momentum), jnp.where(take, before + extra, before))

    momentum, before = lax.fori_loop(0, counts.shape[0], one, (jnp.int32(0), jnp.int32(0)))
    momentum = jnp.minimum(momentum, counts.shape[0] - 1)
    level = jnp.clip(1 + wanted - before, 0, EMAX - 1)
    own_momentum, own_level = first_level_item(slot)
    own = takes_first_levels()
    return jnp.where(own, own_momentum, momentum), jnp.where(own, own_level, level)


def entry_amounts(constants, impulse_count, momentum, level):
    energy = bottom_sample_mark + sample_gap * level.astype(F32)
    return constants[momentum], energy, constants[impulse_count + level]


def inverse_diagonal(position, cosine, energy, contact, onsite, hopping, potential):
    slabs, orbitals = onsite.shape
    diag_real = energy + (-onsite[...] - potential[...]) - cosine * hopping[...]
    slab_in = lax.broadcasted_iota(jnp.int32, (slabs, orbitals), 0) + position * slabs
    at_contact = jnp.logical_or(slab_in == contact[0], slab_in == contact[1])
    diag_imag = broadening + contact_width * at_contact.astype(F32)
    magnitude = diag_real * diag_real + diag_imag * diag_imag
    inv_real = diag_real / magnitude
    inv_imag = -diag_imag / magnitude
    return inv_real, inv_imag


def local_rows(parts):
    return 2 * len(blocks_on_or_below(parts)) * LANE


def columns_of(inv_real, inv_imag):
    return jnp.concatenate([inv_real, inv_imag], axis=0).T


def store_left(left, piece, half, c, parts):
    last = (parts - 1) * LANE
    left[half * last : (half + 1) * last, span(c)] = piece[:last]
    bottom = 2 * last + half * LANE
    left[bottom : bottom + LANE, span(c)] = piece[last:]


def times_carried(coupled, g, left, parts):
    product = jnp.dot(coupled, g[...], preferred_element_type=F32)
    keep_product(product.astype(BF16), left, parts)


def keep_product(product, left, parts):
    for column in range(2 * parts):
        half, c = (
            (0, column)
            if column < parts
            else (1, parts - 1 if column == parts else column - parts - 1)
        )
        store_left(left, product[:, span(column)], half, c, parts)


def finish_slab(
    s, times_turned, left, g, packed, columns, real_row, imag_row, note, parts, local=None, offset=0
):
    last = (parts - 1) * LANE
    rows, cols = tile_indices()
    diagonal = rows == cols
    numbers = {block: k for k, block in enumerate(blocks_on_or_below(parts))}
    middles = {}

    def finish(r, c, sr, si):
        k = numbers[r, c]
        real_col, imag_col = columns[0][span(r)], columns[1][span(r)]
        half_real = real_col * sr - imag_col * si
        half_imag = real_col * si + imag_col * sr
        rr, ri = real_row[:, span(c)], imag_row[:, span(c)]
        green_real = half_real * rr - half_imag * ri
        green_imag = half_real * ri + half_imag * rr
        if r == c:
            green_real = green_real + jnp.where(diagonal, real_row[:, span(c)], 0.0)
            green_imag = green_imag + jnp.where(diagonal, imag_row[:, span(c)], 0.0)
            if note is not None:
                middles[r] = diagonal_row(green_imag)
                note(r, middles[r])
        if packed is not None:
            pack_block(packed, r, c, green_real, green_imag, parts)
        if local is not None:
            local[span(2 * k), :] = green_real
            local[span(2 * k + 1), :] = green_imag
        if g is None:
            return
        for half, green in ((0, green_real), (1, green_imag)):
            rounded = green.astype(BF16)
            g[span(r), span(offset + place(parts, half, c))] = rounded
            if r != c:
                g[span(c), span(offset + place(parts, half, r))] = rounded.T

    turned = times_turned(left[...])
    far = turned[2 * last :, :]
    near = turned[: 2 * last, :]
    for c in range(parts):
        finish(parts - 1, c, far[:LANE, span(c)], far[LANE:, span(c)])
    for r in range(parts - 1):
        for c in range(r + 1):
            finish(r, c, near[span(r), span(c)], near[last:, :][span(r), span(c)])
    if packed is not None:
        pack_middles(packed, [middles[r] for r in range(parts)], parts)


def coupling_of(base, wave, cosine):
    return (base.astype(F32) + cosine * wave.astype(F32)).astype(BF16)


def first_segment(
    coupled_of, inv_real, inv_imag, weight, g, left, sent, density, local=None
):
    slabs, orbitals = inv_real.shape
    parts = orbitals // LANE
    down = columns_of(inv_real, inv_imag)
    if density is not None:
        density[0:1, :] += -weight * inv_imag[0:1, :]
    for s in range(1, slabs):
        coupled = coupled_of(s)
        if s == 1:
            wide = coupled.astype(F32)
            for half, inv in ((0, inv_real), (1, inv_imag)):
                piece = (wide * inv[0:1, :].astype(BF16).astype(F32)).astype(BF16)
                for c in range(parts):
                    store_left(left, piece[:, span(c)], half, c, parts)
        else:
            times_carried(coupled, g, left, parts)

        def times_turned(rows):
            return lax.dot_general(
                rows, coupled, (((1,), (1,)), ((), ())), preferred_element_type=F32
            )

        def note(r, middle):
            density[s : s + 1, span(r)] += -weight * middle

        final = s == slabs - 1
        finish_slab(
            s, times_turned, left, None if final else g, sent if final else None,
            (down[:, s : s + 1], down[:, slabs + s : slabs + s + 1]),
            inv_real[s : s + 1, :], inv_imag[s : s + 1, :],
            None if density is None else note, parts, local if final else None,
        )


def copies_of_constants(constants_hbm, contact_hbm, constants, contact, sem):
    return [
        pltpu.make_async_copy(constants_hbm, constants, sem.at[0]),
        pltpu.make_async_copy(contact_hbm, contact, sem.at[1]),
    ]


def copies_of_couplings(base_hbm, wave_hbm, base, wave, sem, slabs_wanted):
    return {
        s: (
            pltpu.make_async_copy(base_hbm.at[s], base.at[s], sem.at[0, s]),
            pltpu.make_async_copy(wave_hbm.at[s], wave.at[s], sem.at[1, s]),
        )
        for s in slabs_wanted
    }


def lead_kernel(
    impulse_count,
    constants_hbm, contact_hbm, onsite_hbm, hopping_hbm, potential_hbm, base_hbm, wave_hbm,
    sent, density, base, wave,
    constants, contact, tables, g, left, small_sem, table_sem, couple_sem,
):
    slabs, orbitals = onsite_hbm.shape
    parts = orbitals // LANE
    position = lax.axis_index("en")
    density[...] = jnp.zeros_like(density)
    small_copies = copies_of_constants(
        constants_hbm, contact_hbm, constants, contact, small_sem
    ) + [
        pltpu.make_async_copy(source, tables.at[k], table_sem.at[k])
        for k, source in enumerate((onsite_hbm, hopping_hbm, potential_hbm))
    ]
    for copy in small_copies:
        copy.start()

    def first_level_amounts():
        momentum, level = first_level_item(0)
        cosine, energy, weight = entry_amounts(constants, impulse_count, momentum, level)
        inv_real, inv_imag = inverse_diagonal(
            position, cosine, energy, contact, tables.at[0], tables.at[1], tables.at[2]
        )
        return cosine, weight, inv_real, inv_imag

    @pl.when(position == 0)
    def _():
        couple_copies = copies_of_couplings(
            base_hbm, wave_hbm, base, wave, couple_sem, range(1, slabs)
        )
        for s in couple_copies:
            for copy in couple_copies[s]:
                copy.start()
        for copy in small_copies:
            copy.wait()

        @pl.when(takes_first_levels())
        def _():
            cosine, weight, inv_real, inv_imag = first_level_amounts()

            def coupled_of(s):
                for copy in couple_copies[s]:
                    copy.wait()
                return coupling_of(base[s], wave[s], cosine)

            first_segment(
                coupled_of, inv_real, inv_imag, weight, g, left, sent, density
            )

        @pl.when(jnp.logical_not(takes_first_levels()))
        def _():
            for s in couple_copies:
                for copy in couple_copies[s]:
                    copy.wait()


    @pl.when(position > 0)
    def _():
        couple_copies = copies_of_couplings(
            base_hbm, wave_hbm, base, wave, couple_sem, range(slabs)
        )
        for s in couple_copies:
            for copy in couple_copies[s]:
                copy.start()
        for copy in small_copies:
            copy.wait()
        for s in couple_copies:
            for copy in couple_copies[s]:
                copy.wait()


def with_scalars(refs, scratch, sem):
    copies = [
        pltpu.make_async_copy(source, target, sem.at[k])
        for k, (source, target) in enumerate(zip(refs, scratch))
    ]
    for copy in copies:
        copy.start()
    for copy in copies:
        copy.wait()


def begin_kernel(
    impulse_count, slot,
    constants_ref, contact_ref, counts_ref,
    onsite, hopping, potential, base, wave, so_far, *refs,
):
    held, refs = refs[:-8], refs[-8:]
    density, sent, constants, contact, counts, scalar_sem, g, left = refs
    slabs, orbitals = onsite.shape
    parts = orbitals // LANE
    position = lax.axis_index("en")
    density[...] = so_far[...]
    active = position == 0
    if slot == 0:

        @pl.when(jnp.logical_and(active, takes_first_levels()))
        def _():
            sent[...] = held[0][...]

        active = jnp.logical_and(active, jnp.logical_not(takes_first_levels()))

    @pl.when(active)
    def _():
        with_scalars(
            (constants_ref, contact_ref, counts_ref), (constants, contact, counts), scalar_sem
        )
        momentum, level = item_of(counts, slot)
        cosine, energy, weight = entry_amounts(constants, impulse_count, momentum, level)
        inv_real, inv_imag = inverse_diagonal(
            position, cosine, energy, contact, onsite, hopping, potential
        )

        def coupled_of(s):
            return coupling_of(base[s], wave[s], cosine)

        first_segment(coupled_of, inv_real, inv_imag, weight, g, left, sent, density)


def prepare(cosine, weight, inv_real, inv_imag, base, wave, couple, entry):
    slabs, orbitals = inv_real.shape
    parts = orbitals // LANE
    for s in range(slabs):
        entry[s] = jnp.broadcast_to(inv_real[s : s + 1, :], entry.shape[1:])
        entry[slabs + s] = jnp.broadcast_to(inv_imag[s : s + 1, :], entry.shape[1:])
    entry[2 * slabs] = jnp.full(entry.shape[1:], weight, F32)

    def one(s, carry):
        couple[s] = coupling_of(base[s], wave[s], cosine)
        return carry

    lax.fori_loop(0, slabs, one, 0)


def prepare_kernel(
    impulse_count,
    constants_ref, contact_ref, counts_ref, onsite, hopping, potential, base, wave,
    couple_0, entry_0,
    couple_1, entry_1,
    constants, contact, counts, scalar_sem,
):
    position = lax.axis_index("en")

    def prepare_slot(slot, made):
        momentum, level = item_of(counts, slot)
        cosine, energy, weight = entry_amounts(constants, impulse_count, momentum, level)
        inv_real, inv_imag = inverse_diagonal(
            position, cosine, energy, contact, onsite, hopping, potential
        )
        prepare(cosine, weight, inv_real, inv_imag, base, wave, *made)

    @pl.when(position > 0)
    def _():
        with_scalars(
            (constants_ref, contact_ref, counts_ref), (constants, contact, counts), scalar_sem
        )
        prepare_slot(0, (couple_0, entry_0))
        prepare_slot(1, (couple_1, entry_1))


def rows_of_entry(entry, slabs):
    inv_real = jnp.concatenate([entry[s, 0:1, :] for s in range(slabs)], axis=0)
    inv_imag = jnp.concatenate([entry[slabs + s, 0:1, :] for s in range(slabs)], axis=0)
    return inv_real, inv_imag, entry[2 * slabs, 0:1, 0:1]


def operator_kernel(couple, entry, carriers, cross, local, densities, both, left):
    slabs, orbitals, _ = couple.shape
    parts = orbitals // LANE

    @pl.when(lax.axis_index("en") > 0)
    def _():
        inv_real, inv_imag, weight = rows_of_entry(entry, slabs)
        down = columns_of(inv_real, inv_imag)
        for s in range(slabs):
            coupled = couple[s]
            real_col = down[:, s : s + 1]
            imag_col = down[:, slabs + s : slabs + s + 1]
            real_row, imag_row = inv_real[s : s + 1, :], inv_imag[s : s + 1, :]
            if s == 0:
                wide = coupled.astype(F32)
                real, imag = real_col * wide, imag_col * wide
                densities[0:1, :] = -weight * imag_row
            else:
                width = 2 * orbitals if s == 1 else 4 * orbitals
                product = jnp.dot(coupled, both[:, :width], preferred_element_type=F32)
                from_real, from_imag = product[:, :orbitals], product[:, orbitals : 2 * orbitals]
                real = real_col * from_real - imag_col * from_imag
                imag = real_col * from_imag + imag_col * from_real
                if s == 1:
                    wide = coupled.astype(F32)
                    for half, inv in ((0, inv_real), (1, inv_imag)):
                        piece = (wide * inv[0:1, :].astype(BF16).astype(F32)).astype(BF16)
                        for c in range(parts):
                            store_left(left, piece[:, span(c)], half, c, parts)
                else:
                    keep_product(product[:, 2 * orbitals :].astype(BF16), left, parts)
            real, imag = real.astype(BF16), imag.astype(BF16)
            here = slice(s * orbitals, (s + 1) * orbitals)
            carriers[here, :orbitals] = real
            carriers[here, orbitals:] = imag
            if s < slabs - 1:
                both[:, :orbitals] = real
                both[:, orbitals : 2 * orbitals] = imag
            if s == 0:
                continue

            def times_turned(rows):
                return lax.dot_general(
                    rows, coupled, (((1,), (1,)), ((), ())), preferred_element_type=F32
                )

            def note(r, middle):
                densities[s : s + 1, span(r)] = -weight * middle

            final = s == slabs - 1
            finish_slab(
                s, times_turned, left, None if final else both, None,
                (real_col, imag_col), real_row, imag_row, note, parts,
                local if final else None, 2 * parts,
            )
        top = (slabs - 1) * parts
        for r in range(parts):
            for c in range(parts):
                real = carriers[span(top + r), span(c)].T
                imag = carriers[span(top + r), span(parts + c)].T
                cross[span(c), span(r)] = real
                cross[span(parts + c), span(parts + r)] = real
                cross[span(c), span(parts + r)] = imag
                cross[span(parts + c), span(r)] = -imag


def pass_kernel(stage, calls, *refs):
    local = Either(refs[:calls])
    carriers, cross, arrived, sent, wide, half_way = refs[calls:]
    orbitals = carriers.shape[1] // 2
    parts = orbitals // LANE

    @pl.when(lax.axis_index("en") == stage)
    def _():
        def put(half, r, c, block):
            if half == 0:
                wide[span(r), span(c)] = block
                wide[span(parts + r), span(parts + c)] = block
            else:
                wide[span(r), span(parts + c)] = block
                wide[span(parts + r), span(c)] = -block

        unpack_blocks(arrived, put, parts)
        half_way[...] = jnp.dot(
            carriers[carriers.shape[0] - orbitals :, :], wide[...], preferred_element_type=F32
        ).astype(BF16)
        out = jnp.dot(half_way[...], cross[...], preferred_element_type=F32)
        middles = []
        for k, (r, c) in enumerate(blocks_on_or_below(parts)):
            green_real = local[span(2 * k), :] + out[span(r), span(c)]
            green_imag = local[span(2 * k + 1), :] + out[span(r), span(parts + c)]
            pack_block(sent, r, c, green_real, green_imag, parts)
            if r == c:
                middles.append(diagonal_row(green_imag))
        pack_middles(sent, middles, parts)


def density_kernel(calls, carriers, *refs):
    entry, refs = Either(refs[: calls[0]]), refs[calls[0] :]
    local_densities, refs = Either(refs[: calls[1]]), refs[calls[1] :]
    so_far, arrived, (density, wide, total) = refs[0], refs[1:-3], refs[-3:]
    slabs, orbitals = so_far.shape
    parts = orbitals // LANE
    position = lax.axis_index("en")
    density[...] = so_far[...]

    def put(half, r, c, block):
        if half == 0:
            wide[span(r), span(2 * c)] = block
            wide[span(parts + r), span(2 * c + 1)] = block
        else:
            wide[span(r), span(2 * c + 1)] = block
            wide[span(parts + r), span(2 * c)] = -block

    for stage, block in enumerate(arrived, 1):

        @pl.when(position == stage)
        def _():
            unpack_blocks(block, put, parts)

    @pl.when(position > 0)
    def _():
        for c in range(parts):
            product = jnp.dot(
                carriers[...],
                wide[:, 2 * c * LANE : 2 * (c + 1) * LANE],
                preferred_element_type=F32,
            )
            term = product[:, :LANE] * carriers[:, span(parts + c)].astype(F32) + product[
                :, LANE:
            ] * carriers[:, span(c)].astype(F32)
            if c == 0:
                total[...] = term
            else:
                total[...] += term
        weight = entry[2 * slabs, 0:1, :LANE]
        for s in range(slabs):
            for r in range(parts):
                row = jnp.sum(total[span(s * parts + r), :].T, axis=0, keepdims=True)
                density[s : s + 1, span(r)] += (
                    local_densities[s : s + 1, span(r)] - weight * row
                )


def vmem_call(kernel, outs, operands, in_specs, scratch, name, flops, traffic=2**21, **more):
    vmem = pl.BlockSpec(memory_space=pltpu.VMEM)
    return pl.pallas_call(
        kernel,
        out_shape=tuple(outs),
        in_specs=in_specs,
        out_specs=(vmem,) * len(outs),
        scratch_shapes=scratch,
        compiler_params=pltpu.CompilerParams(vmem_limit_bytes=16 * 2**20),
        cost_estimate=pl.CostEstimate(flops=flops, bytes_accessed=traffic, transcendentals=0),
        name=name,
        **more,
    )(*operands)


def split_kernel(inverse, high, middle, low):
    for r in range(inverse.shape[0] // LANE):
        for c in range(inverse.shape[1] // LANE):
            block = inverse[span(r), span(c)].T
            for part in (high, middle, low):
                rounded = block.astype(BF16)
                part[span(c), span(r)] = rounded
                block = block - rounded.astype(F32)


def last_kernel(gathered, doping, high, middle, low, summed, potential):
    total = jnp.sum(gathered[...], axis=0)
    summed[...] = total
    rest = total - doping[...]
    pieces = []
    for _ in range(3):
        pieces.append(rest.astype(BF16).astype(F32))
        rest = rest - pieces[-1]
    rows = total.shape[0]
    answer = jnp.zeros_like(total)
    for count, part in ((1, low), (2, middle), (3, high)):
        padded = -(-3 * rows // 16) * 16 - count * rows
        stacked = jnp.concatenate(
            pieces[:count] + [jnp.zeros((padded, total.shape[1]), F32)], axis=0
        ).astype(BF16)
        product = jnp.dot(stacked, part[...], preferred_element_type=F32)
        for k in reversed(range(count)):
            answer = answer + product[k * rows : (k + 1) * rows]
    potential[...] = answer


def gather_over(values, axis):
    copies = jnp.broadcast_to(values[None], (lax.axis_size(axis),) + values.shape)
    return lax.all_to_all(copies, axis, 0, 0)


def body(
    counts,
    contact_slabs,
    onsite,
    hopping,
    potential_in,
    couple_base,
    couple_wave,
    doping,
    poisson_inverse,
):
    kt_size = lax.axis_size("kt")
    en_size = lax.axis_size("en")
    slabs, orbitals = onsite.shape
    parts = orbitals // LANE
    impulse_count = counts.shape[0] * kt_size
    constants = jnp.asarray(item_constants(impulse_count))
    smem = pl.BlockSpec(memory_space=pltpu.SMEM)
    hbm = pl.BlockSpec(memory_space=pltpu.HBM)
    vmem = pl.BlockSpec(memory_space=pltpu.VMEM)
    flops = 2 * slabs * orbitals**3

    def forward(block, stage):
        return lax.ppermute(block, "en", [(stage, stage + 1)])

    block_shape = jax.ShapeDtypeStruct((packed_rows(orbitals), LANE), BF16)
    density_shape = jax.ShapeDtypeStruct((slabs, orbitals), F32)
    couple_shape = jax.ShapeDtypeStruct((slabs, orbitals, orbitals), BF16)
    entry_shape = jax.ShapeDtypeStruct((2 * slabs + 1, 8, orbitals), F32)
    work = [
        pltpu.VMEM((orbitals, 2 * orbitals), BF16),
        pltpu.VMEM((2 * orbitals, orbitals), BF16),
    ]

    counts_all = gather_over(
        jnp.broadcast_to(counts[:, None], (counts.shape[0], 128)), "kt"
    )
    given = (constants, contact_slabs, onsite, hopping, potential_in, couple_base, couple_wave)
    pinned = [pltpu.with_memory_space_constraint(t, pltpu.HBM) for t in given]
    block, density, *loaded = vmem_call(
        functools.partial(lead_kernel, impulse_count),
        (block_shape, density_shape, couple_shape, couple_shape),
        pinned,
        [hbm] * len(pinned),
        [
            pltpu.SMEM(constants.shape, F32),
            pltpu.SMEM(contact_slabs.shape, jnp.int32),
            pltpu.VMEM((3, slabs, orbitals), F32),
        ]
        + work
        + [
            pltpu.SemaphoreType.DMA((2,)),
            pltpu.SemaphoreType.DMA((3,)),
            pltpu.SemaphoreType.DMA((2, slabs)),
        ],
        "lead",
        3 * flops,
    )
    block, counts_all = lax.optimization_barrier((block, counts_all))
    small = (constants, contact_slabs, counts_all, onsite, hopping, potential_in)

    anywhere = pl.BlockSpec(memory_space=pl.ANY)
    scalar_scratch = [
        pltpu.SMEM(constants.shape, F32),
        pltpu.SMEM(contact_slabs.shape, jnp.int32),
        pltpu.SMEM(counts_all.shape, jnp.int32),
        pltpu.SemaphoreType.DMA((3,)),
    ]

    def begin(slot, density, *held):
        return vmem_call(
            functools.partial(begin_kernel, impulse_count, slot),
            (density_shape, block_shape),
            (*small, *loaded, density, *held),
            [anywhere] * 3 + [vmem] * (6 + len(held)),
            scalar_scratch + work,
            f"begin_{slot}",
            3 * flops,
            input_output_aliases={8: 0, 9: 1} if held else {8: 0},
        )

    density, block = begin(0, density, block)
    arrived = [forward(block, 0)]
    density, block = begin(1, density)
    arrived.append(forward(block, 0))
    small, _ = lax.optimization_barrier((small, block))
    made = vmem_call(
        functools.partial(prepare_kernel, impulse_count),
        (couple_shape, entry_shape) * 2,
        (*small, *loaded),
        [anywhere] * 3 + [vmem] * 5,
        scalar_scratch,
        "prepare",
        flops // 16,
        2**16,
    )
    made = [[(one,) for one in made[:2]], [(one,) for one in made[2:]]]

    carriers_shape = jax.ShapeDtypeStruct((slabs * orbitals, 2 * orbitals), BF16)
    double_shape = jax.ShapeDtypeStruct((2 * orbitals, 2 * orbitals), BF16)

    def operator_of(slot):
        (couple,), (entry,) = made[slot]
        results = vmem_call(
            operator_kernel,
            (
                carriers_shape,
                double_shape,
                jax.ShapeDtypeStruct((local_rows(parts), LANE), F32),
                density_shape,
            ),
            (couple, entry),
            [vmem] * 2,
            [
                pltpu.VMEM((orbitals, 4 * orbitals), BF16),
                pltpu.VMEM((2 * orbitals, orbitals), BF16),
            ],
            f"operator_{slot}",
            flops // 16,
            2**16,
        )
        carried.append(results[:2])
        local.append([results[2:]])

    def pass_on(stage, slot, block):
        calls = [one[0] for one in local[slot]]
        return vmem_call(
            functools.partial(pass_kernel, stage, len(calls)),
            (block_shape,),
            (*calls, *carried[slot], block),
            [vmem] * (3 + len(calls)),
            [
                pltpu.VMEM(double_shape.shape, BF16),
                pltpu.VMEM((orbitals, 2 * orbitals), BF16),
            ],
            f"pass_{stage}_{slot}",
            2 * flops,
        )[0]

    def densities(slot, density, came):
        entry = made[slot][1]
        calls = [one[1] for one in local[slot]]
        before = 1 + len(entry) + len(calls)
        return vmem_call(
            functools.partial(density_kernel, (len(entry), len(calls))),
            (density_shape,),
            (carried[slot][0], *entry, *calls, density, *came),
            [vmem] * (before + 1 + len(came)),
            [
                pltpu.VMEM(double_shape.shape, BF16),
                pltpu.VMEM((slabs * orbitals, LANE), F32),
            ],
            f"density_{slot}",
            4 * flops,
            input_output_aliases={before: 0},
        )[0]

    came = [[arrived[0]], [arrived[1]]]
    carried, local = [], []
    operator_of(0)
    for stage in range(1, en_size - 1):
        for slot in range(2):
            if stage == 1 and slot == 1:
                made[1], _ = lax.optimization_barrier((made[1], block))
                operator_of(1)
            block = pass_on(stage, slot, came[slot][-1])
            came[slot].append(forward(block, stage))
    for slot in range(2):
        density = densities(slot, density, came[slot])
    part_shape = jax.ShapeDtypeStruct(poisson_inverse.shape, BF16)
    inverse, _ = lax.optimization_barrier((poisson_inverse, block))
    split = vmem_call(
        split_kernel, (part_shape,) * 3, (inverse,), [vmem], [], "split_inverse", 2 * flops
    )
    density, *split = lax.optimization_barrier((density, *split))
    return vmem_call(
        last_kernel,
        (density_shape, density_shape),
        (gather_over(density, "kt"), doping, *split),
        [vmem] * 5,
        [],
        "last",
        flops // slabs,
    )


def solution(mesh):
    return jax.shard_map(
        body,
        mesh=mesh,
        in_specs=(
            P("kt"),
            P(),
            P("en", None),
            P("en", None),
            P("en", None),
            P("en", None, None),
            P("en", None, None),
            P("en", None),
            P(),
        ),
        out_specs=(P("en", None), P("en", None)),
        check_vma=False,
    )
```

```python
import functools

import jax
import jax.numpy as jnp
import numpy as np
from jax import lax
from jax.experimental import pallas as pl
from jax.experimental.pallas import tpu as pltpu
from jax.sharding import PartitionSpec as P

EMAX = 4
LANE = 128
F32 = jnp.float32
BF16 = jnp.bfloat16

bottom_sample_mark = -1.0
sample_gap = 0.25
electrode_filling = -0.5
boltzmann_spread = 0.1
broadening = 1.0
contact_width = 0.5


def item_constants(impulse_count):
    wave = np.float32(np.pi) * (np.arange(impulse_count, dtype=np.float32) + np.float32(0.5))
    cosine = np.cos(wave / np.float32(impulse_count))
    energy = bottom_sample_mark + sample_gap * np.arange(EMAX)
    weight = sample_gap / (1.0 + np.exp((energy - electrode_filling) / boltzmann_spread)) / np.pi
    return np.concatenate([cosine, weight]).astype(np.float32)


def span(k):
    return slice(k * LANE, (k + 1) * LANE)


def place(parts, half, c):
    if c == parts - 1:
        return parts - 1 + half
    return c if half == 0 else parts + 1 + c


def blocks_on_or_below(parts):
    return [(r, c) for r in range(parts) for c in range(r + 1)]


def packed_rows(orbitals):
    parts = orbitals // LANE
    return parts * parts * LANE + 16


def pairs_below(parts):
    return [(r, c) for r in range(parts) for c in range(r)]


def pair_slot(parts, r, c, half):
    return 2 * pairs_below(parts).index((r, c)) + half


def middle_slot(parts, r):
    return parts * (parts - 1) + r


def tile_indices():
    rows = lax.broadcasted_iota(jnp.int32, (LANE, LANE), 0)
    cols = lax.broadcasted_iota(jnp.int32, (LANE, LANE), 1)
    return rows, cols


def unpack_blocks(packed, put, parts):
    rows, cols = tile_indices()
    for r, c in pairs_below(parts):
        for half in range(2):
            block = packed[span(pair_slot(parts, r, c, half)), :]
            put(half, r, c, block)
            put(half, c, r, block.T)
    at = parts * parts * LANE
    for r in range(parts):
        block = packed[span(middle_slot(parts, r)), :]
        turned = block.T
        middle = packed[at : at + 16, :][r : r + 1, :]
        put(0, r, r, jnp.where(rows <= cols, block, turned))
        put(1, r, r, jnp.where(rows > cols, block, jnp.where(rows == cols, middle, turned)))


def pack_block(packed, r, c, green_real, green_imag, parts):
    rows, cols = tile_indices()
    if r == c:
        packed[span(middle_slot(parts, r)), :] = jnp.where(
            rows <= cols, green_real, green_imag
        ).astype(BF16)
    else:
        packed[span(pair_slot(parts, r, c, 0)), :] = green_real.astype(BF16)
        packed[span(pair_slot(parts, r, c, 1)), :] = green_imag.astype(BF16)


def pack_middles(packed, middles, parts):
    rest = jnp.zeros((16 - parts, LANE), F32)
    at = parts * parts * LANE
    packed[at : at + 16, :] = jnp.concatenate(middles + [rest], axis=0).astype(BF16)


def diagonal_row(block):
    rows, cols = tile_indices()
    return jnp.sum(jnp.where(rows == cols, block, 0.0), axis=0, keepdims=True)


def takes_first_levels():
    return lax.axis_index("kt") % 2 == 1


class Either:
    def __init__(self, refs):
        self.refs = refs
        self.shape = refs[0].shape

    def __getitem__(self, index):
        if len(self.refs) == 1:
            return self.refs[0][index]
        return jnp.where(takes_first_levels(), self.refs[1][index], self.refs[0][index])


def first_level_item(slot):
    return lax.axis_index("kt") - 1 + slot, jnp.int32(0)


def item_of(counts, slot):
    wanted = lax.axis_index("kt") + slot

    def one(k, state):
        momentum, before = state
        extra = counts[k, 0, 0] - 1
        take = jnp.logical_and(momentum == k, before + extra <= wanted)
        return (jnp.where(take, k + 1, momentum), jnp.where(take, before + extra, before))

    momentum, before = lax.fori_loop(0, counts.shape[0], one, (jnp.int32(0), jnp.int32(0)))
    momentum = jnp.minimum(momentum, counts.shape[0] - 1)
    level = jnp.clip(1 + wanted - before, 0, EMAX - 1)
    own_momentum, own_level = first_level_item(slot)
    own = takes_first_levels()
    return jnp.where(own, own_momentum, momentum), jnp.where(own, own_level, level)


def entry_amounts(constants, impulse_count, momentum, level):
    energy = bottom_sample_mark + sample_gap * level.astype(F32)
    return constants[momentum], energy, constants[impulse_count + level]


def inverse_diagonal(position, cosine, energy, contact, onsite, hopping, potential):
    slabs, orbitals = onsite.shape
    diag_real = energy + (-onsite[...] - potential[...]) - cosine * hopping[...]
    slab_in = lax.broadcasted_iota(jnp.int32, (slabs, orbitals), 0) + position * slabs
    at_contact = jnp.logical_or(slab_in == contact[0], slab_in == contact[1])
    diag_imag = broadening + contact_width * at_contact.astype(F32)
    magnitude = diag_real * diag_real + diag_imag * diag_imag
    inv_real = diag_real / magnitude
    inv_imag = -diag_imag / magnitude
    return inv_real, inv_imag


def local_rows(parts):
    return 2 * len(blocks_on_or_below(parts)) * LANE


def columns_of(inv_real, inv_imag):
    return jnp.concatenate([inv_real, inv_imag], axis=0).T


def store_left(left, piece, half, c, parts):
    last = (parts - 1) * LANE
    left[half * last : (half + 1) * last, span(c)] = piece[:last]
    bottom = 2 * last + half * LANE
    left[bottom : bottom + LANE, span(c)] = piece[last:]


def times_carried(coupled, g, left, parts):
    product = jnp.dot(coupled, g[...], preferred_element_type=F32)
    keep_product(product.astype(BF16), left, parts)


def keep_product(product, left, parts):
    for column in range(2 * parts):
        half, c = (
            (0, column)
            if column < parts
            else (1, parts - 1 if column == parts else column - parts - 1)
        )
        store_left(left, product[:, span(column)], half, c, parts)


def finish_slab(
    s, times_turned, left, g, packed, columns, real_row, imag_row, note, parts, local=None, offset=0
):
    last = (parts - 1) * LANE
    rows, cols = tile_indices()
    diagonal = rows == cols
    numbers = {block: k for k, block in enumerate(blocks_on_or_below(parts))}
    middles = {}

    def finish(r, c, sr, si):
        k = numbers[r, c]
        real_col, imag_col = columns[0][span(r)], columns[1][span(r)]
        half_real = real_col * sr - imag_col * si
        half_imag = real_col * si + imag_col * sr
        rr, ri = real_row[:, span(c)], imag_row[:, span(c)]
        green_real = half_real * rr - half_imag * ri
        green_imag = half_real * ri + half_imag * rr
        if r == c:
            green_real = green_real + jnp.where(diagonal, real_row[:, span(c)], 0.0)
            green_imag = green_imag + jnp.where(diagonal, imag_row[:, span(c)], 0.0)
            if note is not None:
                middles[r] = diagonal_row(green_imag)
                note(r, middles[r])
        if packed is not None:
            pack_block(packed, r, c, green_real, green_imag, parts)
        if local is not None:
            local[span(2 * k), :] = green_real
            local[span(2 * k + 1), :] = green_imag
        if g is None:
            return
        for half, green in ((0, green_real), (1, green_imag)):
            rounded = green.astype(BF16)
            g[span(r), span(offset + place(parts, half, c))] = rounded
            if r != c:
                g[span(c), span(offset + place(parts, half, r))] = rounded.T

    turned = times_turned(left[...])
    far = turned[2 * last :, :]
    near = turned[: 2 * last, :]
    for c in range(parts):
        finish(parts - 1, c, far[:LANE, span(c)], far[LANE:, span(c)])
    for r in range(parts - 1):
        for c in range(r + 1):
            finish(r, c, near[span(r), span(c)], near[last:, :][span(r), span(c)])
    if packed is not None:
        pack_middles(packed, [middles[r] for r in range(parts)], parts)


def coupling_of(base, wave, cosine):
    return (base.astype(F32) + cosine * wave.astype(F32)).astype(BF16)


def first_segment(
    coupled_of, inv_real, inv_imag, weight, g, left, sent, density, local=None
):
    slabs, orbitals = inv_real.shape
    parts = orbitals // LANE
    down = columns_of(inv_real, inv_imag)
    if density is not None:
        density[0:1, :] += -weight * inv_imag[0:1, :]
    for s in range(1, slabs):
        coupled = coupled_of(s)
        if s == 1:
            wide = coupled.astype(F32)
            for half, inv in ((0, inv_real), (1, inv_imag)):
                piece = (wide * inv[0:1, :].astype(BF16).astype(F32)).astype(BF16)
                for c in range(parts):
                    store_left(left, piece[:, span(c)], half, c, parts)
        else:
            times_carried(coupled, g, left, parts)

        def times_turned(rows):
            return lax.dot_general(
                rows, coupled, (((1,), (1,)), ((), ())), preferred_element_type=F32
            )

        def note(r, middle):
            density[s : s + 1, span(r)] += -weight * middle

        final = s == slabs - 1
        finish_slab(
            s, times_turned, left, None if final else g, sent if final else None,
            (down[:, s : s + 1], down[:, slabs + s : slabs + s + 1]),
            inv_real[s : s + 1, :], inv_imag[s : s + 1, :],
            None if density is None else note, parts, local if final else None,
        )


def copies_of_constants(constants_hbm, contact_hbm, constants, contact, sem):
    return [
        pltpu.make_async_copy(constants_hbm, constants, sem.at[0]),
        pltpu.make_async_copy(contact_hbm, contact, sem.at[1]),
    ]


def copies_of_couplings(base_hbm, wave_hbm, base, wave, sem, slabs_wanted):
    return {
        s: (
            pltpu.make_async_copy(base_hbm.at[s], base.at[s], sem.at[0, s]),
            pltpu.make_async_copy(wave_hbm.at[s], wave.at[s], sem.at[1, s]),
        )
        for s in slabs_wanted
    }


def lead_kernel(
    impulse_count,
    constants_hbm, contact_hbm, onsite_hbm, hopping_hbm, potential_hbm, base_hbm, wave_hbm,
    sent, density, base, wave,
    constants, contact, tables, g, left, small_sem, table_sem, couple_sem,
):
    slabs, orbitals = onsite_hbm.shape
    parts = orbitals // LANE
    position = lax.axis_index("en")
    density[...] = jnp.zeros_like(density)
    small_copies = copies_of_constants(
        constants_hbm, contact_hbm, constants, contact, small_sem
    ) + [
        pltpu.make_async_copy(source, tables.at[k], table_sem.at[k])
        for k, source in enumerate((onsite_hbm, hopping_hbm, potential_hbm))
    ]
    for copy in small_copies:
        copy.start()

    def first_level_amounts():
        momentum, level = first_level_item(0)
        cosine, energy, weight = entry_amounts(constants, impulse_count, momentum, level)
        inv_real, inv_imag = inverse_diagonal(
            position, cosine, energy, contact, tables.at[0], tables.at[1], tables.at[2]
        )
        return cosine, weight, inv_real, inv_imag

    @pl.when(position == 0)
    def _():
        couple_copies = copies_of_couplings(
            base_hbm, wave_hbm, base, wave, couple_sem, range(1, slabs)
        )
        for s in couple_copies:
            for copy in couple_copies[s]:
                copy.start()
        for copy in small_copies:
            copy.wait()

        @pl.when(takes_first_levels())
        def _():
            cosine, weight, inv_real, inv_imag = first_level_amounts()

            def coupled_of(s):
                for copy in couple_copies[s]:
                    copy.wait()
                return coupling_of(base[s], wave[s], cosine)

            first_segment(
                coupled_of, inv_real, inv_imag, weight, g, left, sent, density
            )

        @pl.when(jnp.logical_not(takes_first_levels()))
        def _():
            for s in couple_copies:
                for copy in couple_copies[s]:
                    copy.wait()


    @pl.when(position > 0)
    def _():
        couple_copies = copies_of_couplings(
            base_hbm, wave_hbm, base, wave, couple_sem, range(slabs)
        )
        for s in couple_copies:
            for copy in couple_copies[s]:
                copy.start()
        for copy in small_copies:
            copy.wait()
        for s in couple_copies:
            for copy in couple_copies[s]:
                copy.wait()


def with_scalars(refs, scratch, sem):
    copies = [
        pltpu.make_async_copy(source, target, sem.at[k])
        for k, (source, target) in enumerate(zip(refs, scratch))
    ]
    for copy in copies:
        copy.start()
    for copy in copies:
        copy.wait()


def begin_kernel(
    impulse_count, slot,
    constants_ref, contact_ref, counts_ref,
    onsite, hopping, potential, base, wave, so_far, *refs,
):
    held, refs = refs[:-8], refs[-8:]
    density, sent, constants, contact, counts, scalar_sem, g, left = refs
    slabs, orbitals = onsite.shape
    parts = orbitals // LANE
    position = lax.axis_index("en")
    density[...] = so_far[...]
    active = position == 0
    if slot == 0:

        @pl.when(jnp.logical_and(active, takes_first_levels()))
        def _():
            sent[...] = held[0][...]

        active = jnp.logical_and(active, jnp.logical_not(takes_first_levels()))

    @pl.when(active)
    def _():
        with_scalars(
            (constants_ref, contact_ref, counts_ref), (constants, contact, counts), scalar_sem
        )
        momentum, level = item_of(counts, slot)
        cosine, energy, weight = entry_amounts(constants, impulse_count, momentum, level)
        inv_real, inv_imag = inverse_diagonal(
            position, cosine, energy, contact, onsite, hopping, potential
        )

        def coupled_of(s):
            return coupling_of(base[s], wave[s], cosine)

        first_segment(coupled_of, inv_real, inv_imag, weight, g, left, sent, density)


def prepare(cosine, weight, inv_real, inv_imag, base, wave, couple, entry):
    slabs, orbitals = inv_real.shape
    parts = orbitals // LANE
    for s in range(slabs):
        entry[s] = jnp.broadcast_to(inv_real[s : s + 1, :], entry.shape[1:])
        entry[slabs + s] = jnp.broadcast_to(inv_imag[s : s + 1, :], entry.shape[1:])
    entry[2 * slabs] = jnp.full(entry.shape[1:], weight, F32)

    def one(s, carry):
        couple[s] = coupling_of(base[s], wave[s], cosine)
        return carry

    lax.fori_loop(0, slabs, one, 0)


def prepare_kernel(
    impulse_count,
    constants_ref, contact_ref, counts_ref, onsite, hopping, potential, base, wave,
    couple_0, entry_0,
    couple_1, entry_1,
    constants, contact, counts, scalar_sem,
):
    position = lax.axis_index("en")

    def prepare_slot(slot, made):
        momentum, level = item_of(counts, slot)
        cosine, energy, weight = entry_amounts(constants, impulse_count, momentum, level)
        inv_real, inv_imag = inverse_diagonal(
            position, cosine, energy, contact, onsite, hopping, potential
        )
        prepare(cosine, weight, inv_real, inv_imag, base, wave, *made)

    @pl.when(position > 0)
    def _():
        with_scalars(
            (constants_ref, contact_ref, counts_ref), (constants, contact, counts), scalar_sem
        )
        prepare_slot(0, (couple_0, entry_0))
        prepare_slot(1, (couple_1, entry_1))


def rows_of_entry(entry, slabs):
    inv_real = jnp.concatenate([entry[s, 0:1, :] for s in range(slabs)], axis=0)
    inv_imag = jnp.concatenate([entry[slabs + s, 0:1, :] for s in range(slabs)], axis=0)
    return inv_real, inv_imag, entry[2 * slabs, 0:1, 0:1]


def operator_kernel(couple, entry, carriers, cross, local, densities, both, left):
    slabs, orbitals, _ = couple.shape
    parts = orbitals // LANE

    @pl.when(lax.axis_index("en") > 0)
    def _():
        inv_real, inv_imag, weight = rows_of_entry(entry, slabs)
        down = columns_of(inv_real, inv_imag)
        for s in range(slabs):
            coupled = couple[s]
            real_col = down[:, s : s + 1]
            imag_col = down[:, slabs + s : slabs + s + 1]
            real_row, imag_row = inv_real[s : s + 1, :], inv_imag[s : s + 1, :]
            if s == 0:
                wide = coupled.astype(F32)
                real, imag = real_col * wide, imag_col * wide
                densities[0:1, :] = -weight * imag_row
            else:
                width = 2 * orbitals if s == 1 else 4 * orbitals
                product = jnp.dot(coupled, both[:, :width], preferred_element_type=F32)
                from_real, from_imag = product[:, :orbitals], product[:, orbitals : 2 * orbitals]
                real = real_col * from_real - imag_col * from_imag
                imag = real_col * from_imag + imag_col * from_real
                if s == 1:
                    wide = coupled.astype(F32)
                    for half, inv in ((0, inv_real), (1, inv_imag)):
                        piece = (wide * inv[0:1, :].astype(BF16).astype(F32)).astype(BF16)
                        for c in range(parts):
                            store_left(left, piece[:, span(c)], half, c, parts)
                else:
                    keep_product(product[:, 2 * orbitals :].astype(BF16), left, parts)
            real, imag = real.astype(BF16), imag.astype(BF16)
            here = slice(s * orbitals, (s + 1) * orbitals)
            carriers[here, :orbitals] = real
            carriers[here, orbitals:] = imag
            if s < slabs - 1:
                both[:, :orbitals] = real
                both[:, orbitals : 2 * orbitals] = imag
            if s == 0:
                continue

            def times_turned(rows):
                return lax.dot_general(
                    rows, coupled, (((1,), (1,)), ((), ())), preferred_element_type=F32
                )

            def note(r, middle):
                densities[s : s + 1, span(r)] = -weight * middle

            final = s == slabs - 1
            finish_slab(
                s, times_turned, left, None if final else both, None,
                (real_col, imag_col), real_row, imag_row, note, parts,
                local if final else None, 2 * parts,
            )
        top = (slabs - 1) * parts
        for r in range(parts):
            for c in range(parts):
                real = carriers[span(top + r), span(c)].T
                imag = carriers[span(top + r), span(parts + c)].T
                cross[span(c), span(r)] = real
                cross[span(parts + c), span(parts + r)] = real
                cross[span(c), span(parts + r)] = imag
                cross[span(parts + c), span(r)] = -imag


def pass_kernel(stage, calls, *refs):
    local = Either(refs[:calls])
    carriers, cross, arrived, sent, wide, half_way = refs[calls:]
    orbitals = carriers.shape[1] // 2
    parts = orbitals // LANE

    @pl.when(lax.axis_index("en") == stage)
    def _():
        def put(half, r, c, block):
            if half == 0:
                wide[span(r), span(c)] = block
                wide[span(parts + r), span(parts + c)] = block
            else:
                wide[span(r), span(parts + c)] = block
                wide[span(parts + r), span(c)] = -block

        unpack_blocks(arrived, put, parts)
        half_way[...] = jnp.dot(
            carriers[carriers.shape[0] - orbitals :, :], wide[...], preferred_element_type=F32
        ).astype(BF16)
        out = jnp.dot(half_way[...], cross[...], preferred_element_type=F32)
        middles = []
        for k, (r, c) in enumerate(blocks_on_or_below(parts)):
            green_real = local[span(2 * k), :] + out[span(r), span(c)]
            green_imag = local[span(2 * k + 1), :] + out[span(r), span(parts + c)]
            pack_block(sent, r, c, green_real, green_imag, parts)
            if r == c:
                middles.append(diagonal_row(green_imag))
        pack_middles(sent, middles, parts)


def density_kernel(calls, carriers, *refs):
    entry, refs = Either(refs[: calls[0]]), refs[calls[0] :]
    local_densities, refs = Either(refs[: calls[1]]), refs[calls[1] :]
    so_far, arrived, (density, wide, total) = refs[0], refs[1:-3], refs[-3:]
    slabs, orbitals = so_far.shape
    parts = orbitals // LANE
    position = lax.axis_index("en")
    density[...] = so_far[...]

    def put(half, r, c, block):
        if half == 0:
            wide[span(r), span(2 * c)] = block
            wide[span(parts + r), span(2 * c + 1)] = block
        else:
            wide[span(r), span(2 * c + 1)] = block
            wide[span(parts + r), span(2 * c)] = -block

    for stage, block in enumerate(arrived, 1):

        @pl.when(position == stage)
        def _():
            unpack_blocks(block, put, parts)

    @pl.when(position > 0)
    def _():
        for c in range(parts):
            product = jnp.dot(
                carriers[...],
                wide[:, 2 * c * LANE : 2 * (c + 1) * LANE],
                preferred_element_type=F32,
            )
            term = product[:, :LANE] * carriers[:, span(parts + c)].astype(F32) + product[
                :, LANE:
            ] * carriers[:, span(c)].astype(F32)
            if c == 0:
                total[...] = term
            else:
                total[...] += term
        weight = entry[2 * slabs, 0:1, :LANE]
        for s in range(slabs):
            for r in range(parts):
                row = jnp.sum(total[span(s * parts + r), :].T, axis=0, keepdims=True)
                density[s : s + 1, span(r)] += (
                    local_densities[s : s + 1, span(r)] - weight * row
                )


def vmem_call(kernel, outs, operands, in_specs, scratch, name, flops, traffic=2**21, **more):
    vmem = pl.BlockSpec(memory_space=pltpu.VMEM)
    return pl.pallas_call(
        kernel,
        out_shape=tuple(outs),
        in_specs=in_specs,
        out_specs=(vmem,) * len(outs),
        scratch_shapes=scratch,
        compiler_params=pltpu.CompilerParams(vmem_limit_bytes=16 * 2**20),
        cost_estimate=pl.CostEstimate(flops=flops, bytes_accessed=traffic, transcendentals=0),
        name=name,
        **more,
    )(*operands)


def split_kernel(inverse, high, middle, low):
    for r in range(inverse.shape[0] // LANE):
        for c in range(inverse.shape[1] // LANE):
            block = inverse[span(r), span(c)].T
            for part in (high, middle, low):
                rounded = block.astype(BF16)
                part[span(c), span(r)] = rounded
                block = block - rounded.astype(F32)


def last_kernel(gathered, doping, high, middle, low, summed, potential):
    total = jnp.sum(gathered[...], axis=0)
    summed[...] = total
    rest = total - doping[...]
    pieces = []
    for _ in range(3):
        pieces.append(rest.astype(BF16).astype(F32))
        rest = rest - pieces[-1]
    rows = total.shape[0]
    answer = jnp.zeros_like(total)
    for count, part in ((1, low), (2, middle), (3, high)):
        padded = -(-3 * rows // 16) * 16 - count * rows
        stacked = jnp.concatenate(
            pieces[:count] + [jnp.zeros((padded, total.shape[1]), F32)], axis=0
        ).astype(BF16)
        product = jnp.dot(stacked, part[...], preferred_element_type=F32)
        for k in reversed(range(count)):
            answer = answer + product[k * rows : (k + 1) * rows]
    potential[...] = answer


def gather_over(values, axis):
    copies = jnp.broadcast_to(values[None], (lax.axis_size(axis),) + values.shape)
    return lax.all_to_all(copies, axis, 0, 0)


def body(
    counts,
    contact_slabs,
    onsite,
    hopping,
    potential_in,
    couple_base,
    couple_wave,
    doping,
    poisson_inverse,
):
    kt_size = lax.axis_size("kt")
    en_size = lax.axis_size("en")
    slabs, orbitals = onsite.shape
    parts = orbitals // LANE
    impulse_count = counts.shape[0] * kt_size
    constants = jnp.asarray(item_constants(impulse_count))
    smem = pl.BlockSpec(memory_space=pltpu.SMEM)
    hbm = pl.BlockSpec(memory_space=pltpu.HBM)
    vmem = pl.BlockSpec(memory_space=pltpu.VMEM)
    flops = 2 * slabs * orbitals**3

    def forward(block, stage):
        return lax.ppermute(block, "en", [(stage, stage + 1)])

    block_shape = jax.ShapeDtypeStruct((packed_rows(orbitals), LANE), BF16)
    density_shape = jax.ShapeDtypeStruct((slabs, orbitals), F32)
    couple_shape = jax.ShapeDtypeStruct((slabs, orbitals, orbitals), BF16)
    entry_shape = jax.ShapeDtypeStruct((2 * slabs + 1, 8, orbitals), F32)
    work = [
        pltpu.VMEM((orbitals, 2 * orbitals), BF16),
        pltpu.VMEM((2 * orbitals, orbitals), BF16),
    ]

    counts_all = gather_over(
        jnp.broadcast_to(counts[:, None], (counts.shape[0], 1)), "kt"
    )
    given = (constants, contact_slabs, onsite, hopping, potential_in, couple_base, couple_wave)
    pinned = [pltpu.with_memory_space_constraint(t, pltpu.HBM) for t in given]
    block, density, *loaded = vmem_call(
        functools.partial(lead_kernel, impulse_count),
        (block_shape, density_shape, couple_shape, couple_shape),
        pinned,
        [hbm] * len(pinned),
        [
            pltpu.SMEM(constants.shape, F32),
            pltpu.SMEM(contact_slabs.shape, jnp.int32),
            pltpu.VMEM((3, slabs, orbitals), F32),
        ]
        + work
        + [
            pltpu.SemaphoreType.DMA((2,)),
            pltpu.SemaphoreType.DMA((3,)),
            pltpu.SemaphoreType.DMA((2, slabs)),
        ],
        "lead",
        3 * flops,
    )
    block, counts_all = lax.optimization_barrier((block, counts_all))
    small = (constants, contact_slabs, counts_all, onsite, hopping, potential_in)

    anywhere = pl.BlockSpec(memory_space=pl.ANY)
    scalar_scratch = [
        pltpu.SMEM(constants.shape, F32),
        pltpu.SMEM(contact_slabs.shape, jnp.int32),
        pltpu.SMEM(counts_all.shape, jnp.int32),
        pltpu.SemaphoreType.DMA((3,)),
    ]

    def begin(slot, density, *held):
        return vmem_call(
            functools.partial(begin_kernel, impulse_count, slot),
            (density_shape, block_shape),
            (*small, *loaded, density, *held),
            [anywhere] * 3 + [vmem] * (6 + len(held)),
            scalar_scratch + work,
            f"begin_{slot}",
            3 * flops,
            input_output_aliases={8: 0, 9: 1} if held else {8: 0},
        )

    density, block = begin(0, density, block)
    arrived = [forward(block, 0)]
    density, block = begin(1, density)
    arrived.append(forward(block, 0))
    small, _ = lax.optimization_barrier((small, block))
    made = vmem_call(
        functools.partial(prepare_kernel, impulse_count),
        (couple_shape, entry_shape) * 2,
        (*small, *loaded),
        [anywhere] * 3 + [vmem] * 5,
        scalar_scratch,
        "prepare",
        flops // 16,
        2**16,
    )
    made = [[(one,) for one in made[:2]], [(one,) for one in made[2:]]]

    carriers_shape = jax.ShapeDtypeStruct((slabs * orbitals, 2 * orbitals), BF16)
    double_shape = jax.ShapeDtypeStruct((2 * orbitals, 2 * orbitals), BF16)

    def operator_of(slot):
        (couple,), (entry,) = made[slot]
        results = vmem_call(
            operator_kernel,
            (
                carriers_shape,
                double_shape,
                jax.ShapeDtypeStruct((local_rows(parts), LANE), F32),
                density_shape,
            ),
            (couple, entry),
            [vmem] * 2,
            [
                pltpu.VMEM((orbitals, 4 * orbitals), BF16),
                pltpu.VMEM((2 * orbitals, orbitals), BF16),
            ],
            f"operator_{slot}",
            flops // 16,
            2**16,
        )
        carried.append(results[:2])
        local.append([results[2:]])

    def pass_on(stage, slot, block):
        calls = [one[0] for one in local[slot]]
        return vmem_call(
            functools.partial(pass_kernel, stage, len(calls)),
            (block_shape,),
            (*calls, *carried[slot], block),
            [vmem] * (3 + len(calls)),
            [
                pltpu.VMEM(double_shape.shape, BF16),
                pltpu.VMEM((orbitals, 2 * orbitals), BF16),
            ],
            f"pass_{stage}_{slot}",
            2 * flops,
        )[0]

    def densities(slot, density, came):
        entry = made[slot][1]
        calls = [one[1] for one in local[slot]]
        before = 1 + len(entry) + len(calls)
        return vmem_call(
            functools.partial(density_kernel, (len(entry), len(calls))),
            (density_shape,),
            (carried[slot][0], *entry, *calls, density, *came),
            [vmem] * (before + 1 + len(came)),
            [
                pltpu.VMEM(double_shape.shape, BF16),
                pltpu.VMEM((slabs * orbitals, LANE), F32),
            ],
            f"density_{slot}",
            4 * flops,
            input_output_aliases={before: 0},
        )[0]

    came = [[arrived[0]], [arrived[1]]]
    carried, local = [], []
    operator_of(0)
    for stage in range(1, en_size - 1):
        for slot in range(2):
            if stage == 1 and slot == 1:
                made[1], _ = lax.optimization_barrier((made[1], block))
                operator_of(1)
            block = pass_on(stage, slot, came[slot][-1])
            came[slot].append(forward(block, stage))
    for slot in range(2):
        density = densities(slot, density, came[slot])
    part_shape = jax.ShapeDtypeStruct(poisson_inverse.shape, BF16)
    inverse, _ = lax.optimization_barrier((poisson_inverse, block))
    split = vmem_call(
        split_kernel, (part_shape,) * 3, (inverse,), [vmem], [], "split_inverse", 2 * flops
    )
    density, *split = lax.optimization_barrier((density, *split))
    return vmem_call(
        last_kernel,
        (density_shape, density_shape),
        (gather_over(density, "kt"), doping, *split),
        [vmem] * 5,
        [],
        "last",
        flops // slabs,
    )


def solution(mesh):
    return jax.shard_map(
        body,
        mesh=mesh,
        in_specs=(
            P("kt"),
            P(),
            P("en", None),
            P("en", None),
            P("en", None),
            P("en", None, None),
            P("en", None, None),
            P("en", None),
            P(),
        ),
        out_specs=(P("en", None), P("en", None)),
        check_vma=False,
    )
```
